32 devices in a mesh: dp: 4 (over y, x), fsdp: 8 (over z, core).
Axes of the slice: x: 2, y: 2, z: 4, core: 2. Of those that a mesh axis runs over, the one named last changes fastest.
Arguments:
- tokens: bfloat16 [8192, 2048], P(('dp', 'fsdp')), may hold values from -6 to 6
- lengths: int32 [32, 2], P(('dp', 'fsdp')), may hold values from 1 to 224, as said below
- attn_gain: bfloat16 [2048], P(('dp', 'fsdp')), may hold values from 0.5 to 1.5
- query_down: bfloat16 [2048, 1024], P(('dp', 'fsdp')), may hold values from -0.125 to 0.125
- query_gain: bfloat16 [1024], P(('dp', 'fsdp')), may hold values from 0.5 to 1.5
- query_up: bfloat16 [1024, 4096], P(('dp', 'fsdp')), may hold values from -0.375 to 0.375
- key_weight: bfloat16 [2048, 256], P(('dp', 'fsdp')), may hold values from -0.125 to 0.125
- value_weight: bfloat16 [2048, 256], P(('dp', 'fsdp')), may hold values from -0.125 to 0.125
- out_weight: bfloat16 [4096, 2048], P(('dp', 'fsdp')), may hold values from -0.375 to 0.375
- mlp_gain: bfloat16 [2048], P(('dp', 'fsdp')), may hold values from 0.5 to 1.5
- gate_weight: bfloat16 [2048, 5632], P(('dp', 'fsdp')), may hold values from -0.125 to 0.125
- up_weight: bfloat16 [2048, 5632], P(('dp', 'fsdp')), may hold values from -0.125 to 0.125
- down_weight: bfloat16 [5632, 2048], P(('dp', 'fsdp')), may hold values from -0.109375 to 0.109375
- cotangent: bfloat16 [8192, 2048], P(('dp', 'fsdp')), may hold values from -6 to 6
Outputs:
- layer_out: bfloat16 [8192, 2048], P(('dp', 'fsdp'))
- tokens_grad: float32 [8192, 2048], P(('dp', 'fsdp'))
- attn_gain_grad: float32 [2048], P(('dp', 'fsdp'))
- query_down_grad: float32 [2048, 1024], P(('dp', 'fsdp'))
- query_gain_grad: float32 [1024], P(('dp', 'fsdp'))
- query_up_grad: float32 [1024, 4096], P(('dp', 'fsdp'))
- key_weight_grad: float32 [2048, 256], P(('dp', 'fsdp'))
- value_weight_grad: float32 [2048, 256], P(('dp', 'fsdp'))
- out_weight_grad: float32 [4096, 2048], P(('dp', 'fsdp'))
- mlp_gain_grad: float32 [2048], P(('dp', 'fsdp'))
- gate_weight_grad: float32 [2048, 5632], P(('dp', 'fsdp'))
- up_weight_grad: float32 [2048, 5632], P(('dp', 'fsdp'))
- down_weight_grad: float32 [5632, 2048], P(('dp', 'fsdp'))
The draws below stay inside these ranges and needn't reach their ends.
Inputs may be any that keep to these rules, and one draw needn't show every extreme that they name: A row holds the lengths of one device's 2 sequences; rounded up to multiples of 32 they sum to at most 256. On one device, drawn from the seed, they sum to exactly 256 and one of its sequences is 224 long.
All inputs are finite; a program needn't handle non-finite values.
Results may differ from the reference program's by a relative error of at most 0.017.
Values may be sent and summed in bfloat16 or wider, within the bound.
No kernel may reach another device: no remote copies, remote signals or barrier semaphores. Data moves between devices by JAX's collectives and lax.ppermute only.
A program may use at most 384 MiB of HBM per device.

```python
import math
import jax
import jax.numpy as jnp
from jax import lax

D = 2048
QR = 1024
H = 16
HD = 256
FF = 5632
TOK_DEV = 256
PAD = 32
TOKENS = 8192


def draw_lengths(key, part):
    key = jax.random.fold_in(key, 11)
    device_count = TOKENS // TOK_DEV
    units = TOK_DEV // PAD
    key_used, key_full, key_first, key_pick, key_trim = jax.random.split(key, 5)
    used = jax.random.randint(key_used, (device_count,), max(2, units // 2), units + 1)
    full_device = jax.random.randint(key_full, (), 0, device_count)
    is_full = jnp.arange(device_count, dtype=jnp.int32) == full_device
    used = jnp.where(is_full, units, used)
    first_units = jax.random.randint(key_first, (device_count,), 1, used)
    pick_side = jax.random.randint(key_pick, (device_count,), 0, 2)
    first_units = jnp.where(is_full, jnp.where(pick_side == 0, 1, units - 1), first_units)
    second_units = used - first_units
    trims = jax.random.randint(key_trim, (device_count, 2), 0, PAD)
    trims = jnp.where(is_full[:, None], 0, trims)
    return (jnp.stack([first_units, second_units], axis=1) * PAD - trims).astype(jnp.int32)


def with_spikes(values, stream_key, source, target, shards_of, factor):
    def block_of(dim):
        return (jnp.arange(values.shape[dim]) // (values.shape[dim] // shards_of)).reshape((-1,) + (1,) * (values.ndim - 1 - dim))

    one_side = jax.random.permutation(stream_key, shards_of)[block_of(target)]
    second = (block_of(target) + shards_of // 2) % shards_of
    return jnp.where((block_of(source) == one_side) | (block_of(source) == second), factor * values, values)


def block_levels(stream_key, dims, cuts, low, high):
    def one(position, blocks):
        heights = jax.random.uniform(jax.random.fold_in(jax.random.fold_in(stream_key, 6), position), (blocks,), jnp.float32, low / len(cuts), high / len(cuts))
        return jnp.repeat(jnp.exp(heights), dims[position] // blocks).reshape((-1,) + (1,) * (len(dims) - position - 1))

    level = one(*cuts[0])
    for cut in cuts[1:]:
        level = level * one(*cut)
    return level


def normal_values(rng, extent, width, reach, cuts=(), kind=jnp.bfloat16):
    entries = width * jax.random.normal(rng, extent, jnp.float32)
    if cuts:
        entries = entries * block_levels(rng, extent, cuts, -0.22, 0.18)
    return jnp.clip(entries, -reach, reach).astype(kind)


def bell_draw_with(rng, dims, deviation, bound, shards, heavy, held_as=jnp.bfloat16):
    array = deviation * jax.random.normal(rng, dims, jnp.float32)
    if shards:
        array = array * block_levels(rng, dims, shards, -0.22, 0.18)
    return jnp.clip(with_spikes(array, jax.random.fold_in(rng, 3), *heavy), -bound, bound).astype(held_as)


def setup_inputs(seed: int = 0) -> dict:
    arg_keys = jax.random.split(jax.random.key(seed), 15)
    return {
        "tokens": bell_draw_with(arg_keys[0], (TOKENS, D), 1.0, 6.0, ((0, 32),), (0, 1, 32, 2.75)),
        "lengths": draw_lengths(jax.random.fold_in(arg_keys[14], 71), 0),
        "attn_gain": jnp.clip(1.0 + 0.1 * jax.random.normal(arg_keys[2], (D,), jnp.float32), 0.5, 1.5).astype(jnp.bfloat16),
        "query_down": normal_values(arg_keys[3], (D, QR), D ** -0.5, 0.125, ((0, 32),)),
        "query_gain": jnp.clip(1.0 + 0.1 * jax.random.normal(arg_keys[4], (QR,), jnp.float32), 0.5, 1.5).astype(jnp.bfloat16),
        "query_up": normal_values(arg_keys[5], (QR, H * HD), (QR // 4) ** -0.5, 0.375, ((0, 32),)),
        "key_weight": normal_values(arg_keys[6], (D, HD), D ** -0.5, 0.125, ((0, 32),)),
        "value_weight": normal_values(arg_keys[7], (D, HD), D ** -0.5, 0.125, ((0, 32),)),
        "out_weight": normal_values(arg_keys[8], (H * HD, D), (H * HD // 16) ** -0.5, 0.375, ((0, 32),)),
        "mlp_gain": jnp.clip(1.0 + 0.1 * jax.random.normal(arg_keys[9], (D,), jnp.float32), 0.5, 1.5).astype(jnp.bfloat16),
        "gate_weight": normal_values(arg_keys[10], (D, FF), D ** -0.5, 0.125, ((0, 32),)),
        "up_weight": normal_values(arg_keys[11], (D, FF), D ** -0.5, 0.125, ((0, 32),)),
        "down_weight": normal_values(arg_keys[12], (FF, D), (FF // 2) ** -0.5, 0.109375, ((0, 32),)),
        "cotangent": bell_draw_with(arg_keys[13], (TOKENS, D), 1.0, 6.0, ((0, 32),), (0, 1, 32, 2.75)),
    }


@jax.custom_vjp
def low(v):
    return lax.optimization_barrier(v.astype(jnp.bfloat16)).astype(jnp.float32)

@jax.custom_vjp
def low_back(v):
    return v

def low_keep(v):
    return (low(v), None)

def low_pass(kept, grad):
    return (grad,)

def back_keep(v):
    return (v, None)

def back_low(kept, grad):
    return (low(grad),)
low.defvjp(low_keep, low_pass)
low_back.defvjp(back_keep, back_low)
eps = 1e-06
rope_base = 10000.0
masked_score = -1e+30

def layout(lengths, row_total):
    padded = (lengths + PAD - 1) // PAD * PAD
    slot_end = jnp.cumsum(padded).astype(jnp.int32)
    slot_start = slot_end - padded
    row_index = jnp.arange(row_total, dtype=jnp.int32)
    member = (row_index[:, None] >= slot_start[None, :]) & (row_index[:, None] < slot_end[None, :])
    slot_number = jnp.arange(1, lengths.shape[0] + 1, dtype=jnp.int32)
    segment = lax.optimization_barrier(jnp.sum(jnp.where(member, slot_number[None, :], 0), axis=1))
    offset = row_index - lax.optimization_barrier(jnp.sum(jnp.where(member, slot_start[None, :], 0), axis=1))
    alive = jnp.any(member & (offset[:, None] < lengths[None, :]), axis=1)
    allowed = (segment[:, None] == segment[None, :]) & (segment[:, None] > 0) & (row_index[None, :] <= row_index[:, None]) & alive[None, :]
    allowed = allowed | (row_index[:, None] == row_index[None, :])
    return (offset, alive, allowed)

def angles(offset, head_size):
    half_width = head_size // 2
    frequency = jnp.exp(jnp.arange(half_width, dtype=jnp.float32) * (-2.0 * math.log(rope_base) / head_size))
    phase = offset.astype(jnp.float32)[:, None] * frequency[None, :]
    return (jnp.cos(phase), jnp.sin(phase))

def rotate(values, cos_part, sin_part):
    half_width = values.shape[-1] // 2
    first_half = values[..., :half_width]
    second_half = values[..., half_width:]
    return jnp.concatenate([first_half * cos_part - second_half * sin_part, second_half * cos_part + first_half * sin_part], axis=-1)

def normalize(values, scale_gain):
    return values * lax.rsqrt(lax.optimization_barrier(jnp.mean(values * values, axis=-1, keepdims=True)) + eps) * scale_gain

def product(left, right):
    return jnp.dot(left, right, precision=lax.Precision.HIGHEST, preferred_element_type=jnp.float32)

def attend(inputs_block):
    query_rot, key_rot, value_low, lengths_row = inputs_block
    offset, alive, allowed = layout(lengths_row, TOK_DEV)
    scores = jnp.einsum('thd,sd->hts', query_rot, key_rot, precision=lax.Precision.HIGHEST) * (1.0 / math.sqrt(HD))
    scores = low_back(scores)
    scores = jnp.where(allowed[None, :, :], scores, masked_score)
    attn_probs = low(jax.nn.softmax(scores, axis=-1))
    return jnp.einsum('hts,sd->thd', attn_probs, value_low, precision=lax.Precision.HIGHEST)

def forward(token_rows, weights, lengths):
    attn_gain, query_down, query_gain, query_up, key_weight, value_weight, out_weight, mlp_gain, gate_weight, up_weight, down_weight = weights
    block_count = lengths.shape[0]
    offsets, alives, unused_mask = jax.vmap(lambda lengths_row: layout(lengths_row, TOK_DEV))(lengths)
    living = alives.reshape(-1, 1).astype(jnp.float32)
    cos_part, sin_part = angles(offsets.reshape(-1), HD)
    attn_in = low(normalize(token_rows, attn_gain))
    latent = low_back(product(attn_in, query_down))
    latent_in = low(normalize(latent, query_gain))
    queries = low_back(product(latent_in, query_up)).reshape(-1, H, HD)
    query_rot = low(rotate(queries, cos_part[:, None, :], sin_part[:, None, :]))
    key_plain = low_back(product(attn_in, key_weight))
    key_rot = low(rotate(key_plain, cos_part, sin_part))
    value_low = low(low_back(product(attn_in, value_weight)))
    inputs_all = (query_rot.reshape(block_count, TOK_DEV, H, HD), key_rot.reshape(block_count, TOK_DEV, HD), value_low.reshape(block_count, TOK_DEV, HD), lengths)
    mixture = lax.map(jax.checkpoint(attend), inputs_all)
    mixture = low(low_back(mixture.reshape(-1, H * HD)))
    residual = token_rows + living * low_back(product(mixture, out_weight))
    ffn_in = low(normalize(residual, mlp_gain))
    gate_act = low_back(product(ffn_in, gate_weight))
    up_act = low_back(product(ffn_in, up_weight))
    hidden = low(jax.nn.silu(gate_act) * up_act)
    return residual + living * low_back(product(hidden, down_weight))

def reference(tokens, lengths, attn_gain, query_down, query_gain, query_up, key_weight, value_weight, out_weight, mlp_gain, gate_weight, up_weight, down_weight, cotangent):
    weights = tuple((weight_item.astype(jnp.float32) for weight_item in (attn_gain, query_down, query_gain, query_up, key_weight, value_weight, out_weight, mlp_gain, gate_weight, up_weight, down_weight)))
    token_rows = tokens.astype(jnp.float32)
    layer_value, pullback = jax.vjp(lambda rows_in, params_in: forward(rows_in, params_in, lengths), token_rows, weights)
    tokens_grad, weight_grads = pullback(cotangent.astype(jnp.float32))
    return (layer_value.astype(jnp.bfloat16), tokens_grad, weight_grads[0], weight_grads[1], weight_grads[2], weight_grads[3], weight_grads[4], weight_grads[5], weight_grads[6], weight_grads[7], weight_grads[8], weight_grads[9], weight_grads[10])
```

```python
import math

import jax
import jax.numpy as jnp
from jax import lax
from jax.sharding import PartitionSpec as P

H = 16
HD = 256
PAD = 32

eps = 1e-06
rope_base = 10000.0
masked_score = -1e30
ALL = ("dp", "fsdp")
f32 = jnp.float32
bf16 = jnp.bfloat16


def layout(lengths, row_total):
    padded = (lengths + PAD - 1) // PAD * PAD
    count = lengths.shape[0]
    ends = []
    for s in range(count):
        ends.append(padded[s] if s == 0 else ends[-1] + padded[s])
    row = lax.broadcasted_iota(jnp.int32, (row_total, 1), 0)
    segment = jnp.zeros_like(row)
    start = jnp.zeros_like(row)
    alive = jnp.zeros(row.shape, jnp.bool_)
    for s in range(count):
        first = ends[s] - padded[s]
        member = (row >= first) & (row < ends[s])
        segment = jnp.where(member, s + 1, segment)
        start = jnp.where(member, first, start)
        alive = alive | (member & (row - first < lengths[s]))
    return row - start, alive, segment


def mask_of(alive, segment, row_total):
    seg, live = segment[:, 0], alive[:, 0]
    row = jnp.arange(row_total, dtype=jnp.int32)
    allowed = (
        (seg[:, None] == seg[None, :])
        & (seg[:, None] > 0)
        & (row[None, :] <= row[:, None])
        & live[None, :]
    )
    return allowed | (row[:, None] == row[None, :])


def angles(offset, head_size):
    half_width = head_size // 2
    frequency = jnp.exp(
        jnp.arange(half_width, dtype=f32) * (-2.0 * math.log(rope_base) / head_size)
    )
    phase = offset.astype(f32) * frequency[None, :]
    return (jnp.cos(phase), jnp.sin(phase))


def rotate(values, cos_part, sin_part):
    half_width = values.shape[-1] // 2
    first_half = values[..., :half_width]
    second_half = values[..., half_width:]
    return jnp.concatenate(
        [
            first_half * cos_part - second_half * sin_part,
            second_half * cos_part + first_half * sin_part,
        ],
        axis=-1,
    )


def normalize(values, scale_gain):
    factor = lax.rsqrt(jnp.mean(values * values, axis=-1, keepdims=True) + eps)
    normed = values * factor
    return (normed * scale_gain, normed, factor)


def normalize_back(upstream, normed, factor, scale_gain):
    scaled = upstream * scale_gain
    gain_grad = jnp.sum(upstream * normed, axis=0)
    inner_mean = jnp.mean(scaled * normed, axis=-1, keepdims=True)
    return (factor * (scaled - normed * inner_mean), gain_grad)


def dot(a, b):
    return jnp.dot(a, b, preferred_element_type=f32)


def dot_nt(a, b):
    return lax.dot_general(a, b, (((1,), (1,)), ((), ())), preferred_element_type=f32)


def dot_tn(a, b):
    return lax.dot_general(a, b, (((0,), (0,)), ((), ())), preferred_element_type=f32)


def swap(values, mask):
    return lax.ppermute(values, "dp", [(i, i ^ mask) for i in range(4)])


def gather_group(values):
    half = values.shape[0] // 2
    one = swap(values, 1)
    two = swap(values, 2)
    three = jnp.concatenate([swap(two[:half], 1), swap(one[half:], 2)], axis=0)
    return jnp.concatenate([values, one, two, three], axis=0)


def scatter_group(own, others):
    rows = own.shape[0]
    half = rows // 2
    s1, s2, s3 = (others[i * rows : (i + 1) * rows] for i in range(3))
    ra = swap(jnp.concatenate([s1[:half], s3[:half]], axis=0), 1)
    rb = swap(jnp.concatenate([s2[half:], s3[half:]], axis=0), 2)
    pass_a = (s2[:half].astype(f32) + ra[half:].astype(f32)).astype(bf16)
    pass_b = (s1[half:].astype(f32) + rb[half:].astype(f32)).astype(bf16)
    last_a = swap(pass_a, 2)
    last_b = swap(pass_b, 1)
    top = own[:half] + ra[:half].astype(f32) + last_a.astype(f32)
    low = own[half:] + rb[:half].astype(f32) + last_b.astype(f32)
    return jnp.concatenate([top, low], axis=0)


def columns_in(weight, members):
    rows, width = weight.shape
    cut = weight.reshape(rows, members, width // members).transpose(1, 0, 2)
    return lax.all_to_all(cut, "dp", 0, 0, tiled=True).reshape(members * rows, width // members)


def columns_back(grad, members):
    rows, width = grad.shape[0] // members, grad.shape[1]
    cut = lax.all_to_all(grad.reshape(members, rows, width), "dp", 0, 0, tiled=True)
    return cut.transpose(1, 0, 2).reshape(rows, members * width).astype(f32)


def to_shards(values, members, ring):
    rows, width = values.shape
    cut = values.reshape(rows, members, ring, width // (members * ring))
    return cut.transpose(0, 2, 1, 3).reshape(rows, width)


def from_shards(values, members, ring):
    rows, width = values.shape
    cut = values.reshape(rows, ring, members, width // (members * ring))
    return cut.transpose(0, 2, 1, 3).reshape(rows, width)


def shards(
    members,
    ring,
    tokens,
    lengths,
    attn_gain,
    query_down,
    query_gain,
    query_up,
    key_weight,
    value_weight,
    out_weight,
    mlp_gain,
    gate_weight,
    up_weight,
    down_weight,
    cotangent,
):
    rows = tokens.shape[0]
    width = tokens.shape[1]
    latent_width = query_down.shape[1]
    heads = H // members
    devices = members * ring
    score_scale = 1.0 / math.sqrt(HD)
    d_rows = query_down.shape[0]

    def column(v):
        v = v.astype(bf16).reshape(-1, 1)
        return jnp.pad(v, ((0, d_rows - v.shape[0]), (0, 0)))

    extra = jnp.concatenate(
        [column(attn_gain), column(mlp_gain), column(query_gain), column(lengths[0])], axis=1
    )
    extra = jnp.pad(extra, ((0, 0), (0, 128 - extra.shape[1])))
    small = jnp.concatenate([query_down, key_weight, value_weight, extra], axis=1)
    small = lax.all_gather(small, ALL, axis=0, tiled=True)
    qkv_full = small[:, : latent_width + 2 * HD]
    extra = small[:, latent_width + 2 * HD :].astype(f32).T
    attn_scale = extra[0:1]
    mlp_scale = extra[1:2]
    latent_scale = extra[2].reshape(devices, d_rows)[:, : query_gain.shape[0]].reshape(1, -1)
    all_lengths = extra[3].reshape(devices, d_rows)[:, : lengths.shape[1]].astype(jnp.int32)

    query_full = lax.all_gather(columns_in(query_up, members), "fsdp", axis=0, tiled=True)
    out_full = lax.all_gather(out_weight, "fsdp", axis=0, tiled=True)
    gate_up = jnp.concatenate([columns_in(gate_weight, members), columns_in(up_weight, members)], axis=1)
    gate_up = lax.all_gather(gate_up, "fsdp", axis=0, tiled=True)
    cut = gate_up.shape[1] // 2
    gate_full, up_full = gate_up[:, :cut], gate_up[:, cut:]
    down_full = lax.all_gather(down_weight, "fsdp", axis=0, tiled=True)

    me, lane = lax.axis_index("dp"), lax.axis_index("fsdp")
    parts = []
    for slot in range(members):
        mine = lax.dynamic_slice_in_dim(all_lengths, (me ^ slot) * ring + lane, 1, 0)[0]
        parts.append(layout(mine, rows))
    offset = jnp.concatenate([p[0] for p in parts], axis=0)
    alive = parts[0][1]
    living = alive.astype(f32)
    allowed = jnp.stack([mask_of(p[1], p[2], rows) for p in parts])
    cos_part, sin_part = angles(offset, HD)

    grad_rows = cotangent.astype(f32)
    ffn_grad = gather_group((living * grad_rows).astype(bf16))
    token_rows = tokens.astype(f32)
    attn_out, attn_normed, attn_factor = normalize(token_rows, attn_scale)
    attn_in = attn_out.astype(bf16)
    low = dot(attn_in, qkv_full)
    latent = low[:, :latent_width]
    latent_out, latent_normed, latent_factor = normalize(latent, latent_scale)
    latent_in = to_shards(latent_out.astype(bf16), members, ring)
    key_own = rotate(low[:, latent_width : latent_width + HD], cos_part[:rows], sin_part[:rows])
    value_own = low[:, latent_width + HD :]
    packed = jnp.concatenate([latent_in, key_own.astype(bf16), value_own.astype(bf16)], axis=1)
    packed = gather_group(packed)
    latent_in = packed[:, :latent_width]
    key_rot = packed[:, latent_width : latent_width + HD].reshape(members, rows, HD)
    value_low = packed[:, latent_width + HD :].reshape(members, rows, HD)

    queries = dot(latent_in, query_full).reshape(members * rows, heads, HD)
    query_rot = rotate(queries, cos_part[:, None, :], sin_part[:, None, :]).astype(bf16)
    query_rot = query_rot.reshape(members, rows, heads, HD)

    def score_block():
        scores = (
            jnp.einsum("mthd,msd->mhts", query_rot, key_rot, preferred_element_type=f32) * score_scale
        )
        return jnp.where(allowed[:, None], scores, masked_score)

    scores = score_block()
    top_score = jnp.max(scores, axis=-1, keepdims=True)
    expo_scores = jnp.exp(scores - top_score)
    total_mass = jnp.sum(expo_scores, axis=-1, keepdims=True)
    attn_probs = expo_scores / total_mass
    probs_low = attn_probs.astype(bf16)
    mixture = jnp.einsum("mhts,msd->mthd", probs_low, value_low, preferred_element_type=f32)
    mixture = mixture.reshape(members * rows, heads * HD).astype(bf16)
    attn_sum = scatter_group(dot(mixture[:rows], out_full), dot(mixture[rows:], out_full).astype(bf16))
    residual = token_rows + living * attn_sum

    ffn_out, ffn_normed, ffn_factor = normalize(residual, mlp_scale)
    ffn_in = gather_group(to_shards(ffn_out.astype(bf16), members, ring))
    gate_act = dot(ffn_in, gate_full)
    up_act = dot(ffn_in, up_full)
    sigmoid_gate = jax.nn.sigmoid(gate_act)
    silu_gate = gate_act * sigmoid_gate
    hidden = (silu_gate * up_act).astype(bf16)

    hidden_grad = dot_nt(ffn_grad, down_full)
    gate_grad = (
        hidden_grad * up_act * sigmoid_gate * (1.0 + gate_act * (1.0 - sigmoid_gate))
    ).astype(bf16)
    up_grad = (hidden_grad * silu_gate).astype(bf16)
    ffn_in_grad = scatter_group(
        dot_nt(gate_grad[:rows], gate_full) + dot_nt(up_grad[:rows], up_full),
        (dot_nt(gate_grad[rows:], gate_full) + dot_nt(up_grad[rows:], up_full)).astype(bf16),
    )
    ffn_in_grad = from_shards(ffn_in_grad, members, ring)
    down_wgrad = dot_tn(hidden, ffn_grad).astype(bf16)
    gate_wgrad = dot_tn(ffn_in, gate_grad).astype(bf16)
    up_wgrad = dot_tn(ffn_in, up_grad).astype(bf16)
    down_share = lax.psum_scatter(down_wgrad, "fsdp", scatter_dimension=0, tiled=True)
    gate_share = lax.psum_scatter(gate_wgrad, "fsdp", scatter_dimension=0, tiled=True)
    up_share = lax.psum_scatter(up_wgrad, "fsdp", scatter_dimension=0, tiled=True)
    ffn_sum = scatter_group(dot(hidden[:rows], down_full), dot(hidden[rows:], down_full).astype(bf16))
    layer_out = (residual + living * ffn_sum).astype(bf16)

    residual_back, mlp_scale_grad = normalize_back(ffn_in_grad, ffn_normed, ffn_factor, mlp_scale)
    residual_grad = grad_rows + residual_back
    attn_grad = gather_group((living * residual_grad).astype(bf16))
    out_wgrad = dot_tn(mixture, attn_grad).astype(bf16)
    out_share = lax.psum_scatter(out_wgrad, "fsdp", scatter_dimension=0, tiled=True)
    mixture_grad = dot_nt(attn_grad, out_full).astype(bf16).reshape(members, rows, heads, HD)
    probs_grad = jnp.einsum("mthd,msd->mhts", mixture_grad, value_low, preferred_element_type=f32)
    row_dot = jnp.sum(attn_probs * probs_grad, axis=-1, keepdims=True)
    score_grad = (attn_probs * (probs_grad - row_dot)).astype(bf16)
    query_rot_grad = (
        jnp.einsum("mhts,msd->mthd", score_grad, key_rot, preferred_element_type=f32) * score_scale
    )
    key_rot_grad = (
        jnp.einsum("mhts,mthd->msd", score_grad, query_rot, preferred_element_type=f32) * score_scale
    ).reshape(members * rows, HD)
    value_grad = jnp.einsum(
        "mhts,mthd->msd", probs_low, mixture_grad, preferred_element_type=f32
    ).reshape(members * rows, HD)
    query_rot_grad = query_rot_grad.reshape(members * rows, heads, HD)
    query_grad = rotate(query_rot_grad, cos_part[:, None, :], -sin_part[:, None, :])
    query_grad = query_grad.astype(bf16).reshape(members * rows, heads * HD)
    query_wgrad = dot_tn(latent_in, query_grad).astype(bf16)
    query_share = lax.psum_scatter(query_wgrad, "fsdp", scatter_dimension=0, tiled=True)
    packed_grad = jnp.concatenate([dot_nt(query_grad, query_full), key_rot_grad, value_grad], axis=1)
    packed_grad = scatter_group(packed_grad[:rows], packed_grad[rows:].astype(bf16))
    latent_in_grad = from_shards(packed_grad[:, :latent_width], members, ring)
    key_grad = rotate(
        packed_grad[:, latent_width : latent_width + HD], cos_part[:rows], -sin_part[:rows]
    ).astype(bf16)
    value_grad = packed_grad[:, latent_width + HD :].astype(bf16)
    latent_back, latent_scale_grad = normalize_back(
        latent_in_grad, latent_normed, latent_factor, latent_scale
    )
    qkv_grad = jnp.concatenate([latent_back.astype(bf16), key_grad, value_grad], axis=1)
    attn_in_grad = dot_nt(qkv_grad, qkv_full)
    token_back, attn_scale_grad = normalize_back(attn_in_grad, attn_normed, attn_factor, attn_scale)
    tokens_grad = residual_grad + token_back

    small_grad = dot_tn(attn_in, qkv_grad)
    latent_column = jnp.pad(
        latent_scale_grad.reshape(devices, -1), ((0, 0), (0, d_rows - query_gain.shape[0]))
    ).reshape(-1)
    columns = jnp.stack([attn_scale_grad, mlp_scale_grad, latent_column])
    columns = jnp.pad(columns, ((0, 128 - 3), (0, 0))).T
    small_grad = jnp.concatenate([small_grad, columns], axis=1).astype(bf16)
    small_grad = small_grad.reshape(members, ring, d_rows, -1).transpose(1, 0, 2, 3)
    small_grad = small_grad.reshape(devices * d_rows, -1)
    small_share = lax.psum_scatter(small_grad, "fsdp", scatter_dimension=0, tiled=True)
    small_share = lax.psum_scatter(small_share, "dp", scatter_dimension=0, tiled=True).astype(f32)
    return (
        layer_out,
        tokens_grad,
        small_share[:, latent_width + 2 * HD],
        small_share[:, :latent_width],
        small_share[: query_gain.shape[0], latent_width + 2 * HD + 2],
        columns_back(query_share, members),
        small_share[:, latent_width : latent_width + HD],
        small_share[:, latent_width + HD : latent_width + 2 * HD],
        out_share.astype(f32),
        small_share[:, latent_width + 2 * HD + 1],
        columns_back(gate_share, members),
        columns_back(up_share, members),
        down_share.astype(f32),
    )


def solution(mesh):
    members, ring = mesh.shape["dp"], mesh.shape["fsdp"]
    matrix, vector = P(ALL, None), P(ALL)
    in_specs = (
        matrix,
        matrix,
        vector,
        matrix,
        vector,
        matrix,
        matrix,
        matrix,
        matrix,
        vector,
        matrix,
        matrix,
        matrix,
        matrix,
    )
    out_specs = (
        matrix,
        matrix,
        vector,
        matrix,
        vector,
        matrix,
        matrix,
        matrix,
        matrix,
        vector,
        matrix,
        matrix,
        matrix,
    )

    def body(*args):
        return shards(members, ring, *args)

    return jax.shard_map(body, mesh=mesh, in_specs=in_specs, out_specs=out_specs, check_vma=False)
```

```python
import functools
import math

import jax
import jax.numpy as jnp
from jax import lax
from jax.experimental import pallas as pl
from jax.experimental.pallas import tpu as pltpu
from jax.sharding import PartitionSpec as P

H = 16
HD = 256
PAD = 32

eps = 1e-06
rope_base = 10000.0
masked_score = -1e30
ALL = ("y", "x", "zh", "zl", "r")
DP = ("y", "x")
GROUP = ("x", "y")
RING = ("zh", "zl", "r")
f32 = jnp.float32
bf16 = jnp.bfloat16


def layout(lengths, row_total):
    padded = (lengths + PAD - 1) // PAD * PAD
    count = lengths.shape[0]
    ends = []
    for s in range(count):
        ends.append(padded[s] if s == 0 else ends[-1] + padded[s])
    row = lax.broadcasted_iota(jnp.int32, (row_total, 1), 0)
    segment = jnp.zeros_like(row)
    start = jnp.zeros_like(row)
    alive = jnp.zeros(row.shape, jnp.bool_)
    for s in range(count):
        first = ends[s] - padded[s]
        member = (row >= first) & (row < ends[s])
        segment = jnp.where(member, s + 1, segment)
        start = jnp.where(member, first, start)
        alive = alive | (member & (row - first < lengths[s]))
    return row - start, alive, segment


def angles(offset, head_size):
    half_width = head_size // 2
    frequency = jnp.exp(
        jnp.arange(half_width, dtype=f32) * (-2.0 * math.log(rope_base) / head_size)
    )
    phase = offset.astype(f32) * frequency[None, :]
    return (jnp.cos(phase), jnp.sin(phase))


def rotate(values, cos_part, sin_part):
    half_width = values.shape[-1] // 2
    first_half = values[..., :half_width]
    second_half = values[..., half_width:]
    return jnp.concatenate(
        [
            first_half * cos_part - second_half * sin_part,
            second_half * cos_part + first_half * sin_part,
        ],
        axis=-1,
    )


def normalize(values, scale_gain):
    factor = lax.rsqrt(jnp.mean(values * values, axis=-1, keepdims=True) + eps)
    normed = values * factor
    return (normed * scale_gain, normed, factor)


def normalize_back(upstream, normed, factor, scale_gain):
    scaled = upstream * scale_gain
    gain_grad = jnp.sum(upstream * normed, axis=0)
    inner_mean = jnp.mean(scaled * normed, axis=-1, keepdims=True)
    return (factor * (scaled - normed * inner_mean), gain_grad)


def dot(a, b):
    return jnp.dot(a, b, preferred_element_type=f32)


def dot_nt(a, b):
    return lax.dot_general(a, b, (((1,), (1,)), ((), ())), preferred_element_type=f32)


def dot_tn(a, b):
    return lax.dot_general(a, b, (((0,), (0,)), ((), ())), preferred_element_type=f32)


def after(values, *others):
    return lax.optimization_barrier((values, others))[0]


def trade(values, axis):
    return lax.ppermute(values, axis, [(0, 1), (1, 0)])


def gather_quad(values, first, second):
    half = values.shape[0] // 2
    one = trade(values, first)
    two = trade(values, second)
    three = jnp.concatenate([trade(two[:half], first), trade(one[half:], second)], axis=0)
    return [values, one, two, three]


def scatter_quad(slots, first, second):
    s0, s1, s2, s3 = slots
    half = s0.shape[0] // 2
    ra = trade(jnp.concatenate([s1[:half], s3[:half]], axis=0), first)
    rb = trade(jnp.concatenate([s2[half:], s3[half:]], axis=0), second)
    pass_a = (s2[:half].astype(f32) + ra[half:].astype(f32)).astype(bf16)
    pass_b = (s1[half:].astype(f32) + rb[half:].astype(f32)).astype(bf16)
    last_a = trade(pass_a, second)
    last_b = trade(pass_b, first)
    top = s0[:half].astype(f32) + ra[:half].astype(f32) + last_a.astype(f32)
    low = s0[half:].astype(f32) + rb[:half].astype(f32) + last_b.astype(f32)
    return jnp.concatenate([top, low], axis=0)


def scatter_rows(own, others, first, second):
    rows = own.shape[0]
    slots = [own] + [others[i * rows : (i + 1) * rows] for i in range(3)]
    return scatter_quad(slots, first, second)


def split_cores(values, cores):
    if cores != 2:
        return lax.psum_scatter(values, "r", scatter_dimension=4, tiled=False), None
    core = lax.axis_index("r")
    mine = lax.dynamic_index_in_dim(values, core, 4, keepdims=False)
    theirs = lax.dynamic_index_in_dim(values, 1 - core, 4, keepdims=False)
    return mine, trade(theirs.reshape(-1, values.shape[-1]), "r").reshape(mine.shape)


def join_cores(mine, theirs):
    if theirs is None:
        return mine
    return (mine.astype(f32) + theirs.astype(f32)).astype(bf16)


def scatter_small(values, cores):
    n, c = values.shape[5:]
    total = join_cores(*split_cores(values, cores)).reshape(4, 4, n, c)
    me = lax.axis_index("y") * 2 + lax.axis_index("x")
    slots = [lax.dynamic_index_in_dim(total, me ^ code, 0, keepdims=False) for code in range(4)]
    total = scatter_quad([v.reshape(4 * n, c) for v in slots], "x", "y").astype(bf16).reshape(4, n, c)
    me = lax.axis_index("zh") * 2 + lax.axis_index("zl")
    slots = [lax.dynamic_index_in_dim(total, me ^ code, 0, keepdims=False) for code in range(4)]
    return scatter_quad(slots, "zl", "zh")


def turn(values, cos_part, sin_part):
    half = values.shape[-1] // 2
    one, two = values[:, :half], values[:, half:]
    return jnp.concatenate([one * cos_part - two * sin_part, two * cos_part + one * sin_part], axis=-1)


def probabilities(query_rot, key_rot, seg_ref, code_ref):
    rows = query_rot.shape[0]
    scores = dot_nt(query_rot, key_rot) * (1.0 / math.sqrt(HD))
    i = lax.broadcasted_iota(jnp.int32, (rows, rows), 0)
    j = lax.broadcasted_iota(jnp.int32, (rows, rows), 1)
    allowed = ((seg_ref[...] == code_ref[0]) & (j <= i)) | (i == j)
    scores = jnp.where(allowed, scores, masked_score)
    expo = jnp.exp(scores - jnp.max(scores, axis=-1, keepdims=True))
    return expo / jnp.sum(expo, axis=-1, keepdims=True)


def attend_kernel(
    latent_ref, weight_ref, key_ref, value_ref, cos_ref, sin_ref, seg_ref, code_ref, query_ref, mix_ref
):
    query_rot = turn(dot(latent_ref[...], weight_ref[...]), cos_ref[...], sin_ref[...]).astype(bf16)
    query_ref[...] = query_rot
    probs = probabilities(query_rot, key_ref[...], seg_ref, code_ref)
    mix_ref[...] = dot(probs.astype(bf16), value_ref[...]).astype(bf16)


def attend(packed, query_full, cos_part, sin_part, segment, code, rows, heads):
    total, latent_width = packed.shape[0], query_full.shape[0]
    last = latent_width // HD
    block = pl.BlockSpec((rows, HD), lambda m, h: (m, h))
    trig = pl.BlockSpec((rows, HD // 2), lambda m, h: (m, 0))
    out = jax.ShapeDtypeStruct((total, heads * HD), bf16)
    return pl.pallas_call(
        attend_kernel,
        grid=(total // rows, heads),
        in_specs=[
            pl.BlockSpec((rows, latent_width), lambda m, h: (m, 0)),
            pl.BlockSpec((latent_width, HD), lambda m, h: (0, h)),
            pl.BlockSpec((rows, HD), lambda m, h: (m, last)),
            pl.BlockSpec((rows, HD), lambda m, h: (m, last + 1)),
            trig,
            trig,
            pl.BlockSpec((rows, 1), lambda m, h: (m, 0)),
            pl.BlockSpec((1, 1, rows), lambda m, h: (m, 0, 0)),
        ],
        out_specs=[block, block],
        out_shape=[out, out],
        compiler_params=pltpu.CompilerParams(vmem_limit_bytes=32 * 2**20),
        cost_estimate=pl.CostEstimate(
            flops=2 * total * heads * HD * (latent_width + 2 * rows),
            bytes_accessed=total * heads * HD * 4 + total * latent_width * 3,
            transcendentals=total * heads * rows,
        ),
    )(packed, query_full, packed, packed, cos_part, sin_part, segment, code)


def attend_back_kernel(
    heads,
    grad_ref,
    out_ref,
    weight_ref,
    query_ref,
    key_ref,
    value_ref,
    cos_ref,
    sin_ref,
    seg_ref,
    code_ref,
    query_grad_ref,
    packed_ref,
    total_ref,
):
    head = pl.program_id(1)
    latent_width = weight_ref.shape[0]
    scale = 1.0 / math.sqrt(HD)
    query_rot, key_rot, value_low = query_ref[...], key_ref[...], value_ref[...]
    mixture_grad = dot_nt(grad_ref[...], out_ref[...]).astype(bf16)
    probs = probabilities(query_rot, key_rot, seg_ref, code_ref)
    probs_grad = dot_nt(mixture_grad, value_low)
    row_dot = jnp.sum(probs * probs_grad, axis=-1, keepdims=True)
    score_grad = (probs * (probs_grad - row_dot)).astype(bf16)
    query_rot_grad = dot(score_grad, key_rot) * scale
    query_grad = turn(query_rot_grad, cos_ref[...], -sin_ref[...]).astype(bf16)
    query_grad_ref[...] = query_grad

    @pl.when(head == 0)
    def _():
        total_ref[...] = jnp.zeros_like(total_ref)

    total_ref[:, :latent_width] += dot_nt(query_grad, weight_ref[...])
    total_ref[:, latent_width : latent_width + HD] += dot_tn(score_grad, query_rot) * scale
    total_ref[:, latent_width + HD :] += dot_tn(probs.astype(bf16), mixture_grad)

    @pl.when(head == heads - 1)
    def _():
        packed_ref[...] = total_ref[...].astype(bf16)


def attend_back(attn_grad, out_full, query_full, query_rot, packed, cos_part, sin_part, segment, code, rows, heads):
    total, width = attn_grad.shape
    latent_width = query_full.shape[0]
    last = latent_width // HD
    block = pl.BlockSpec((rows, HD), lambda m, h: (m, h))
    trig = pl.BlockSpec((rows, HD // 2), lambda m, h: (m, 0))
    return pl.pallas_call(
        functools.partial(attend_back_kernel, heads),
        grid=(total // rows, heads),
        in_specs=[
            pl.BlockSpec((rows, width), lambda m, h: (m, 0)),
            pl.BlockSpec((HD, width), lambda m, h: (h, 0)),
            pl.BlockSpec((latent_width, HD), lambda m, h: (0, h)),
            block,
            pl.BlockSpec((rows, HD), lambda m, h: (m, last)),
            pl.BlockSpec((rows, HD), lambda m, h: (m, last + 1)),
            trig,
            trig,
            pl.BlockSpec((rows, 1), lambda m, h: (m, 0)),
            pl.BlockSpec((1, 1, rows), lambda m, h: (m, 0, 0)),
        ],
        out_specs=[block, pl.BlockSpec((rows, packed.shape[1]), lambda m, h: (m, 0))],
        out_shape=[
            jax.ShapeDtypeStruct((total, heads * HD), bf16),
            jax.ShapeDtypeStruct(packed.shape, bf16),
        ],
        scratch_shapes=[pltpu.VMEM((rows, packed.shape[1]), f32)],
        compiler_params=pltpu.CompilerParams(vmem_limit_bytes=32 * 2**20),
        cost_estimate=pl.CostEstimate(
            flops=2 * total * heads * HD * (width + latent_width + 5 * rows),
            bytes_accessed=total * heads * HD * 8 + total * width * 4,
            transcendentals=total * heads * rows,
        ),
    )(attn_grad, out_full, query_full, query_rot, packed, packed, cos_part, sin_part, segment, code)


def by_member(values, members):
    me = lax.axis_index(DP)
    step = values.shape[1] // members
    return jnp.concatenate(
        [lax.dynamic_slice_in_dim(values, (me ^ slot) * step, step, 1) for slot in range(members)], axis=1
    )


def columns_in(weight, members):
    rows, width = weight.shape
    cut = weight.reshape(rows, members, width // members).transpose(1, 0, 2)
    return lax.all_to_all(cut, DP, 0, 0, tiled=True)


def columns_back(grad):
    members, rows, width = grad.shape
    cut = lax.all_to_all(grad, DP, 0, 0, tiled=True)
    return cut.transpose(1, 0, 2).reshape(rows, members * width).astype(f32)


def shards(
    members,
    ring,
    cores,
    tokens,
    lengths,
    attn_gain,
    query_down,
    query_gain,
    query_up,
    key_weight,
    value_weight,
    out_weight,
    mlp_gain,
    gate_weight,
    up_weight,
    down_weight,
    cotangent,
):
    rows = tokens.shape[0]
    width = tokens.shape[1]
    latent_width = query_down.shape[1]
    heads = H // members
    devices = members * ring
    score_scale = 1.0 / math.sqrt(HD)
    d_rows = query_down.shape[0]

    def column(v):
        v = v.astype(bf16).reshape(-1, 1)
        return jnp.pad(v, ((0, d_rows - v.shape[0]), (0, 0)))

    extra = jnp.concatenate(
        [column(attn_gain), column(mlp_gain), column(query_gain), column(lengths[0])], axis=1
    )
    extra = jnp.pad(extra, ((0, 0), (0, 128 - extra.shape[1])))
    small = jnp.concatenate([query_down, key_weight, value_weight, extra], axis=1)
    small = lax.all_gather(small, RING, axis=0, tiled=True)
    gate_up = jnp.stack([gate_weight, up_weight]).reshape(2, d_rows, members, -1)
    gate_up = gate_up.transpose(2, 1, 0, 3).reshape(members, d_rows, -1)
    gate_up = lax.all_to_all(gate_up, DP, 0, 0, tiled=True)
    query_own = columns_in(query_up, members)
    small = after(small, gate_up, query_own)
    small_parts = gather_quad(small, *GROUP)
    query_full = lax.all_gather(query_own, RING, axis=1, tiled=True)
    query_full = query_full.reshape(latent_width, heads * HD)
    out_full = lax.all_gather(after(out_weight, small), RING, axis=0, tiled=True)
    gate_up = after(gate_up, small)
    gate_up = lax.all_gather(gate_up, RING, axis=1, tiled=True).reshape(width, -1)
    cut = gate_up.shape[1] // 2
    down_full = lax.all_gather(after(down_weight, small), RING, axis=0, tiled=True)

    me, lane = lax.axis_index(DP), lax.axis_index(RING)
    qkv_parts = jnp.concatenate([part[:, : latent_width + 2 * HD] for part in small_parts], axis=0)
    extra = jnp.stack([part[:, latent_width + 2 * HD :] for part in small_parts])
    extra = [lax.dynamic_index_in_dim(extra, me ^ slot, 0, keepdims=False) for slot in range(members)]
    extra = jnp.concatenate(extra, axis=0).astype(f32).T
    attn_scale = extra[0:1]
    mlp_scale = extra[1:2]
    latent_scale = extra[2].reshape(devices, d_rows)[:, : query_gain.shape[0]].reshape(1, -1)
    all_lengths = extra[3].reshape(devices, d_rows)[:, : lengths.shape[1]].astype(jnp.int32)

    own_offset, own_alive, own_segment = layout(lengths[0], rows)
    living = own_alive.astype(f32)
    own_cos, own_sin = angles(own_offset, HD)
    parts = [(own_offset, own_alive, own_segment)]
    for slot in range(1, members):
        mine = lax.dynamic_slice_in_dim(all_lengths, (me ^ slot) * ring + lane, 1, 0)[0]
        parts.append(layout(mine, rows))
    offset = jnp.concatenate([p[0] for p in parts], axis=0)
    segment = jnp.concatenate([p[2] for p in parts], axis=0)
    code = jnp.stack([jnp.where(p[1], p[2], -1).reshape(1, rows) for p in parts])
    cos_part, sin_part = angles(offset, HD)

    grad_rows = cotangent.astype(f32)
    ffn_grad = jnp.concatenate(gather_quad((living * grad_rows).astype(bf16), *GROUP), axis=0)
    token_rows = tokens.astype(f32)
    attn_out, attn_normed, attn_factor = normalize(token_rows, attn_scale)
    attn_in = attn_out.astype(bf16)
    low = dot(by_member(attn_in, members), qkv_parts)
    latent = low[:, :latent_width]
    latent_out, latent_normed, latent_factor = normalize(latent, latent_scale)
    latent_in = latent_out.astype(bf16)
    key_own = rotate(low[:, latent_width : latent_width + HD], own_cos, own_sin)
    value_own = low[:, latent_width + HD :]
    packed = jnp.concatenate([latent_in, key_own.astype(bf16), value_own.astype(bf16)], axis=1)
    packed = jnp.concatenate(gather_quad(after(packed, ffn_grad), *GROUP), axis=0)
    query_rot, mixture = attend(packed, query_full, cos_part, sin_part, segment, code, rows, heads)
    attn_sum = scatter_rows(
        dot(mixture[:rows], out_full), dot(mixture[rows:], out_full).astype(bf16), *GROUP
    )
    residual = token_rows + living * attn_sum

    ffn_out, ffn_normed, ffn_factor = normalize(residual, mlp_scale)
    ffn_in = jnp.concatenate(gather_quad(ffn_out.astype(bf16), *GROUP), axis=0)
    gate_up_act = dot(ffn_in, gate_up)
    gate_act, up_act = gate_up_act[:, :cut], gate_up_act[:, cut:]
    sigmoid_gate = jax.nn.sigmoid(gate_act)
    silu_gate = gate_act * sigmoid_gate
    hidden = (silu_gate * up_act).astype(bf16)

    down_wgrad = dot_tn(hidden, ffn_grad).astype(bf16)
    down_share = lax.psum_scatter(down_wgrad, RING, scatter_dimension=0, tiled=True)

    hidden_grad = dot_nt(after(ffn_grad, down_wgrad), down_full)
    gate_grad = (
        hidden_grad * up_act * sigmoid_gate * (1.0 + gate_act * (1.0 - sigmoid_gate))
    ).astype(bf16)
    up_grad = (hidden_grad * silu_gate).astype(bf16)
    gate_up_grad = jnp.concatenate([gate_grad, up_grad], axis=1)
    ffn_in_grad = scatter_rows(
        dot_nt(gate_up_grad[:rows], gate_up), dot_nt(gate_up_grad[rows:], gate_up).astype(bf16), *GROUP
    )
    gate_up_wgrad = dot_tn(ffn_in, gate_up_grad).astype(bf16)
    residual_back, mlp_scale_grad = normalize_back(ffn_in_grad, ffn_normed, ffn_factor, mlp_scale)
    residual_grad = grad_rows + residual_back
    attn_grad = (living * residual_grad).astype(bf16)
    attn_grad = after(attn_grad, down_share, gate_up_wgrad)
    gate_up_share = lax.psum_scatter(
        gate_up_wgrad.reshape(members, width // members, -1), RING, scatter_dimension=1, tiled=True
    )
    attn_grad = jnp.concatenate(gather_quad(attn_grad, *GROUP), axis=0)
    query_grad, packed_grad = attend_back(
        attn_grad, out_full, query_full, query_rot, packed, cos_part, sin_part, segment, code, rows, heads
    )
    hidden = after(hidden, query_grad)
    ffn_sum = scatter_rows(
        dot(hidden[:rows], down_full), dot(hidden[rows:], down_full).astype(bf16), *GROUP
    )
    layer_out = (residual + living * ffn_sum).astype(bf16)
    packed_grad = scatter_rows(packed_grad[:rows], packed_grad[rows:], *GROUP)
    packed_grad = after(packed_grad, gate_up_share)
    out_wgrad = dot_tn(after(mixture, gate_up_share), attn_grad).astype(bf16)
    out_share = lax.psum_scatter(out_wgrad, RING, scatter_dimension=0, tiled=True)
    query_wgrad = dot_tn(packed[:, :latent_width], after(query_grad, gate_up_share)).astype(bf16)
    query_wgrad = query_wgrad.reshape(members, latent_width // members, heads * HD)
    query_share = lax.psum_scatter(query_wgrad, RING, scatter_dimension=1, tiled=True)
    latent_in_grad = packed_grad[:, :latent_width]
    key_grad = rotate(
        packed_grad[:, latent_width : latent_width + HD], own_cos, -own_sin
    ).astype(bf16)
    value_grad = packed_grad[:, latent_width + HD :].astype(bf16)
    latent_back, latent_scale_grad = normalize_back(
        latent_in_grad, latent_normed, latent_factor, latent_scale
    )
    qkv_grad = jnp.concatenate([latent_back.astype(bf16), key_grad, value_grad], axis=1)
    attn_in_grad = by_member(dot_nt(qkv_grad, qkv_parts), members)
    token_back, attn_scale_grad = normalize_back(attn_in_grad, attn_normed, attn_factor, attn_scale)
    tokens_grad = residual_grad + token_back

    small_grad = dot_tn(attn_in, qkv_grad)
    latent_column = jnp.pad(
        latent_scale_grad.reshape(devices, -1), ((0, 0), (0, d_rows - query_gain.shape[0]))
    ).reshape(-1)
    columns = jnp.stack([attn_scale_grad, mlp_scale_grad, latent_column])
    columns = jnp.pad(columns, ((0, 128 - 3), (0, 0))).T
    small_grad = jnp.concatenate([small_grad, columns], axis=1).astype(bf16)
    gate_up_share = after(gate_up_share, small_grad)
    gate_up_share = lax.all_to_all(gate_up_share, DP, 0, 0, tiled=True)
    gate_up_share = gate_up_share.reshape(members, d_rows, 2, -1).transpose(2, 1, 0, 3)
    gate_up_share = gate_up_share.reshape(2, d_rows, -1).astype(f32)
    small_share = scatter_small(small_grad.reshape(2, 2, 2, 2, cores, d_rows, -1), cores)
    return (
        layer_out,
        tokens_grad,
        small_share[:, latent_width + 2 * HD],
        small_share[:, :latent_width],
        small_share[: query_gain.shape[0], latent_width + 2 * HD + 2],
        columns_back(query_share),
        small_share[:, latent_width : latent_width + HD],
        small_share[:, latent_width + HD : latent_width + 2 * HD],
        out_share.astype(f32),
        small_share[:, latent_width + 2 * HD + 1],
        gate_up_share[0],
        gate_up_share[1],
        down_share.astype(f32),
    )


def solution(mesh):
    members, ring = mesh.shape["dp"], mesh.shape["fsdp"]
    cores = mesh.devices.size // 16
    fine = jax.sharding.Mesh(mesh.devices.reshape(2, 2, 2, 2, cores), ALL)
    matrix, vector = P(ALL, None), P(ALL)
    in_specs = (
        matrix,
        matrix,
        vector,
        matrix,
        vector,
        matrix,
        matrix,
        matrix,
        matrix,
        vector,
        matrix,
        matrix,
        matrix,
        matrix,
    )
    out_specs = (
        matrix,
        matrix,
        vector,
        matrix,
        vector,
        matrix,
        matrix,
        matrix,
        matrix,
        vector,
        matrix,
        matrix,
        matrix,
    )

    def body(*args):
        return shards(members, ring, cores, *args)

    return jax.shard_map(body, mesh=fine, in_specs=in_specs, out_specs=out_specs, check_vma=False)
```

```python
import functools
import math

import jax
import jax.numpy as jnp
from jax import lax
from jax.experimental import pallas as pl
from jax.experimental.pallas import tpu as pltpu
from jax.sharding import PartitionSpec as P

H = 16
HD = 256
PAD = 32

eps = 1e-06
rope_base = 10000.0
masked_score = -1e30
ALL = ("y", "x", "zh", "zl", "r")
DP = ("y", "x")
GROUP = ("x", "y")
RING = ("zh", "zl", "r")
f32 = jnp.float32
bf16 = jnp.bfloat16


def layout(lengths, row_total):
    padded = (lengths + PAD - 1) // PAD * PAD
    count = lengths.shape[0]
    ends = []
    for s in range(count):
        ends.append(padded[s] if s == 0 else ends[-1] + padded[s])
    row = lax.broadcasted_iota(jnp.int32, (row_total, 1), 0)
    segment = jnp.zeros_like(row)
    start = jnp.zeros_like(row)
    alive = jnp.zeros(row.shape, jnp.bool_)
    for s in range(count):
        first = ends[s] - padded[s]
        member = (row >= first) & (row < ends[s])
        segment = jnp.where(member, s + 1, segment)
        start = jnp.where(member, first, start)
        alive = alive | (member & (row - first < lengths[s]))
    return row - start, alive, segment


def angles(offset, head_size):
    half_width = head_size // 2
    frequency = jnp.exp(
        jnp.arange(half_width, dtype=f32) * (-2.0 * math.log(rope_base) / head_size)
    )
    phase = offset.astype(f32) * frequency[None, :]
    return (jnp.cos(phase), jnp.sin(phase))


def rotate(values, cos_part, sin_part):
    half_width = values.shape[-1] // 2
    first_half = values[..., :half_width]
    second_half = values[..., half_width:]
    return jnp.concatenate(
        [
            first_half * cos_part - second_half * sin_part,
            second_half * cos_part + first_half * sin_part,
        ],
        axis=-1,
    )


def normalize(values, scale_gain):
    factor = lax.rsqrt(jnp.mean(values * values, axis=-1, keepdims=True) + eps)
    normed = values * factor
    return (normed * scale_gain, normed, factor)


def normalize_back(upstream, normed, factor, scale_gain):
    scaled = upstream * scale_gain
    gain_grad = jnp.sum(upstream * normed, axis=0)
    inner_mean = jnp.mean(scaled * normed, axis=-1, keepdims=True)
    return (factor * (scaled - normed * inner_mean), gain_grad)


def dot(a, b):
    return jnp.dot(a, b, preferred_element_type=f32)


def dot_nt(a, b):
    return lax.dot_general(a, b, (((1,), (1,)), ((), ())), preferred_element_type=f32)


def dot_tn(a, b):
    return lax.dot_general(a, b, (((0,), (0,)), ((), ())), preferred_element_type=f32)


def after(values, *others):
    return lax.optimization_barrier((values, others))[0]


def trade(values, axis):
    return lax.ppermute(values, axis, [(0, 1), (1, 0)])


def gather_quad(values, first, second):
    half = values.shape[0] // 2
    one = trade(values, first)
    two = trade(values, second)
    three = jnp.concatenate([trade(two[:half], first), trade(one[half:], second)], axis=0)
    return [values, one, two, three]


def fetch_first(values, first, second):
    return trade(values, first), trade(values, second)


def fetch_last(values, found, first, second):
    one, two = found
    half = values.shape[0] // 2
    return [values, one, two, trade(two[:half], first), trade(one[half:], second)]


def first_loads(slots):
    half = slots[1].shape[0] // 2
    return (
        jnp.concatenate([slots[1][:half], slots[3][:half]], axis=0),
        jnp.concatenate([slots[2][half:], slots[3][half:]], axis=0),
    )


def send_loads(loads, first, second):
    return trade(loads[0], first), trade(loads[1], second)


def last_loads(slots, sent):
    half, (ra, rb) = slots[1].shape[0] // 2, sent
    return (
        (slots[2][:half].astype(f32) + ra[half:].astype(f32)).astype(bf16),
        (slots[1][half:].astype(f32) + rb[half:].astype(f32)).astype(bf16),
    )


def sum_up(own, sent, last):
    half, own = own.shape[0] // 2, own.astype(f32)
    return jnp.concatenate(
        [
            own[:half] + sent[0][:half].astype(f32) + last[0].astype(f32),
            own[half:] + sent[1][:half].astype(f32) + last[1].astype(f32),
        ],
        axis=0,
    )


def send_first(slots, first, second):
    return send_loads(first_loads(slots), first, second)


def send_last(slots, sent, first, second):
    return sum_up(slots[0], sent, send_loads(last_loads(slots, sent), second, first))


def scatter_quad(slots, first, second):
    return send_last(slots, send_first(slots, first, second), first, second)


def scatter_rows(own, others, first, second):
    rows = own.shape[0]
    slots = [own] + [others[i * rows : (i + 1) * rows] for i in range(3)]
    return scatter_quad(slots, first, second)


def split_cores(values, cores):
    if cores != 2:
        return lax.psum_scatter(values, "r", scatter_dimension=4, tiled=False), None
    core = lax.axis_index("r")
    mine = lax.dynamic_index_in_dim(values, core, 4, keepdims=False)
    theirs = lax.dynamic_index_in_dim(values, 1 - core, 4, keepdims=False)
    return mine, trade(theirs.reshape(-1, values.shape[-1]), "r").reshape(mine.shape)


def join_cores(mine, theirs):
    if theirs is None:
        return mine
    return (mine.astype(f32) + theirs.astype(f32)).astype(bf16)


def small_first(values, cores):
    n, c = values.shape[5:]
    total = join_cores(*split_cores(values, cores)).reshape(4, 4 * n, c)
    me = lax.axis_index(DP)
    return [lax.dynamic_index_in_dim(total, me ^ code, 0, keepdims=False) for code in range(4)]


def small_middle(slots):
    total = scatter_quad(slots, *GROUP).astype(bf16)
    total = total.reshape(4, -1, total.shape[1])
    me = lax.axis_index("zh") * 2 + lax.axis_index("zl")
    return [lax.dynamic_index_in_dim(total, me ^ code, 0, keepdims=False) for code in range(4)]


def swap_blocks(block):
    me = lax.axis_index(DP)
    found = [block(me)]
    for code in (1, 2, 3):
        found.append(lax.ppermute(block(me ^ code), DP, [(i, i ^ code) for i in range(4)]))
    return found


def in_order(found):
    me, found = lax.axis_index(DP), jnp.stack(found)
    return [lax.dynamic_index_in_dim(found, me ^ k, 0, keepdims=False) for k in range(4)]


def take_columns(weight, k, members):
    step = weight.shape[1] // members
    return lax.dynamic_slice_in_dim(weight, k * step, step, 1)


def turn(values, cos_part, sin_part):
    half = values.shape[-1] // 2
    one, two = values[:, :half], values[:, half:]
    return jnp.concatenate([one * cos_part - two * sin_part, two * cos_part + one * sin_part], axis=-1)


def spans(lengths_ref, member):
    first, found = 0, []
    for s in range(lengths_ref.shape[1]):
        length = lengths_ref[member, s]
        end = first + (length + PAD - 1) // PAD * PAD
        found.append((first, end, first + length))
        first = end
    return found


def fill_angles(lengths_ref, cos_ref, sin_ref):
    rows, half = cos_ref.shape
    row = lax.broadcasted_iota(jnp.int32, (rows, half), 0)
    position = row
    for first, end, _ in spans(lengths_ref, pl.program_id(0)):
        position = jnp.where((row >= first) & (row < end), row - first, position)
    step = lax.broadcasted_iota(jnp.int32, (rows, half), 1).astype(f32)
    phase = position.astype(f32) * jnp.exp(step * (-math.log(rope_base) / half))
    cos_ref[...] = jnp.cos(phase)
    sin_ref[...] = jnp.sin(phase)


def probabilities(query_rot, key_rot, lengths_ref):
    rows = query_rot.shape[0]
    scores = dot_nt(query_rot, key_rot) * (1.0 / math.sqrt(HD))
    i = lax.broadcasted_iota(jnp.int32, (rows, rows), 0)
    j = lax.broadcasted_iota(jnp.int32, (rows, rows), 1)
    allowed = i == j
    for first, end, live in spans(lengths_ref, pl.program_id(0)):
        allowed = allowed | ((i >= first) & (i < end) & (j >= first) & (j < live) & (j <= i))
    scores = jnp.where(allowed, scores, masked_score)
    expo = jnp.exp(scores - jnp.max(scores, axis=-1, keepdims=True))
    return expo / jnp.sum(expo, axis=-1, keepdims=True)


def attend_kernel(
    lengths_ref, latent_ref, weight_ref, key_ref, value_ref, query_ref, mix_ref, cos_ref, sin_ref
):
    @pl.when(pl.program_id(1) == 0)
    def _():
        fill_angles(lengths_ref, cos_ref, sin_ref)

    query_rot = turn(dot(latent_ref[...], weight_ref[...]), cos_ref[...], sin_ref[...]).astype(bf16)
    query_ref[...] = query_rot
    probs = probabilities(query_rot, key_ref[...], lengths_ref)
    mix_ref[...] = dot(probs.astype(bf16), value_ref[...]).astype(bf16)


def attend(lengths, packed, query_full, rows, heads):
    total, latent_width = packed.shape[0], query_full.shape[0]
    last = latent_width // HD
    block = pl.BlockSpec((rows, HD), lambda m, h, s: (m, h))
    out = jax.ShapeDtypeStruct((total, heads * HD), bf16)
    return pl.pallas_call(
        attend_kernel,
        grid_spec=pltpu.PrefetchScalarGridSpec(
            num_scalar_prefetch=1,
            grid=(total // rows, heads),
            in_specs=[
                pl.BlockSpec((rows, latent_width), lambda m, h, s: (m, 0)),
                pl.BlockSpec((latent_width, HD), lambda m, h, s: (0, h)),
                pl.BlockSpec((rows, HD), lambda m, h, s: (m, last)),
                pl.BlockSpec((rows, HD), lambda m, h, s: (m, last + 1)),
            ],
            out_specs=[block, block],
            scratch_shapes=[pltpu.VMEM((rows, HD // 2), f32), pltpu.VMEM((rows, HD // 2), f32)],
        ),
        out_shape=[out, out],
        compiler_params=pltpu.CompilerParams(vmem_limit_bytes=32 * 2**20),
        cost_estimate=pl.CostEstimate(
            flops=2 * total * heads * HD * (latent_width + 2 * rows),
            bytes_accessed=total * heads * HD * 4 + total * latent_width * 3,
            transcendentals=total * heads * rows,
        ),
    )(lengths, packed, query_full, packed, packed)


def attend_back_kernel(
    members,
    heads,
    lengths_ref,
    grad_ref,
    out_ref,
    weight_ref,
    query_ref,
    latent_ref,
    key_ref,
    value_ref,
    mix_ref,
    packed_ref,
    out_grad_ref,
    weight_grad_ref,
    total_ref,
    out_total_ref,
    weight_total_ref,
    cos_ref,
    sin_ref,
):
    member, head = pl.program_id(0), pl.program_id(1)

    @pl.when(head == 0)
    def _():
        fill_angles(lengths_ref, cos_ref, sin_ref)
        total_ref[...] = jnp.zeros_like(total_ref)

    @pl.when(member == 0)
    def _():
        out_total_ref[head] = jnp.zeros_like(out_total_ref.at[0])
        weight_total_ref[head] = jnp.zeros_like(weight_total_ref.at[0])

    latent_width = weight_ref.shape[0]
    scale = 1.0 / math.sqrt(HD)
    query_rot, key_rot, value_low = query_ref[...], key_ref[...], value_ref[...]
    mixture_grad = dot_nt(grad_ref[...], out_ref[...]).astype(bf16)
    out_total_ref[head] += dot_tn(mix_ref[...], grad_ref[...])
    probs = probabilities(query_rot, key_rot, lengths_ref)
    probs_grad = dot_nt(mixture_grad, value_low)
    row_dot = jnp.sum(probs * probs_grad, axis=-1, keepdims=True)
    score_grad = (probs * (probs_grad - row_dot)).astype(bf16)
    query_rot_grad = dot(score_grad, key_rot) * scale
    query_grad = turn(query_rot_grad, cos_ref[...], -sin_ref[...]).astype(bf16)
    weight_total_ref[head] += dot_tn(latent_ref[...], query_grad)
    total_ref[:, :latent_width] += dot_nt(query_grad, weight_ref[...])
    total_ref[:, latent_width : latent_width + HD] += dot_tn(score_grad, query_rot) * scale
    total_ref[:, latent_width + HD :] += dot_tn(probs.astype(bf16), mixture_grad)

    @pl.when(head == heads - 1)
    def _():
        packed_ref[...] = total_ref[...].astype(bf16)

    @pl.when(member == members - 1)
    def _():
        out_grad_ref[...] = out_total_ref[head].astype(bf16)
        weight_grad_ref[...] = weight_total_ref[head].astype(bf16)


def attend_back(lengths, attn_grad, out_full, query_full, query_rot, mixture, packed, rows, heads):
    total, width = attn_grad.shape
    latent_width = query_full.shape[0]
    last, members = latent_width // HD, total // rows
    block = pl.BlockSpec((rows, HD), lambda m, h, s: (m, h))

    def when_last(m, h):
        return jnp.where(m == members - 1, h, 0)

    return pl.pallas_call(
        functools.partial(attend_back_kernel, members, heads),
        grid_spec=pltpu.PrefetchScalarGridSpec(
            num_scalar_prefetch=1,
            grid=(members, heads),
            in_specs=[
                pl.BlockSpec((rows, width), lambda m, h, s: (m, 0)),
                pl.BlockSpec((HD, width), lambda m, h, s: (h, 0)),
                pl.BlockSpec((latent_width, HD), lambda m, h, s: (0, h)),
                block,
                pl.BlockSpec((rows, latent_width), lambda m, h, s: (m, 0)),
                pl.BlockSpec((rows, HD), lambda m, h, s: (m, last)),
                pl.BlockSpec((rows, HD), lambda m, h, s: (m, last + 1)),
                block,
            ],
            out_specs=[
                pl.BlockSpec((rows, packed.shape[1]), lambda m, h, s: (m, 0)),
                pl.BlockSpec((HD, width), lambda m, h, s: (when_last(m, h), 0)),
                pl.BlockSpec((latent_width, HD), lambda m, h, s: (0, when_last(m, h))),
            ],
            scratch_shapes=[
                pltpu.VMEM((rows, packed.shape[1]), f32),
                pltpu.VMEM((heads, HD, width), f32),
                pltpu.VMEM((heads, latent_width, HD), f32),
                pltpu.VMEM((rows, HD // 2), f32),
                pltpu.VMEM((rows, HD // 2), f32),
            ],
        ),
        out_shape=[
            jax.ShapeDtypeStruct(packed.shape, bf16),
            jax.ShapeDtypeStruct((heads * HD, width), bf16),
            jax.ShapeDtypeStruct((latent_width, heads * HD), bf16),
        ],
        compiler_params=pltpu.CompilerParams(vmem_limit_bytes=48 * 2**20),
        cost_estimate=pl.CostEstimate(
            flops=2 * total * heads * HD * (2 * width + 2 * latent_width + 5 * rows),
            bytes_accessed=total * heads * HD * 8 + total * width * 4,
            transcendentals=total * heads * rows,
        ),
    )(lengths, attn_grad, out_full, query_full, query_rot, packed, packed, packed, mixture)


def by_member(values, members):
    me = lax.axis_index(DP)
    step = values.shape[1] // members
    return jnp.concatenate(
        [lax.dynamic_slice_in_dim(values, (me ^ slot) * step, step, 1) for slot in range(members)], axis=1
    )


def shards(
    members,
    ring,
    cores,
    tokens,
    lengths,
    attn_gain,
    query_down,
    query_gain,
    query_up,
    key_weight,
    value_weight,
    out_weight,
    mlp_gain,
    gate_weight,
    up_weight,
    down_weight,
    cotangent,
):
    rows = tokens.shape[0]
    width = tokens.shape[1]
    latent_width = query_down.shape[1]
    heads = H // members
    devices = members * ring
    score_scale = 1.0 / math.sqrt(HD)
    d_rows = query_down.shape[0]

    def column(v):
        v = v.astype(bf16).reshape(-1, 1)
        return jnp.pad(v, ((0, d_rows - v.shape[0]), (0, 0)))

    own_offset, own_alive, _ = layout(lengths[0], rows)
    living = own_alive.astype(f32)
    own_cos, own_sin = angles(own_offset, HD)
    grad_rows = cotangent.astype(f32)
    ffn_grad_own = (living * grad_rows).astype(bf16)

    extra = jnp.concatenate(
        [column(attn_gain), column(mlp_gain), column(query_gain), column(lengths[0])], axis=1
    )
    extra = jnp.pad(extra, ((0, 0), (0, 128 - extra.shape[1])))
    small = jnp.concatenate([query_down, key_weight, value_weight, extra], axis=1)
    small = lax.all_gather(small, RING, axis=0, tiled=True)
    query_own = jnp.stack(in_order(swap_blocks(lambda k: take_columns(query_up, k, members))))
    gate_up_own = swap_blocks(
        lambda k: jnp.concatenate(
            [take_columns(gate_weight, k, members), take_columns(up_weight, k, members)], axis=1
        )
    )
    gate_up_own = jnp.stack(in_order(gate_up_own))
    query_own = after(query_own, gate_up_own)
    small_parts = gather_quad(after(small, query_own), *GROUP)
    query_full = lax.all_gather(query_own, RING, axis=1, tiled=True)
    query_full = query_full.reshape(latent_width, heads * HD)
    out_full = lax.all_gather(after(out_weight, small), RING, axis=0, tiled=True)
    gate_up = lax.all_gather(after(gate_up_own, small), RING, axis=1, tiled=True).reshape(width, -1)
    cut = gate_up.shape[1] // 2
    down_full = lax.all_gather(after(down_weight, small), RING, axis=0, tiled=True)

    me, lane = lax.axis_index(DP), lax.axis_index(RING)
    qkv_width = latent_width + 2 * HD
    qkv_parts = jnp.concatenate(small_parts, axis=0)
    extra = jnp.stack([part[:, qkv_width:] for part in small_parts])
    group_lengths = lax.dynamic_slice(
        extra, (0, lane * d_rows, 3), (members, lengths.shape[1], 1)
    ).reshape(members, -1).astype(jnp.int32)
    extra = [lax.dynamic_index_in_dim(extra, me ^ slot, 0, keepdims=False) for slot in range(members)]
    extra = jnp.concatenate(extra, axis=0).astype(f32).T
    attn_scale = extra[0:1]
    mlp_scale = extra[1:2]
    latent_scale = extra[2].reshape(devices, d_rows)[:, : query_gain.shape[0]].reshape(1, -1)

    token_rows = tokens.astype(f32)
    attn_out, attn_normed, attn_factor = normalize(token_rows, attn_scale)
    attn_in = attn_out.astype(bf16)
    low = dot(by_member(attn_in, members), qkv_parts)
    latent = low[:, :latent_width]
    latent_out, latent_normed, latent_factor = normalize(latent, latent_scale)
    latent_in = latent_out.astype(bf16)
    key_own = rotate(low[:, latent_width : latent_width + HD], own_cos, own_sin)
    value_own = low[:, latent_width + HD : qkv_width]
    packed = jnp.concatenate([latent_in, key_own.astype(bf16), value_own.astype(bf16)], axis=1)
    packed = jnp.concatenate(gather_quad(packed, *GROUP), axis=0)
    query_rot, mixture = attend(group_lengths, packed, query_full, rows, heads)
    ffn_grad_found = fetch_first(after(ffn_grad_own, packed), *GROUP)
    ffn_grad = fetch_last(ffn_grad_own, after(ffn_grad_found, mixture), *GROUP)
    mixture = after(mixture, ffn_grad_found)
    attn_sum = scatter_rows(
        dot(mixture[:rows], out_full), dot(mixture[rows:], out_full).astype(bf16), *GROUP
    )
    residual = token_rows + living * attn_sum

    ffn_out, ffn_normed, ffn_factor = normalize(residual, mlp_scale)
    ffn_in = jnp.concatenate(gather_quad(ffn_out.astype(bf16), *GROUP), axis=0)
    gate_up_act = dot(ffn_in, gate_up)
    ffn_grad = jnp.concatenate(after(ffn_grad, gate_up_act), axis=0)
    gate_act, up_act = gate_up_act[:, :cut], gate_up_act[:, cut:]
    sigmoid_gate = jax.nn.sigmoid(gate_act)
    silu_gate = gate_act * sigmoid_gate
    hidden = (silu_gate * up_act).astype(bf16)

    down_wgrad = dot_tn(hidden, ffn_grad).astype(bf16)
    down_share = lax.psum_scatter(down_wgrad, RING, scatter_dimension=0, tiled=True)

    hidden_grad = dot_nt(after(ffn_grad, down_wgrad), down_full)
    gate_grad = (
        hidden_grad * up_act * sigmoid_gate * (1.0 + gate_act * (1.0 - sigmoid_gate))
    ).astype(bf16)
    up_grad = (hidden_grad * silu_gate).astype(bf16)
    gate_up_grad = jnp.concatenate([gate_grad, up_grad], axis=1)
    back = dot_nt(gate_up_grad[rows:], gate_up).astype(bf16)
    slots = [None] + [back[i * rows : (i + 1) * rows] for i in range(members - 1)]
    loads = first_loads(slots)
    back_sent = send_loads(loads, *GROUP)
    back_own = dot_nt(after(gate_up_grad[:rows], loads), gate_up)
    loads = last_loads(slots, after(back_sent, back_own))
    ffn_in_grad = sum_up(back_own, back_sent, send_loads(loads, *GROUP[::-1]))
    gate_up_wgrad = dot_tn(ffn_in, after(gate_up_grad, loads)).astype(bf16)
    residual_back, mlp_scale_grad = normalize_back(ffn_in_grad, ffn_normed, ffn_factor, mlp_scale)
    residual_grad = grad_rows + residual_back
    attn_grad = (living * residual_grad).astype(bf16)
    attn_grad = after(attn_grad, down_share, gate_up_wgrad)
    gate_up_share = lax.psum_scatter(
        gate_up_wgrad.reshape(members, width // members, -1), RING, scatter_dimension=1, tiled=True
    )
    attn_found = fetch_first(attn_grad, *GROUP)
    attn_grad = jnp.concatenate(fetch_last(attn_grad, attn_found, *GROUP), axis=0)
    ffn_back = dot(after(hidden, attn_found), down_full).astype(bf16)
    ffn_slots = after(ffn_back, attn_grad)
    ffn_slots = [ffn_slots[i * rows : (i + 1) * rows] for i in range(members)]
    ffn_sent = send_first(ffn_slots, *GROUP)
    packed_grad, out_wgrad, query_wgrad = attend_back(
        group_lengths,
        after(attn_grad, ffn_back),
        out_full,
        query_full,
        query_rot,
        mixture,
        packed,
        rows,
        heads,
    )
    packed_grad = after(packed_grad, ffn_sent)
    slots = [packed_grad[i * rows : (i + 1) * rows] for i in range(members)]
    loads = first_loads(slots)
    packed_sent = send_loads(loads, *GROUP)
    out_share = lax.psum_scatter(out_wgrad, RING, scatter_dimension=0, tiled=True)
    loads = last_loads(slots, packed_sent)
    packed_grad = sum_up(slots[0], packed_sent, send_loads(loads, *GROUP[::-1]))
    packed_grad = after(packed_grad, gate_up_share)
    ffn_sum = send_last(ffn_slots, after(ffn_sent, packed_grad), *GROUP)
    gate_up_found = swap_blocks(
        lambda k: lax.dynamic_index_in_dim(
            after(gate_up_share, packed_grad).reshape(members, d_rows, -1), k, 0, keepdims=False
        )
    )
    query_wgrad = query_wgrad.reshape(members, latent_width // members, heads * HD)
    query_share = lax.psum_scatter(query_wgrad, RING, scatter_dimension=1, tiled=True)
    latent_in_grad = packed_grad[:, :latent_width]
    key_grad = rotate(
        packed_grad[:, latent_width : latent_width + HD], own_cos, -own_sin
    ).astype(bf16)
    value_grad = packed_grad[:, latent_width + HD :].astype(bf16)
    latent_back, latent_scale_grad = normalize_back(
        latent_in_grad, latent_normed, latent_factor, latent_scale
    )
    spare = jnp.zeros((rows, qkv_parts.shape[1] - qkv_width), bf16)
    qkv_grad = jnp.concatenate([latent_back.astype(bf16), key_grad, value_grad, spare], axis=1)
    attn_in_grad = by_member(dot_nt(qkv_grad, qkv_parts), members)
    token_back, attn_scale_grad = normalize_back(attn_in_grad, attn_normed, attn_factor, attn_scale)

    small_grad = dot_tn(attn_in, qkv_grad[:, :qkv_width])
    latent_column = jnp.pad(
        latent_scale_grad.reshape(devices, -1), ((0, 0), (0, d_rows - query_gain.shape[0]))
    ).reshape(-1)
    columns = jnp.stack([attn_scale_grad, mlp_scale_grad, latent_column])
    columns = jnp.pad(columns, ((0, 128 - 3), (0, 0))).T
    small_grad = jnp.concatenate([small_grad, columns], axis=1).astype(bf16)
    small_slots = small_first(small_grad.reshape(2, 2, 2, 2, cores, d_rows, -1), cores)
    small_pairs = small_middle(small_slots)
    small_share = scatter_quad(small_pairs, "zl", "zh")
    out_share, down_share, query_share = after((out_share, down_share, query_share), small_pairs)

    layer_out = (residual + living * after(ffn_sum, small_slots)).astype(bf16)
    tokens_grad = after(residual_grad, small_slots) + token_back
    found = in_order(after(gate_up_found, small_slots))
    gate_share = jnp.concatenate([part[:, :cut] for part in found], axis=1).astype(f32)
    up_share = jnp.concatenate([part[:, cut:] for part in found], axis=1).astype(f32)
    found = in_order(swap_blocks(lambda k: lax.dynamic_index_in_dim(query_share, k, 0, keepdims=False)))
    query_share = jnp.concatenate(found, axis=1).astype(f32)
    return (
        layer_out,
        tokens_grad,
        small_share[:, latent_width + 2 * HD],
        small_share[:, :latent_width],
        small_share[: query_gain.shape[0], latent_width + 2 * HD + 2],
        query_share,
        small_share[:, latent_width : latent_width + HD],
        small_share[:, latent_width + HD : latent_width + 2 * HD],
        out_share.astype(f32),
        small_share[:, latent_width + 2 * HD + 1],
        gate_share,
        up_share,
        down_share.astype(f32),
    )


def solution(mesh):
    members, ring = mesh.shape["dp"], mesh.shape["fsdp"]
    cores = mesh.devices.size // 16
    fine = jax.sharding.Mesh(mesh.devices.reshape(2, 2, 2, 2, cores), ALL)
    matrix, vector = P(ALL, None), P(ALL)
    in_specs = (
        matrix,
        matrix,
        vector,
        matrix,
        vector,
        matrix,
        matrix,
        matrix,
        matrix,
        vector,
        matrix,
        matrix,
        matrix,
        matrix,
    )
    out_specs = (
        matrix,
        matrix,
        vector,
        matrix,
        vector,
        matrix,
        matrix,
        matrix,
        matrix,
        vector,
        matrix,
        matrix,
        matrix,
    )

    def body(*args):
        return shards(members, ring, cores, *args)

    return jax.shard_map(body, mesh=fine, in_specs=in_specs, out_specs=out_specs, check_vma=False)
```

```python
import functools
import math

import jax
import jax.numpy as jnp
from jax import lax
from jax.experimental import pallas as pl
from jax.experimental.pallas import tpu as pltpu
from jax.sharding import PartitionSpec as P

H = 16
HD = 256
PAD = 32

eps = 1e-06
rope_base = 10000.0
masked_score = -1e30
ALL = ("y", "x", "zh", "zl", "r")
DP = ("y", "x")
GROUP = ("x", "y")
RING = ("zh", "zl", "r")
f32 = jnp.float32
bf16 = jnp.bfloat16


def layout(lengths, row_total):
    padded = (lengths + PAD - 1) // PAD * PAD
    count = lengths.shape[0]
    ends = []
    for s in range(count):
        ends.append(padded[s] if s == 0 else ends[-1] + padded[s])
    row = lax.broadcasted_iota(jnp.int32, (row_total, 1), 0)
    segment = jnp.zeros_like(row)
    start = jnp.zeros_like(row)
    alive = jnp.zeros(row.shape, jnp.bool_)
    for s in range(count):
        first = ends[s] - padded[s]
        member = (row >= first) & (row < ends[s])
        segment = jnp.where(member, s + 1, segment)
        start = jnp.where(member, first, start)
        alive = alive | (member & (row - first < lengths[s]))
    return row - start, alive, segment


def angles(offset, head_size):
    half_width = head_size // 2
    frequency = jnp.exp(
        jnp.arange(half_width, dtype=f32) * (-2.0 * math.log(rope_base) / head_size)
    )
    phase = offset.astype(f32) * frequency[None, :]
    return (jnp.cos(phase), jnp.sin(phase))


def rotate(values, cos_part, sin_part):
    half_width = values.shape[-1] // 2
    first_half = values[..., :half_width]
    second_half = values[..., half_width:]
    return jnp.concatenate(
        [
            first_half * cos_part - second_half * sin_part,
            second_half * cos_part + first_half * sin_part,
        ],
        axis=-1,
    )


def normalize(values, scale_gain):
    factor = lax.rsqrt(jnp.mean(values * values, axis=-1, keepdims=True) + eps)
    normed = values * factor
    return (normed * scale_gain, normed, factor)


def normalize_back(upstream, normed, factor, scale_gain):
    scaled = upstream * scale_gain
    gain_grad = jnp.sum(upstream * normed, axis=0)
    inner_mean = jnp.mean(scaled * normed, axis=-1, keepdims=True)
    return (factor * (scaled - normed * inner_mean), gain_grad)


def dot(a, b):
    return jnp.dot(a, b, preferred_element_type=f32)


def dot_nt(a, b):
    return lax.dot_general(a, b, (((1,), (1,)), ((), ())), preferred_element_type=f32)


def dot_tn(a, b):
    return lax.dot_general(a, b, (((0,), (0,)), ((), ())), preferred_element_type=f32)


def after(values, *others):
    return lax.optimization_barrier((values, others))[0]


def trade(values, axis):
    return lax.ppermute(values, axis, [(0, 1), (1, 0)])


def gather_quad(values, first, second):
    half = values.shape[0] // 2
    one = trade(values, first)
    two = trade(values, second)
    three = jnp.concatenate([trade(two[:half], first), trade(one[half:], second)], axis=0)
    return [values, one, two, three]


def fetch_first(values, first, second):
    return trade(values, first), trade(values, second)


def fetch_last(values, found, first, second):
    one, two = found
    half = values.shape[0] // 2
    return [values, one, two, trade(two[:half], first), trade(one[half:], second)]


def first_loads(slots):
    half = slots[1].shape[0] // 2
    return (
        jnp.concatenate([slots[1][:half], slots[3][:half]], axis=0),
        jnp.concatenate([slots[2][half:], slots[3][half:]], axis=0),
    )


def send_loads(loads, first, second):
    return trade(loads[0], first), trade(loads[1], second)


def last_loads(slots, sent):
    half, (ra, rb) = slots[1].shape[0] // 2, sent
    return (
        (slots[2][:half].astype(f32) + ra[half:].astype(f32)).astype(bf16),
        (slots[1][half:].astype(f32) + rb[half:].astype(f32)).astype(bf16),
    )


def sum_up(own, sent, last):
    half, own = own.shape[0] // 2, own.astype(f32)
    return jnp.concatenate(
        [
            own[:half] + sent[0][:half].astype(f32) + last[0].astype(f32),
            own[half:] + sent[1][:half].astype(f32) + last[1].astype(f32),
        ],
        axis=0,
    )


def send_first(slots, first, second):
    return send_loads(first_loads(slots), first, second)


def send_last(slots, sent, first, second):
    return sum_up(slots[0], sent, send_loads(last_loads(slots, sent), second, first))


def scatter_quad(slots, first, second):
    return send_last(slots, send_first(slots, first, second), first, second)


def scatter_rows(own, others, first, second):
    rows = own.shape[0]
    slots = [own] + [others[i * rows : (i + 1) * rows] for i in range(3)]
    return scatter_quad(slots, first, second)


def split_cores(values, cores):
    if cores != 2:
        return lax.psum_scatter(values, "r", scatter_dimension=4, tiled=False), None
    core = lax.axis_index("r")
    mine = lax.dynamic_index_in_dim(values, core, 4, keepdims=False)
    theirs = lax.dynamic_index_in_dim(values, 1 - core, 4, keepdims=False)
    return mine, trade(theirs.reshape(-1, values.shape[-1]), "r").reshape(mine.shape)


def join_cores(mine, theirs):
    if theirs is None:
        return mine
    return (mine.astype(f32) + theirs.astype(f32)).astype(bf16)


def small_first(values, cores):
    n, c = values.shape[5:]
    total = join_cores(*split_cores(values, cores)).reshape(4, 4 * n, c)
    me = lax.axis_index(DP)
    return [lax.dynamic_index_in_dim(total, me ^ code, 0, keepdims=False) for code in range(4)]


def pairs_along_z(total):
    total = total.reshape(4, -1, total.shape[1])
    me = lax.axis_index("zh") * 2 + lax.axis_index("zl")
    return [lax.dynamic_index_in_dim(total, me ^ code, 0, keepdims=False) for code in range(4)]


def add_up(parts):
    total = parts[0].astype(f32)
    for part in parts[1:]:
        total = total + part.astype(f32)
    return total


def along_z(values, code):
    return lax.ppermute(values, ("zh", "zl"), [(i, i ^ code) for i in range(4)])


def share_small(values, cores):
    n, c = values.shape
    if cores != 2:
        whole = lax.all_gather(values, RING, axis=0, tiled=True)
        return jnp.concatenate(gather_quad(whole, *GROUP), axis=0), whole
    core, place = lax.axis_index("r"), lax.axis_index("zh") * 2 + lax.axis_index("zl")
    line = jnp.stack([values] + [along_z(values, code) for code in (1, 2, 3)])
    line = [lax.dynamic_index_in_dim(line, place ^ k, 0, keepdims=False) for k in range(4)]
    line = jnp.concatenate(line, axis=0)
    total = jnp.zeros((4, 4, 2, n, c), values.dtype)
    for slot, part in enumerate(gather_quad(line, *GROUP)):
        for where, piece in ((core, part), (1 - core, trade(part, "r"))):
            total = lax.dynamic_update_slice(total, piece.reshape(1, 4, 1, n, c), (slot, 0, where, 0, 0))
    return total.reshape(32 * n, c), line


def swap_blocks(block):
    me = lax.axis_index(DP)
    found = [block(me)]
    for code in (1, 2, 3):
        found.append(lax.ppermute(block(me ^ code), DP, [(i, i ^ code) for i in range(4)]))
    return found


def in_order(found):
    me, found = lax.axis_index(DP), jnp.stack(found)
    return [lax.dynamic_index_in_dim(found, me ^ k, 0, keepdims=False) for k in range(4)]


def take_columns(weight, k, members):
    step = weight.shape[1] // members
    return lax.dynamic_slice_in_dim(weight, k * step, step, 1)


def turn(values, cos_part, sin_part):
    half = values.shape[-1] // 2
    one, two = values[:, :half], values[:, half:]
    return jnp.concatenate([one * cos_part - two * sin_part, two * cos_part + one * sin_part], axis=-1)


def spans(lengths_ref, member):
    first, found = 0, []
    for s in range(lengths_ref.shape[1]):
        length = lengths_ref[member, s]
        end = first + (length + PAD - 1) // PAD * PAD
        found.append((first, end, first + length))
        first = end
    return found


def fill_angles(lengths_ref, cos_ref, sin_ref):
    rows, half = cos_ref.shape
    row = lax.broadcasted_iota(jnp.int32, (rows, half), 0)
    position = row
    for first, end, _ in spans(lengths_ref, pl.program_id(0)):
        position = jnp.where((row >= first) & (row < end), row - first, position)
    step = lax.broadcasted_iota(jnp.int32, (rows, half), 1).astype(f32)
    phase = position.astype(f32) * jnp.exp(step * (-math.log(rope_base) / half))
    cos_ref[...] = jnp.cos(phase)
    sin_ref[...] = jnp.sin(phase)


def probabilities(query_rot, key_rot, lengths_ref):
    rows = query_rot.shape[0]
    scores = dot_nt(query_rot, key_rot) * (1.0 / math.sqrt(HD))
    i = lax.broadcasted_iota(jnp.int32, (rows, rows), 0)
    j = lax.broadcasted_iota(jnp.int32, (rows, rows), 1)
    allowed = i == j
    for first, end, live in spans(lengths_ref, pl.program_id(0)):
        allowed = allowed | ((i >= first) & (i < end) & (j >= first) & (j < live) & (j <= i))
    scores = jnp.where(allowed, scores, masked_score)
    expo = jnp.exp(scores - jnp.max(scores, axis=-1, keepdims=True))
    return expo / jnp.sum(expo, axis=-1, keepdims=True)


def query_block(weight_ref, member, heads):
    ring, rows, width = weight_ref.shape
    high, low = divmod(member, 2)
    part = weight_ref[:, low * rows // 2 : (low + 1) * rows // 2, high * width // 2 : (high + 1) * width // 2]
    return part.reshape(ring * rows // 2, width // 2)


def attend_kernel(
    members,
    heads,
    lengths_ref,
    latent_ref,
    weight_ref,
    out_ref,
    key_ref,
    value_ref,
    query_ref,
    mix_ref,
    back_ref,
    cos_ref,
    sin_ref,
):
    fill_angles(lengths_ref, cos_ref, sin_ref)
    step = latent_ref.shape[1] // members
    queries = dot(latent_ref[:, :step], query_block(weight_ref, 0, heads))
    for k in range(1, members):
        queries += dot(latent_ref[:, k * step : (k + 1) * step], query_block(weight_ref, k, heads))
    for head in range(heads):
        columns = slice(head * HD, (head + 1) * HD)
        query_rot = turn(queries[:, columns], cos_ref[...], sin_ref[...]).astype(bf16)
        query_ref[:, columns] = query_rot
        probs = probabilities(query_rot, key_ref[...], lengths_ref)
        mix_ref[:, columns] = dot(probs.astype(bf16), value_ref[...]).astype(bf16)
    out_full = out_ref[...].reshape(heads * HD, -1)
    back_ref[...] = dot(mix_ref[...], out_full).astype(bf16)


def packed_specs(gathered):
    ring, rows, width = gathered.shape
    third = rows // 3
    return [
        pl.BlockSpec((ring, third, width), lambda m, s: (0, 2, 0), pipeline_mode=pl.Buffered(1)),
        pl.BlockSpec((ring, 2 * third, width), lambda m, s: (0, 0, 0), pipeline_mode=pl.Buffered(1)),
    ]


def attend(lengths, packed, gathered, rows, heads):
    total, width = packed.shape[0], gathered.shape[2]
    latent_width = packed.shape[1] - 2 * HD
    last, members = latent_width // HD, total // rows
    block = pl.BlockSpec((rows, heads * HD), lambda m, s: (m, 0))
    out = jax.ShapeDtypeStruct((total, heads * HD), bf16)
    return pl.pallas_call(
        functools.partial(attend_kernel, members, heads),
        grid_spec=pltpu.PrefetchScalarGridSpec(
            num_scalar_prefetch=1,
            grid=(members,),
            in_specs=[
                pl.BlockSpec((rows, latent_width), lambda m, s: (m, 0)),
                *packed_specs(gathered),
                pl.BlockSpec((rows, HD), lambda m, s: (m, last)),
                pl.BlockSpec((rows, HD), lambda m, s: (m, last + 1)),
            ],
            out_specs=[block, block, pl.BlockSpec((rows, width), lambda m, s: (m, 0))],
            scratch_shapes=[pltpu.VMEM((rows, HD // 2), f32), pltpu.VMEM((rows, HD // 2), f32)],
        ),
        out_shape=[out, out, jax.ShapeDtypeStruct((total, width), bf16)],
        compiler_params=pltpu.CompilerParams(vmem_limit_bytes=40 * 2**20),
        cost_estimate=pl.CostEstimate(
            flops=2 * total * heads * HD * (latent_width + 2 * rows + width),
            bytes_accessed=total * heads * HD * 4 + total * latent_width * 3 + 8 * 2**20,
            transcendentals=total * heads * rows,
        ),
    )(lengths, packed, gathered, gathered, packed, packed)


def attend_back_kernel(
    members,
    heads,
    lengths_ref,
    grad_ref,
    weight_ref,
    out_ref,
    query_ref,
    latent_ref,
    key_ref,
    value_ref,
    mix_ref,
    packed_ref,
    gathered_grad_ref,
    grads_ref,
    mixes_ref,
    latents_ref,
    query_grads_ref,
    cos_ref,
    sin_ref,
):
    member = pl.program_id(0)
    fill_angles(lengths_ref, cos_ref, sin_ref)
    latent_width = latent_ref.shape[1]
    step = latent_width // members
    out_full = out_ref[...].reshape(heads * HD, -1)
    scale = 1.0 / math.sqrt(HD)
    grads_ref[member] = grad_ref[...]
    mixes_ref[member] = mix_ref[...]
    latents_ref[member] = latent_ref[...]
    key_rot, value_low = key_ref[...], value_ref[...]
    mixture_grads = dot_nt(grad_ref[...], out_full).astype(bf16)
    key_grad = jnp.zeros(key_rot.shape, f32)
    value_grad = jnp.zeros(key_rot.shape, f32)
    for head in range(heads):
        columns = slice(head * HD, (head + 1) * HD)
        query_rot, mixture_grad = query_ref[:, columns], mixture_grads[:, columns]
        probs = probabilities(query_rot, key_rot, lengths_ref)
        probs_grad = dot_nt(mixture_grad, value_low)
        row_dot = jnp.sum(probs * probs_grad, axis=-1, keepdims=True)
        score_grad = (probs * (probs_grad - row_dot)).astype(bf16)
        query_rot_grad = dot(score_grad, key_rot) * scale
        query_grads_ref[member, :, columns] = turn(query_rot_grad, cos_ref[...], -sin_ref[...]).astype(bf16)
        key_grad += dot_tn(score_grad, query_rot)
        value_grad += dot_tn(probs.astype(bf16), mixture_grad)
    for k in range(members):
        latent_part = dot_nt(query_grads_ref[member], query_block(weight_ref, k, heads))
        packed_ref[:, k * step : (k + 1) * step] = latent_part.astype(bf16)
    packed_ref[:, latent_width : latent_width + HD] = (key_grad * scale).astype(bf16)
    packed_ref[:, latent_width + HD :] = value_grad.astype(bf16)

    @pl.when(member == members - 1)
    def _():
        rows = members * grad_ref.shape[0]
        grads = grads_ref[...].reshape(rows, -1)
        mixes = mixes_ref[...].reshape(rows, -1)
        latents = latents_ref[...].reshape(rows, -1)
        query_grads = query_grads_ref[...].reshape(rows, -1)
        ring, held, width = gathered_grad_ref.shape
        held = held // 3
        count = HD // (2 * held)
        for head in range(heads):
            columns = slice(head * HD, (head + 1) * HD)
            part = dot_tn(mixes[:, columns], grads).astype(bf16)
            gathered_grad_ref[head * count : (head + 1) * count, : 2 * held] = part.reshape(count, 2 * held, width)
        for k in range(members):
            part = dot_tn(latents[:, k * step : (k + 1) * step], query_grads).astype(bf16)
            high, low = divmod(k, 2)
            place = slice(2 * held + low * held // 2, 2 * held + (low + 1) * held // 2)
            columns = slice(high * width // 2, (high + 1) * width // 2)
            gathered_grad_ref[:, place, columns] = part.reshape(ring, held // 2, width // 2)


def attend_back(lengths, attn_grad, gathered, query_rot, mixture, packed, rows, heads):
    total, width = attn_grad.shape
    latent_width = packed.shape[1] - 2 * HD
    last, members = latent_width // HD, total // rows
    block = pl.BlockSpec((rows, heads * HD), lambda m, s: (m, 0))

    def kept(columns):
        return pltpu.VMEM((members, rows, columns), bf16)

    return pl.pallas_call(
        functools.partial(attend_back_kernel, members, heads),
        grid_spec=pltpu.PrefetchScalarGridSpec(
            num_scalar_prefetch=1,
            grid=(members,),
            in_specs=[
                pl.BlockSpec((rows, width), lambda m, s: (m, 0)),
                *packed_specs(gathered),
                block,
                pl.BlockSpec((rows, latent_width), lambda m, s: (m, 0)),
                pl.BlockSpec((rows, HD), lambda m, s: (m, last)),
                pl.BlockSpec((rows, HD), lambda m, s: (m, last + 1)),
                block,
            ],
            out_specs=[
                pl.BlockSpec((rows, packed.shape[1]), lambda m, s: (m, 0)),
                pl.BlockSpec(gathered.shape, lambda m, s: (0, 0, 0)),
            ],
            scratch_shapes=[
                kept(width),
                kept(heads * HD),
                kept(latent_width),
                kept(heads * HD),
                pltpu.VMEM((rows, HD // 2), f32),
                pltpu.VMEM((rows, HD // 2), f32),
            ],
        ),
        out_shape=[
            jax.ShapeDtypeStruct(packed.shape, bf16),
            jax.ShapeDtypeStruct(gathered.shape, bf16),
        ],
        compiler_params=pltpu.CompilerParams(vmem_limit_bytes=56 * 2**20),
        cost_estimate=pl.CostEstimate(
            flops=2 * total * heads * HD * (2 * width + 2 * latent_width + 5 * rows),
            bytes_accessed=total * heads * HD * 8 + total * width * 4,
            transcendentals=total * heads * rows,
        ),
    )(lengths, attn_grad, gathered, gathered, query_rot, packed, packed, packed, mixture)


def by_block(values, code, count):
    step = values.shape[1] // count
    return jnp.concatenate(
        [lax.dynamic_slice_in_dim(values, (code ^ k) * step, step, 1) for k in range(count)], axis=1
    )


def shards(
    members,
    ring,
    cores,
    tokens,
    lengths,
    attn_gain,
    query_down,
    query_gain,
    query_up,
    key_weight,
    value_weight,
    out_weight,
    mlp_gain,
    gate_weight,
    up_weight,
    down_weight,
    cotangent,
):
    rows = tokens.shape[0]
    width = tokens.shape[1]
    latent_width = query_down.shape[1]
    heads = H // members
    devices = members * ring
    score_scale = 1.0 / math.sqrt(HD)
    d_rows = query_down.shape[0]

    def column(v):
        v = v.astype(bf16).reshape(-1, 1)
        return jnp.pad(v, ((0, d_rows - v.shape[0]), (0, 0)))

    own_offset, own_alive, _ = layout(lengths[0], rows)
    living = own_alive.astype(f32)
    own_cos, own_sin = angles(own_offset, HD)
    grad_rows = cotangent.astype(f32)
    ffn_grad_own = (living * grad_rows).astype(bf16)

    extra = jnp.concatenate(
        [column(attn_gain), column(mlp_gain), column(query_gain), column(lengths[0])], axis=1
    )
    extra = jnp.pad(extra, ((0, 0), (0, 128 - extra.shape[1])))
    small = jnp.concatenate([query_down, key_weight, value_weight, extra], axis=1)
    query_own = in_order(swap_blocks(lambda k: take_columns(query_up, k, members)))
    query_own = jnp.concatenate(
        [jnp.concatenate(query_own[:2], axis=0), jnp.concatenate(query_own[2:], axis=0)], axis=1
    )
    gathered = jnp.concatenate([out_weight, query_own], axis=0)
    gathered = lax.all_gather(gathered, RING, axis=0, tiled=False)
    qkv_parts, line = share_small(small, cores)
    gate_up_own = swap_blocks(
        lambda k: jnp.concatenate(
            [take_columns(gate_weight, k, members), take_columns(up_weight, k, members)], axis=1
        )
    )
    gate_up_own, down_own = after((jnp.stack(in_order(gate_up_own)), down_weight), qkv_parts)
    down_full = lax.all_gather(down_own, RING, axis=0, tiled=True)

    me, lane = lax.axis_index(DP), lax.axis_index(RING)
    qkv_width = latent_width + 2 * HD
    extra = qkv_parts[:, qkv_width:].reshape(members, ring * d_rows, -1)
    group_lengths = lax.dynamic_slice(
        extra, (0, lane * d_rows, 3), (members, lengths.shape[1], 1)
    ).reshape(members, -1).astype(jnp.int32)
    extra = [lax.dynamic_index_in_dim(extra, me ^ k, 0, keepdims=False) for k in range(members)]
    extra = jnp.concatenate(extra, axis=0).astype(f32).T
    attn_scale = extra[0:1]
    mlp_scale = extra[1:2]
    latent_scale = extra[2].reshape(devices, d_rows)[:, : query_gain.shape[0]].reshape(1, -1)

    token_rows = tokens.astype(f32)
    attn_out, attn_normed, attn_factor = normalize(token_rows, attn_scale)
    attn_in = attn_out.astype(bf16)
    low = dot(by_block(attn_in, me, members), qkv_parts)
    latent = low[:, :latent_width]
    latent_out, latent_normed, latent_factor = normalize(latent, latent_scale)
    latent_in = latent_out.astype(bf16)
    key_own = rotate(low[:, latent_width : latent_width + HD], own_cos, own_sin)
    value_own = low[:, latent_width + HD : qkv_width]
    packed = jnp.concatenate([latent_in, key_own.astype(bf16), value_own.astype(bf16)], axis=1)
    packed_found = fetch_first(packed, *GROUP)
    gate_up = lax.all_gather(gate_up_own, RING, axis=1, tiled=True).reshape(width, -1)
    cut = gate_up.shape[1] // 2
    packed = jnp.concatenate(fetch_last(packed, packed_found, *GROUP), axis=0)
    query_rot, mixture, attn_back = attend(group_lengths, packed, gathered, rows, heads)
    ffn_grad_found = fetch_first(after(ffn_grad_own, packed), *GROUP)
    attn_back = after(attn_back, ffn_grad_found)
    attn_slots = [attn_back[i * rows : (i + 1) * rows] for i in range(members)]
    attn_sent = send_first(attn_slots, *GROUP)
    one, two = ffn_grad_found
    ffn_grad = jnp.concatenate([ffn_grad_own, one, two, two], axis=0)
    ffn_grad_rest = (two[: rows // 2], one[rows // 2 :])
    attn_sum = send_last(attn_slots, after(attn_sent, ffn_grad, ffn_grad_rest), *GROUP)
    residual = token_rows + living * attn_sum

    ffn_out, ffn_normed, ffn_factor = normalize(residual, mlp_scale)
    ffn_in = jnp.concatenate(gather_quad(ffn_out.astype(bf16), *GROUP), axis=0)
    gate_up_act = dot(ffn_in, gate_up)
    ffn_grad_rest = after(ffn_grad_rest, ffn_in)
    ffn_grad_rest = after((trade(ffn_grad_rest[0], "x"), trade(ffn_grad_rest[1], "y")), gate_up_act)
    ffn_grad = lax.dynamic_update_slice(ffn_grad, ffn_grad_rest[0], (3 * rows, 0))
    ffn_grad = lax.dynamic_update_slice(ffn_grad, ffn_grad_rest[1], (3 * rows + rows // 2, 0))
    gate_act, up_act = gate_up_act[:, :cut], gate_up_act[:, cut:]
    sigmoid_gate = jax.nn.sigmoid(gate_act)
    silu_gate = gate_act * sigmoid_gate
    hidden = (silu_gate * up_act).astype(bf16)

    down_wgrad = dot_tn(hidden, ffn_grad).astype(bf16)
    down_share = lax.psum_scatter(down_wgrad, RING, scatter_dimension=0, tiled=True)

    hidden_grad = dot_nt(after(ffn_grad, down_wgrad), down_full)
    gate_grad = (
        hidden_grad * up_act * sigmoid_gate * (1.0 + gate_act * (1.0 - sigmoid_gate))
    ).astype(bf16)
    up_grad = (hidden_grad * silu_gate).astype(bf16)
    gate_up_grad = jnp.concatenate([gate_grad, up_grad], axis=1)
    back = dot_nt(gate_up_grad, gate_up).astype(bf16)
    slots = [back[i * rows : (i + 1) * rows] for i in range(members)]
    loads = first_loads(slots)
    back_sent = send_loads(loads, *GROUP)
    ffn_back = dot(after(hidden, loads), down_full).astype(bf16)
    back_sent = after(back_sent, ffn_back)
    ffn_slots = [ffn_back[i * rows : (i + 1) * rows] for i in range(members)]
    gate_up_wgrad = dot_tn(ffn_in, after(gate_up_grad, back_sent)).astype(bf16)
    ffn_in_grad = send_last(slots, after(back_sent, gate_up_wgrad), *GROUP)
    residual_back, mlp_scale_grad = normalize_back(ffn_in_grad, ffn_normed, ffn_factor, mlp_scale)
    residual_grad = grad_rows + residual_back
    attn_grad = (living * residual_grad).astype(bf16)
    attn_grad = after(attn_grad, down_share, gate_up_wgrad)
    gate_up_share = lax.psum_scatter(
        gate_up_wgrad.reshape(members, width // members, -1), RING, scatter_dimension=1, tiled=True
    )
    attn_found = fetch_first(attn_grad, *GROUP)
    attn_grad = jnp.concatenate(fetch_last(attn_grad, attn_found, *GROUP), axis=0)
    ffn_sent = send_loads(after(first_loads(ffn_slots), attn_grad), *GROUP)
    packed_grad, gathered_grad = attend_back(
        group_lengths,
        attn_grad,
        gathered,
        query_rot,
        mixture,
        packed,
        rows,
        heads,
    )
    packed_grad = after(packed_grad, ffn_sent)
    slots = [packed_grad[i * rows : (i + 1) * rows] for i in range(members)]
    loads = first_loads(slots)
    packed_sent = send_loads(loads, *GROUP)
    gathered_share = lax.psum_scatter(gathered_grad, RING, scatter_dimension=0, tiled=False)
    loads = last_loads(slots, packed_sent)
    packed_grad = sum_up(slots[0], packed_sent, send_loads(loads, *GROUP[::-1]))
    latent_in_grad = packed_grad[:, :latent_width]
    key_grad = rotate(
        packed_grad[:, latent_width : latent_width + HD], own_cos, -own_sin
    ).astype(bf16)
    value_grad = packed_grad[:, latent_width + HD :].astype(bf16)
    latent_back, latent_scale_grad = normalize_back(
        latent_in_grad, latent_normed, latent_factor, latent_scale
    )
    spare = jnp.zeros((rows, qkv_parts.shape[1] - qkv_width), bf16)
    qkv_grad = jnp.concatenate([latent_back.astype(bf16), key_grad, value_grad, spare], axis=1)
    attn_in_grad = by_block(dot_nt(qkv_grad, qkv_parts), me, members)
    token_back, attn_scale_grad = normalize_back(attn_in_grad, attn_normed, attn_factor, attn_scale)

    small_grad = dot_tn(attn_in, qkv_grad[:, :qkv_width])
    latent_column = jnp.pad(
        latent_scale_grad.reshape(devices, -1), ((0, 0), (0, d_rows - query_gain.shape[0]))
    ).reshape(-1)
    columns = jnp.stack([attn_scale_grad, mlp_scale_grad, latent_column])
    columns = jnp.pad(columns, ((0, 128 - 3), (0, 0))).T
    small_grad = jnp.concatenate([small_grad, columns], axis=1).astype(bf16)
    small_slots = small_first(small_grad.reshape(2, 2, 2, 2, cores, d_rows, -1), cores)
    ffn_last = send_loads(last_loads(ffn_slots, ffn_sent), *GROUP[::-1])
    small_slots = after(small_slots, gate_up_share, ffn_last)
    small_sent = send_first(small_slots, *GROUP)
    loads = last_loads(small_slots, small_sent)
    small_last = send_loads(loads, *GROUP[::-1])
    small_pairs = pairs_along_z(sum_up(small_slots[0], small_sent, small_last).astype(bf16))
    small_share = add_up([small_pairs[0]] + [along_z(small_pairs[code], code) for code in (1, 2, 3)])
    gate_up_share = after(gate_up_share, small_last).reshape(members, d_rows, -1)
    gate_up_found = swap_blocks(lambda k: lax.dynamic_index_in_dim(gate_up_share, k, 0, keepdims=False))
    gathered_share, down_share = after((gathered_share, down_share), small_last)
    held = out_weight.shape[0]
    out_share = gathered_share[:held]

    def query_part(k):
        low = lax.dynamic_slice_in_dim(gathered_share, held + (k % 2) * (held // 4), held // 4, 0)
        return lax.dynamic_slice_in_dim(low, (k // 2) * (width // 2), width // 2, 1)

    query_found = swap_blocks(query_part)
    ffn_sum = sum_up(ffn_slots[0], ffn_sent, after(ffn_last, small_slots))
    layer_out = (residual + living * ffn_sum).astype(bf16)
    tokens_grad = after(residual_grad, small_slots) + token_back
    found = in_order(gate_up_found)
    gate_share = jnp.concatenate([part[:, :cut] for part in found], axis=1).astype(f32)
    up_share = jnp.concatenate([part[:, cut:] for part in found], axis=1).astype(f32)
    found = in_order(query_found)
    query_share = jnp.concatenate(found, axis=1).astype(f32)
    return (
        layer_out,
        tokens_grad,
        small_share[:, latent_width + 2 * HD],
        small_share[:, :latent_width],
        small_share[: query_gain.shape[0], latent_width + 2 * HD + 2],
        query_share,
        small_share[:, latent_width : latent_width + HD],
        small_share[:, latent_width + HD : latent_width + 2 * HD],
        out_share.astype(f32),
        small_share[:, latent_width + 2 * HD + 1],
        gate_share,
        up_share,
        down_share.astype(f32),
    )


def solution(mesh):
    members, ring = mesh.shape["dp"], mesh.shape["fsdp"]
    cores = mesh.devices.size // 16
    fine = jax.sharding.Mesh(mesh.devices.reshape(2, 2, 2, 2, cores), ALL)
    matrix, vector = P(ALL, None), P(ALL)
    in_specs = (
        matrix,
        matrix,
        vector,
        matrix,
        vector,
        matrix,
        matrix,
        matrix,
        matrix,
        vector,
        matrix,
        matrix,
        matrix,
        matrix,
    )
    out_specs = (
        matrix,
        matrix,
        vector,
        matrix,
        vector,
        matrix,
        matrix,
        matrix,
        matrix,
        vector,
        matrix,
        matrix,
        matrix,
    )

    def body(*args):
        return shards(members, ring, cores, *args)

    return jax.shard_map(body, mesh=fine, in_specs=in_specs, out_specs=out_specs, check_vma=False)
```

```python
import functools
import math

import jax
import jax.numpy as jnp
from jax import lax
from jax.experimental import pallas as pl
from jax.experimental.pallas import tpu as pltpu
from jax.sharding import PartitionSpec as P

H = 16
HD = 256
PAD = 32

eps = 1e-06
rope_base = 10000.0
masked_score = -1e30
ALL = ("y", "x", "zh", "zl", "r")
DP = ("y", "x")
GROUP = ("x", "y")
RING = ("zh", "zl", "r")
f32 = jnp.float32
bf16 = jnp.bfloat16


def layout(lengths, row_total):
    padded = (lengths + PAD - 1) // PAD * PAD
    count = lengths.shape[0]
    ends = []
    for s in range(count):
        ends.append(padded[s] if s == 0 else ends[-1] + padded[s])
    row = lax.broadcasted_iota(jnp.int32, (row_total, 1), 0)
    segment = jnp.zeros_like(row)
    start = jnp.zeros_like(row)
    alive = jnp.zeros(row.shape, jnp.bool_)
    for s in range(count):
        first = ends[s] - padded[s]
        member = (row >= first) & (row < ends[s])
        segment = jnp.where(member, s + 1, segment)
        start = jnp.where(member, first, start)
        alive = alive | (member & (row - first < lengths[s]))
    return row - start, alive, segment


def angles(offset, head_size):
    half_width = head_size // 2
    frequency = jnp.exp(
        jnp.arange(half_width, dtype=f32) * (-2.0 * math.log(rope_base) / head_size)
    )
    phase = offset.astype(f32) * frequency[None, :]
    return (jnp.cos(phase), jnp.sin(phase))


def rotate(values, cos_part, sin_part):
    half_width = values.shape[-1] // 2
    first_half = values[..., :half_width]
    second_half = values[..., half_width:]
    return jnp.concatenate(
        [
            first_half * cos_part - second_half * sin_part,
            second_half * cos_part + first_half * sin_part,
        ],
        axis=-1,
    )


def normalize(values, scale_gain):
    factor = lax.rsqrt(jnp.mean(values * values, axis=-1, keepdims=True) + eps)
    normed = values * factor
    return (normed * scale_gain, normed, factor)


def normalize_back(upstream, normed, factor, scale_gain):
    scaled = upstream * scale_gain
    gain_grad = jnp.sum(upstream * normed, axis=0)
    inner_mean = jnp.mean(scaled * normed, axis=-1, keepdims=True)
    return (factor * (scaled - normed * inner_mean), gain_grad)


def dot(a, b):
    return jnp.dot(a, b, preferred_element_type=f32)


def dot_nt(a, b):
    return lax.dot_general(a, b, (((1,), (1,)), ((), ())), preferred_element_type=f32)


def dot_tn(a, b):
    return lax.dot_general(a, b, (((0,), (0,)), ((), ())), preferred_element_type=f32)


def after(values, *others):
    return lax.optimization_barrier((values, others))[0]


def trade(values, axis):
    return lax.ppermute(values, axis, [(0, 1), (1, 0)])


def gather_quad(values, first, second):
    half = values.shape[0] // 2
    one = trade(values, first)
    two = trade(values, second)
    three = jnp.concatenate([trade(two[:half], first), trade(one[half:], second)], axis=0)
    return [values, one, two, three]


def fetch_first(values, first, second):
    return trade(values, first), trade(values, second)


def fetch_last(values, found, first, second):
    one, two = found
    half = values.shape[0] // 2
    return [values, one, two, trade(two[:half], first), trade(one[half:], second)]


def first_loads(slots):
    half = slots[1].shape[0] // 2
    return (
        jnp.concatenate([slots[1][:half], slots[3][:half]], axis=0),
        jnp.concatenate([slots[2][half:], slots[3][half:]], axis=0),
    )


def send_loads(loads, first, second):
    return trade(loads[0], first), trade(loads[1], second)


def last_loads(slots, sent):
    half, (ra, rb) = slots[1].shape[0] // 2, sent
    return (
        (slots[2][:half].astype(f32) + ra[half:].astype(f32)).astype(bf16),
        (slots[1][half:].astype(f32) + rb[half:].astype(f32)).astype(bf16),
    )


def sum_up(own, sent, last):
    half, own = own.shape[0] // 2, own.astype(f32)
    return jnp.concatenate(
        [
            own[:half] + sent[0][:half].astype(f32) + last[0].astype(f32),
            own[half:] + sent[1][:half].astype(f32) + last[1].astype(f32),
        ],
        axis=0,
    )


def send_first(slots, first, second):
    return send_loads(first_loads(slots), first, second)


def send_last(slots, sent, first, second):
    return sum_up(slots[0], sent, send_loads(last_loads(slots, sent), second, first))


def scatter_quad(slots, first, second):
    return send_last(slots, send_first(slots, first, second), first, second)


def scatter_rows(own, others, first, second):
    rows = own.shape[0]
    slots = [own] + [others[i * rows : (i + 1) * rows] for i in range(3)]
    return scatter_quad(slots, first, second)


def join_cores(mine, theirs):
    if theirs is None:
        return mine
    return (mine.astype(f32) + theirs.astype(f32)).astype(bf16)


def small_first(values, cores, n):
    if cores == 2:
        total = join_cores(values[0], trade(values[1], "r"))
    else:
        total = values[0].reshape(16, cores, n, -1)
        total = lax.psum_scatter(total, "r", scatter_dimension=1, tiled=False)
    total = total.reshape(4, 4 * n, -1)
    me = lax.axis_index(DP)
    return [lax.dynamic_index_in_dim(total, me ^ code, 0, keepdims=False) for code in range(4)]


def pairs_along_z(total):
    total = total.reshape(4, -1, total.shape[1])
    me = lax.axis_index("zh") * 2 + lax.axis_index("zl")
    return [lax.dynamic_index_in_dim(total, me ^ code, 0, keepdims=False) for code in range(4)]


def add_up(parts):
    total = parts[0].astype(f32)
    for part in parts[1:]:
        total = total + part.astype(f32)
    return total


def along_z(values, code):
    return lax.ppermute(values, ("zh", "zl"), [(i, i ^ code) for i in range(4)])


def share_small(values, cores):
    n, c = values.shape
    if cores != 2:
        whole = lax.all_gather(values, RING, axis=0, tiled=True)
        return jnp.concatenate(gather_quad(whole, *GROUP), axis=0), whole
    core, place = lax.axis_index("r"), lax.axis_index("zh") * 2 + lax.axis_index("zl")
    line = jnp.stack([values] + [along_z(values, code) for code in (1, 2, 3)])
    line = [lax.dynamic_index_in_dim(line, place ^ k, 0, keepdims=False) for k in range(4)]
    line = jnp.concatenate(line, axis=0)
    total = jnp.zeros((4, 4, 2, n, c), values.dtype)
    for slot, part in enumerate(gather_quad(line, *GROUP)):
        for where, piece in ((core, part), (1 - core, trade(part, "r"))):
            total = lax.dynamic_update_slice(total, piece.reshape(1, 4, 1, n, c), (slot, 0, where, 0, 0))
    return total.reshape(32 * n, c), line


def swap_blocks(block):
    me = lax.axis_index(DP)
    found = [block(me)]
    for code in (1, 2, 3):
        found.append(lax.ppermute(block(me ^ code), DP, [(i, i ^ code) for i in range(4)]))
    return found


def in_order(found):
    me, found = lax.axis_index(DP), jnp.stack(found)
    return [lax.dynamic_index_in_dim(found, me ^ k, 0, keepdims=False) for k in range(4)]


def take_columns(weight, k, members):
    step = weight.shape[1] // members
    return lax.dynamic_slice_in_dim(weight, k * step, step, 1)


def turn(values, cos_part, sin_part):
    half = values.shape[-1] // 2
    one, two = values[:, :half], values[:, half:]
    return jnp.concatenate([one * cos_part - two * sin_part, two * cos_part + one * sin_part], axis=-1)


def spans(lengths_ref, member):
    first, found = 0, []
    for s in range(lengths_ref.shape[1]):
        length = lengths_ref[member, s]
        end = first + (length + PAD - 1) // PAD * PAD
        found.append((first, end, first + length))
        first = end
    return found


def fill_angles(lengths_ref, cos_ref, sin_ref):
    rows, half = cos_ref.shape
    row = lax.broadcasted_iota(jnp.int32, (rows, half), 0)
    position = row
    for first, end, _ in spans(lengths_ref, pl.program_id(0)):
        position = jnp.where((row >= first) & (row < end), row - first, position)
    step = lax.broadcasted_iota(jnp.int32, (rows, half), 1).astype(f32)
    phase = position.astype(f32) * jnp.exp(step * (-math.log(rope_base) / half))
    cos_ref[...] = jnp.cos(phase)
    sin_ref[...] = jnp.sin(phase)


def probabilities(query_rot, key_rot, lengths_ref):
    rows = query_rot.shape[0]
    scores = dot_nt(query_rot, key_rot) * (1.0 / math.sqrt(HD))
    i = lax.broadcasted_iota(jnp.int32, (rows, rows), 0)
    j = lax.broadcasted_iota(jnp.int32, (rows, rows), 1)
    allowed = i == j
    for first, end, live in spans(lengths_ref, pl.program_id(0)):
        allowed = allowed | ((i >= first) & (i < end) & (j >= first) & (j < live) & (j <= i))
    scores = jnp.where(allowed, scores, masked_score)
    expo = jnp.exp(scores - jnp.max(scores, axis=-1, keepdims=True))
    return expo / jnp.sum(expo, axis=-1, keepdims=True)


def query_block(weight_ref, member, heads):
    ring, rows, width = weight_ref.shape
    high, low = divmod(member, 2)
    part = weight_ref[:, low * rows // 2 : (low + 1) * rows // 2, high * width // 2 : (high + 1) * width // 2]
    return part.reshape(ring * rows // 2, width // 2)


def attend_kernel(
    members,
    heads,
    lengths_ref,
    latent_ref,
    weight_ref,
    out_ref,
    key_ref,
    value_ref,
    query_ref,
    mix_ref,
    back_ref,
    cos_ref,
    sin_ref,
):
    fill_angles(lengths_ref, cos_ref, sin_ref)
    step = latent_ref.shape[1] // members
    queries = dot(latent_ref[:, :step], query_block(weight_ref, 0, heads))
    for k in range(1, members):
        queries += dot(latent_ref[:, k * step : (k + 1) * step], query_block(weight_ref, k, heads))
    for head in range(heads):
        columns = slice(head * HD, (head + 1) * HD)
        query_rot = turn(queries[:, columns], cos_ref[...], sin_ref[...]).astype(bf16)
        query_ref[:, columns] = query_rot
        probs = probabilities(query_rot, key_ref[...], lengths_ref)
        mix_ref[:, columns] = dot(probs.astype(bf16), value_ref[...]).astype(bf16)
    out_full = out_ref[...].reshape(heads * HD, -1)
    back_ref[...] = dot(mix_ref[...], out_full).astype(bf16)


def packed_specs(gathered):
    ring, rows, width = gathered.shape
    third = rows // 3
    return [
        pl.BlockSpec((ring, third, width), lambda m, s: (0, 2, 0), pipeline_mode=pl.Buffered(1)),
        pl.BlockSpec((ring, 2 * third, width), lambda m, s: (0, 0, 0), pipeline_mode=pl.Buffered(1)),
    ]


def attend(lengths, packed, gathered, rows, heads):
    total, width = packed.shape[0], gathered.shape[2]
    latent_width = packed.shape[1] - 2 * HD
    last, members = latent_width // HD, total // rows
    block = pl.BlockSpec((rows, heads * HD), lambda m, s: (m, 0))
    out = jax.ShapeDtypeStruct((total, heads * HD), bf16)
    return pl.pallas_call(
        functools.partial(attend_kernel, members, heads),
        grid_spec=pltpu.PrefetchScalarGridSpec(
            num_scalar_prefetch=1,
            grid=(members,),
            in_specs=[
                pl.BlockSpec((rows, latent_width), lambda m, s: (m, 0)),
                *packed_specs(gathered),
                pl.BlockSpec((rows, HD), lambda m, s: (m, last)),
                pl.BlockSpec((rows, HD), lambda m, s: (m, last + 1)),
            ],
            out_specs=[block, block, pl.BlockSpec((rows, width), lambda m, s: (m, 0))],
            scratch_shapes=[pltpu.VMEM((rows, HD // 2), f32), pltpu.VMEM((rows, HD // 2), f32)],
        ),
        out_shape=[out, out, jax.ShapeDtypeStruct((total, width), bf16)],
        compiler_params=pltpu.CompilerParams(vmem_limit_bytes=40 * 2**20),
        cost_estimate=pl.CostEstimate(
            flops=2 * total * heads * HD * (latent_width + 2 * rows + width),
            bytes_accessed=total * heads * HD * 4 + total * latent_width * 3 + 8 * 2**20,
            transcendentals=total * heads * rows,
        ),
    )(lengths, packed, gathered, gathered, packed, packed)


def attend_back_kernel(
    members,
    heads,
    lengths_ref,
    grad_ref,
    weight_ref,
    out_ref,
    query_ref,
    key_ref,
    value_ref,
    packed_ref,
    query_grads_ref,
    cos_ref,
    sin_ref,
):
    fill_angles(lengths_ref, cos_ref, sin_ref)
    latent_width = packed_ref.shape[1] - 2 * HD
    step = latent_width // members
    out_full = out_ref[...].reshape(heads * HD, -1)
    scale = 1.0 / math.sqrt(HD)
    key_rot, value_low = key_ref[...], value_ref[...]
    mixture_grads = dot_nt(grad_ref[...], out_full).astype(bf16)
    key_grad = jnp.zeros(key_rot.shape, f32)
    value_grad = jnp.zeros(key_rot.shape, f32)
    for head in range(heads):
        columns = slice(head * HD, (head + 1) * HD)
        query_rot, mixture_grad = query_ref[:, columns], mixture_grads[:, columns]
        probs = probabilities(query_rot, key_rot, lengths_ref)
        probs_grad = dot_nt(mixture_grad, value_low)
        row_dot = jnp.sum(probs * probs_grad, axis=-1, keepdims=True)
        score_grad = (probs * (probs_grad - row_dot)).astype(bf16)
        query_rot_grad = dot(score_grad, key_rot) * scale
        query_grads_ref[:, columns] = turn(query_rot_grad, cos_ref[...], -sin_ref[...]).astype(bf16)
        key_grad += dot_tn(score_grad, query_rot)
        value_grad += dot_tn(probs.astype(bf16), mixture_grad)
    for k in range(members):
        latent_part = dot_nt(query_grads_ref[...], query_block(weight_ref, k, heads))
        packed_ref[:, k * step : (k + 1) * step] = latent_part.astype(bf16)
    packed_ref[:, latent_width : latent_width + HD] = (key_grad * scale).astype(bf16)
    packed_ref[:, latent_width + HD :] = value_grad.astype(bf16)


def gathered_grad_kernel(members, heads, grads_ref, mixes_ref, latents_ref, query_grads_ref, gathered_grad_ref):
    ring, held, width = gathered_grad_ref.shape
    held = held // 3
    count, step = HD // (2 * held), latents_ref.shape[1] // members
    for head in range(heads):
        columns = slice(head * HD, (head + 1) * HD)
        part = dot_tn(mixes_ref[:, columns], grads_ref[...]).astype(bf16)
        gathered_grad_ref[head * count : (head + 1) * count, : 2 * held] = part.reshape(count, 2 * held, width)
    for k in range(members):
        part = dot_tn(latents_ref[:, k * step : (k + 1) * step], query_grads_ref[...]).astype(bf16)
        high, low = divmod(k, 2)
        place = slice(2 * held + low * held // 2, 2 * held + (low + 1) * held // 2)
        columns = slice(high * width // 2, (high + 1) * width // 2)
        gathered_grad_ref[:, place, columns] = part.reshape(ring, held // 2, width // 2)


def gathered_grads(attn_grad, mixture, packed, query_grads, shape, heads):
    total, width = attn_grad.shape
    members, latent_width = 4, packed.shape[1] - 2 * HD

    def whole(columns):
        return pl.BlockSpec((total, columns), lambda i: (0, 0))

    return pl.pallas_call(
        functools.partial(gathered_grad_kernel, members, heads),
        grid=(1,),
        in_specs=[whole(width), whole(heads * HD), whole(latent_width), whole(heads * HD)],
        out_specs=pl.BlockSpec(shape, lambda i: (0, 0, 0)),
        out_shape=jax.ShapeDtypeStruct(shape, bf16),
        compiler_params=pltpu.CompilerParams(vmem_limit_bytes=52 * 2**20),
        cost_estimate=pl.CostEstimate(
            flops=2 * total * heads * HD * (width + latent_width),
            bytes_accessed=16 * 2**20,
            transcendentals=0,
        ),
    )(attn_grad, mixture, packed, query_grads)


def attend_back(lengths, attn_grad, gathered, query_rot, packed, rows, heads):
    total, width = attn_grad.shape
    latent_width = packed.shape[1] - 2 * HD
    last, members = latent_width // HD, total // rows
    block = pl.BlockSpec((rows, heads * HD), lambda m, s: (m, 0))

    return pl.pallas_call(
        functools.partial(attend_back_kernel, members, heads),
        grid_spec=pltpu.PrefetchScalarGridSpec(
            num_scalar_prefetch=1,
            grid=(members,),
            in_specs=[
                pl.BlockSpec((rows, width), lambda m, s: (m, 0)),
                *packed_specs(gathered),
                block,
                pl.BlockSpec((rows, HD), lambda m, s: (m, last)),
                pl.BlockSpec((rows, HD), lambda m, s: (m, last + 1)),
            ],
            out_specs=[
                pl.BlockSpec((rows, packed.shape[1]), lambda m, s: (m, 0)),
                block,
            ],
            scratch_shapes=[
                pltpu.VMEM((rows, HD // 2), f32),
                pltpu.VMEM((rows, HD // 2), f32),
            ],
        ),
        out_shape=[
            jax.ShapeDtypeStruct(packed.shape, bf16),
            jax.ShapeDtypeStruct((total, heads * HD), bf16),
        ],
        compiler_params=pltpu.CompilerParams(vmem_limit_bytes=56 * 2**20),
        cost_estimate=pl.CostEstimate(
            flops=2 * total * heads * HD * (width + latent_width + 5 * rows),
            bytes_accessed=total * heads * HD * 8 + total * width * 4,
            transcendentals=total * heads * rows,
        ),
    )(lengths, attn_grad, gathered, gathered, query_rot, packed, packed)


def finish_kernel(
    devices,
    held,
    cores,
    me_ref,
    own_ref,
    first_ref,
    second_ref,
    last_a_ref,
    last_b_ref,
    latent_ref,
    latent_scale_ref,
    cos_ref,
    sin_ref,
    attn_in_ref,
    tokens_ref,
    attn_scale_ref,
    parts_ref,
    residual_grad_ref,
    mlp_gain_ref,
    *results,
):
    small_refs, (tokens_grad_ref, qkv_ref, back_ref) = results[:-3], results[-3:]
    rows, latent_width = latent_ref.shape
    width = tokens_ref.shape[1]
    qkv_width = qkv_ref.shape[1]
    half, members = rows // 2, 4
    step = width // members
    top = own_ref[:half].astype(f32) + first_ref[:half].astype(f32) + last_a_ref[...].astype(f32)
    low = own_ref[half:].astype(f32) + second_ref[:half].astype(f32) + last_b_ref[...].astype(f32)
    grads = jnp.concatenate([top, low], axis=0)
    _, normed, factor = normalize(latent_ref[...], 1.0)
    upstream = grads[:, :latent_width]
    latent_gain = jnp.sum(upstream * normed, axis=0, keepdims=True)
    scaled = upstream * latent_scale_ref[...]
    inner = jnp.mean(scaled * normed, axis=-1, keepdims=True)
    qkv_ref[:, :latent_width] = (factor * (scaled - normed * inner)).astype(bf16)
    key_grad = turn(grads[:, latent_width : latent_width + HD], cos_ref[...], -sin_ref[...])
    qkv_ref[:, latent_width : latent_width + HD] = key_grad.astype(bf16)
    qkv_ref[:, latent_width + HD :] = grads[:, latent_width + HD :].astype(bf16)
    qkv_grad = qkv_ref[...]
    for slot in range(members):
        part = dot_nt(qkv_grad, parts_ref[slot * step : (slot + 1) * step, :qkv_width])
        place = pl.multiple_of((me_ref[0] ^ slot) * step, step)
        back_ref[:, pl.ds(place, step)] = part
    _, normed, factor = normalize(tokens_ref[...].astype(f32), 1.0)
    upstream = back_ref[...]
    attn_gain = jnp.sum(upstream * normed, axis=0, keepdims=True)
    scaled = upstream * attn_scale_ref[...]
    inner = jnp.mean(scaled * normed, axis=-1, keepdims=True)
    tokens_grad_ref[...] = residual_grad_ref[...] + factor * (scaled - normed * inner)
    def store(start, columns, part):
        if cores != 2:
            small_refs[0][start : start + part.shape[0], columns] = part
            return
        part = part.reshape(-1, 2, width // devices, part.shape[1])
        one, two = (part[:, r].reshape(-1, part.shape[3]) for r in range(2))
        place = slice(start // 2, start // 2 + one.shape[0])
        for core, (mine, other) in enumerate(((one, two), (two, one))):

            @pl.when(me_ref[1] == core)
            def _():
                small_refs[0][place, columns] = mine
                small_refs[1][place, columns] = other

    for start in range(0, width, step):
        part = dot_tn(attn_in_ref[:, start : start + step], qkv_grad)
        store(start, slice(0, qkv_width), part.astype(bf16))
    line = lax.broadcasted_iota(jnp.int32, (128, width), 0)
    gains = jnp.where(line == 0, attn_gain, jnp.where(line == 1, mlp_gain_ref[...], 0.0))
    line = lax.broadcasted_iota(jnp.int32, (128, latent_width), 0)
    latents = jnp.where(line == 2, latent_gain, 0.0).T.reshape(devices, held, 128)
    gap = jnp.zeros((devices, width // devices - held, 128), f32)
    latents = jnp.concatenate([latents, gap], axis=1).reshape(width, 128)
    store(0, slice(qkv_width, qkv_width + 128), (gains.T + latents).astype(bf16))


def finish(me, cores, devices, held, own, sent, last, latent, latent_scale, cos_part, sin_part, attn_in, tokens,
           attn_scale, parts, residual_grad, mlp_gain_grad):
    args = (own, *sent, *last, latent, latent_scale, cos_part, sin_part, attn_in, tokens, attn_scale, parts,
            residual_grad, mlp_gain_grad)
    width, qkv_width = tokens.shape[1], own.shape[1]
    whole = pl.BlockSpec(memory_space=pltpu.VMEM)
    halves = 2 if cores == 2 else 1
    small = [jax.ShapeDtypeStruct((parts.shape[0] // halves, parts.shape[1]), bf16)] * halves
    return pl.pallas_call(
        functools.partial(finish_kernel, devices, held, cores),
        in_specs=[pl.BlockSpec(memory_space=pltpu.SMEM)] + [whole] * len(args),
        out_specs=[whole] * (len(small) + 1),
        out_shape=[*small, jax.ShapeDtypeStruct(residual_grad.shape, f32)],
        scratch_shapes=[pltpu.VMEM(own.shape, bf16), pltpu.VMEM(tokens.shape, f32)],
        compiler_params=pltpu.CompilerParams(vmem_limit_bytes=52 * 2**20),
        cost_estimate=pl.CostEstimate(
            flops=4 * tokens.shape[0] * width * qkv_width,
            bytes_accessed=parts.size * 4 + tokens.size * 14,
            transcendentals=0,
        ),
    )(jnp.stack([me, lax.axis_index("r")]), *args)


def by_block(values, code, count):
    step = values.shape[1] // count
    return jnp.concatenate(
        [lax.dynamic_slice_in_dim(values, (code ^ k) * step, step, 1) for k in range(count)], axis=1
    )


def shards(
    members,
    ring,
    cores,
    tokens,
    lengths,
    attn_gain,
    query_down,
    query_gain,
    query_up,
    key_weight,
    value_weight,
    out_weight,
    mlp_gain,
    gate_weight,
    up_weight,
    down_weight,
    cotangent,
):
    rows = tokens.shape[0]
    width = tokens.shape[1]
    latent_width = query_down.shape[1]
    heads = H // members
    devices = members * ring
    score_scale = 1.0 / math.sqrt(HD)
    d_rows = query_down.shape[0]

    def column(v):
        v = v.astype(bf16).reshape(-1, 1)
        return jnp.pad(v, ((0, d_rows - v.shape[0]), (0, 0)))

    own_offset, own_alive, _ = layout(lengths[0], rows)
    living = own_alive.astype(f32)
    own_cos, own_sin = angles(own_offset, HD)
    grad_rows = cotangent.astype(f32)
    ffn_grad_own = (living * grad_rows).astype(bf16)

    extra = jnp.concatenate(
        [column(attn_gain), column(mlp_gain), column(query_gain), column(lengths[0])], axis=1
    )
    extra = jnp.pad(extra, ((0, 0), (0, 128 - extra.shape[1])))
    small = jnp.concatenate([query_down, key_weight, value_weight, extra], axis=1)
    query_own = in_order(swap_blocks(lambda k: take_columns(query_up, k, members)))
    query_own = jnp.concatenate(
        [jnp.concatenate(query_own[:2], axis=0), jnp.concatenate(query_own[2:], axis=0)], axis=1
    )
    gathered = jnp.concatenate([out_weight, query_own], axis=0)
    qkv_parts, line = share_small(small, cores)
    gathered = lax.all_gather(after(gathered, line), RING, axis=0, tiled=False)
    gate_up_own = swap_blocks(
        lambda k: jnp.concatenate(
            [take_columns(gate_weight, k, members), take_columns(up_weight, k, members)], axis=1
        )
    )
    gate_up_own, down_own = after((jnp.stack(in_order(gate_up_own)), down_weight), qkv_parts)
    down_full = lax.all_gather(down_own, RING, axis=0, tiled=True)

    me, lane = lax.axis_index(DP), lax.axis_index(RING)
    qkv_width = latent_width + 2 * HD
    extra = qkv_parts[:, qkv_width:].reshape(members, ring * d_rows, -1)
    group_lengths = lax.dynamic_slice(
        extra, (0, lane * d_rows, 3), (members, lengths.shape[1], 1)
    ).reshape(members, -1).astype(jnp.int32)
    extra = [lax.dynamic_index_in_dim(extra, me ^ k, 0, keepdims=False) for k in range(members)]
    extra = jnp.concatenate(extra, axis=0).astype(f32).T
    attn_scale = extra[0:1]
    mlp_scale = extra[1:2]
    latent_scale = extra[2].reshape(devices, d_rows)[:, : query_gain.shape[0]].reshape(1, -1)

    token_rows = tokens.astype(f32)
    attn_out, _, _ = normalize(token_rows, attn_scale)
    attn_in = attn_out.astype(bf16)
    low = dot(by_block(attn_in, me, members), qkv_parts)
    latent = low[:, :latent_width]
    latent_out, _, _ = normalize(latent, latent_scale)
    latent_in = latent_out.astype(bf16)
    key_own = rotate(low[:, latent_width : latent_width + HD], own_cos, own_sin)
    value_own = low[:, latent_width + HD : qkv_width]
    packed = jnp.concatenate([latent_in, key_own.astype(bf16), value_own.astype(bf16)], axis=1)
    packed_found = fetch_first(packed, *GROUP)
    gate_up = lax.all_gather(gate_up_own, RING, axis=1, tiled=True).reshape(width, -1)
    cut = gate_up.shape[1] // 2
    packed = jnp.concatenate(fetch_last(packed, packed_found, *GROUP), axis=0)
    query_rot, mixture, attn_back = attend(group_lengths, packed, gathered, rows, heads)
    ffn_grad_found = fetch_first(after(ffn_grad_own, packed), *GROUP)
    attn_back = after(attn_back, ffn_grad_found)
    attn_slots = [attn_back[i * rows : (i + 1) * rows] for i in range(members)]
    attn_sent = send_first(attn_slots, *GROUP)
    one, two = ffn_grad_found
    ffn_grad = jnp.concatenate([ffn_grad_own, one, two, two], axis=0)
    ffn_grad_rest = (two[: rows // 2], one[rows // 2 :])
    attn_sum = send_last(attn_slots, after(attn_sent, ffn_grad, ffn_grad_rest), *GROUP)
    residual = token_rows + living * attn_sum

    ffn_out, ffn_normed, ffn_factor = normalize(residual, mlp_scale)
    ffn_in = jnp.concatenate(gather_quad(ffn_out.astype(bf16), *GROUP), axis=0)
    gate_up_act = dot(ffn_in, gate_up)
    ffn_grad_rest = after(ffn_grad_rest, ffn_in)
    ffn_grad_rest = after((trade(ffn_grad_rest[0], "x"), trade(ffn_grad_rest[1], "y")), gate_up_act)
    ffn_grad = lax.dynamic_update_slice(ffn_grad, ffn_grad_rest[0], (3 * rows, 0))
    ffn_grad = lax.dynamic_update_slice(ffn_grad, ffn_grad_rest[1], (3 * rows + rows // 2, 0))
    gate_act, up_act = gate_up_act[:, :cut], gate_up_act[:, cut:]
    sigmoid_gate = jax.nn.sigmoid(gate_act)
    silu_gate = gate_act * sigmoid_gate
    hidden = (silu_gate * up_act).astype(bf16)

    down_wgrad = dot_tn(hidden, ffn_grad).astype(bf16)
    down_share = lax.psum_scatter(down_wgrad, RING, scatter_dimension=0, tiled=True)

    hidden_grad = dot_nt(after(ffn_grad, down_wgrad), down_full)
    gate_grad = (
        hidden_grad * up_act * sigmoid_gate * (1.0 + gate_act * (1.0 - sigmoid_gate))
    ).astype(bf16)
    up_grad = (hidden_grad * silu_gate).astype(bf16)
    gate_up_grad = jnp.concatenate([gate_grad, up_grad], axis=1)
    back = dot_nt(gate_up_grad, gate_up).astype(bf16)
    slots = [back[i * rows : (i + 1) * rows] for i in range(members)]
    loads = first_loads(slots)
    back_sent = send_loads(loads, *GROUP)
    gate_up_wgrad = dot_tn(ffn_in, after(gate_up_grad, loads)).astype(bf16)
    loads = last_loads(slots, after(back_sent, gate_up_wgrad))
    gate_up_wgrad = after(gate_up_wgrad, loads)
    ffn_in_grad = sum_up(slots[0], back_sent, send_loads(loads, *GROUP[::-1]))
    residual_back, mlp_scale_grad = normalize_back(ffn_in_grad, ffn_normed, ffn_factor, mlp_scale)
    residual_grad = grad_rows + residual_back
    attn_grad = (living * residual_grad).astype(bf16)
    attn_grad = after(attn_grad, down_share, gate_up_wgrad)
    gate_up_share = lax.psum_scatter(
        gate_up_wgrad.reshape(members, width // members, -1), RING, scatter_dimension=1, tiled=True
    )
    attn_found = fetch_first(attn_grad, *GROUP)
    ffn_back = dot(after(hidden, attn_grad), down_full).astype(bf16)
    ffn_slots = [ffn_back[i * rows : (i + 1) * rows] for i in range(members)]
    attn_found = after(attn_found, ffn_back)
    attn_grad = jnp.concatenate(fetch_last(attn_grad, attn_found, *GROUP), axis=0)
    ffn_sent = send_loads(after(first_loads(ffn_slots), attn_grad), *GROUP)
    packed_grad, query_grads = attend_back(
        group_lengths,
        attn_grad,
        gathered,
        query_rot,
        packed,
        rows,
        heads,
    )
    packed_grad = after(packed_grad, ffn_sent)
    slots = [packed_grad[i * rows : (i + 1) * rows] for i in range(members)]
    loads = first_loads(slots)
    packed_sent = send_loads(loads, *GROUP)
    gathered_grad = gathered_grads(
        attn_grad, mixture, packed, after(query_grads, loads), gathered.shape, heads
    )
    loads = last_loads(slots, after(packed_sent, gathered_grad))
    gathered_grad = after(gathered_grad, loads)
    gathered_share = lax.psum_scatter(gathered_grad, RING, scatter_dimension=0, tiled=False)
    packed_last = send_loads(loads, *GROUP[::-1])
    *small_grad, tokens_grad = finish(
        me,
        cores,
        devices,
        query_gain.shape[0],
        slots[0],
        packed_sent,
        packed_last,
        latent,
        latent_scale,
        own_cos,
        own_sin,
        attn_in,
        tokens,
        attn_scale,
        qkv_parts,
        residual_grad,
        mlp_scale_grad.reshape(1, -1),
    )
    ffn_last = send_loads(last_loads(ffn_slots, ffn_sent), *GROUP[::-1])
    small_grad = after(small_grad, ffn_last)
    small_slots = small_first(small_grad, cores, d_rows)
    small_slots = after(small_slots, gate_up_share)
    small_sent = send_first(small_slots, *GROUP)
    loads = last_loads(small_slots, small_sent)
    small_last = send_loads(loads, *GROUP[::-1])
    gate_up_share = after(gate_up_share, loads).reshape(members, d_rows, -1)
    gate_up_found = swap_blocks(lambda k: lax.dynamic_index_in_dim(gate_up_share, k, 0, keepdims=False))
    small_last = after(small_last, gate_up_found)
    small_pairs = pairs_along_z(sum_up(small_slots[0], small_sent, small_last).astype(bf16))
    along = [along_z(small_pairs[code], code) for code in (1, 2, 3)]
    gathered_share, down_share = after((gathered_share, down_share), small_pairs)
    held = out_weight.shape[0]
    out_share = gathered_share[:held]

    def query_part(k):
        low = lax.dynamic_slice_in_dim(gathered_share, held + (k % 2) * (held // 4), held // 4, 0)
        return lax.dynamic_slice_in_dim(low, (k // 2) * (width // 2), width // 2, 1)

    query_found = swap_blocks(query_part)
    small_share = add_up([small_pairs[0], *after(along, query_found)])
    ffn_sum = sum_up(ffn_slots[0], ffn_sent, after(ffn_last, small_slots))
    layer_out = (residual + living * ffn_sum).astype(bf16)
    found = in_order(gate_up_found)
    gate_share = jnp.concatenate([part[:, :cut] for part in found], axis=1).astype(f32)
    up_share = jnp.concatenate([part[:, cut:] for part in found], axis=1).astype(f32)
    found = in_order(query_found)
    query_share = jnp.concatenate(found, axis=1).astype(f32)
    return (
        layer_out,
        tokens_grad,
        small_share[:, latent_width + 2 * HD],
        small_share[:, :latent_width],
        small_share[: query_gain.shape[0], latent_width + 2 * HD + 2],
        query_share,
        small_share[:, latent_width : latent_width + HD],
        small_share[:, latent_width + HD : latent_width + 2 * HD],
        out_share.astype(f32),
        small_share[:, latent_width + 2 * HD + 1],
        gate_share,
        up_share,
        down_share.astype(f32),
    )


def solution(mesh):
    members, ring = mesh.shape["dp"], mesh.shape["fsdp"]
    cores = mesh.devices.size // 16
    fine = jax.sharding.Mesh(mesh.devices.reshape(2, 2, 2, 2, cores), ALL)
    matrix, vector = P(ALL, None), P(ALL)
    in_specs = (
        matrix,
        matrix,
        vector,
        matrix,
        vector,
        matrix,
        matrix,
        matrix,
        matrix,
        vector,
        matrix,
        matrix,
        matrix,
        matrix,
    )
    out_specs = (
        matrix,
        matrix,
        vector,
        matrix,
        vector,
        matrix,
        matrix,
        matrix,
        matrix,
        vector,
        matrix,
        matrix,
        matrix,
    )

    def body(*args):
        return shards(members, ring, cores, *args)

    return jax.shard_map(body, mesh=fine, in_specs=in_specs, out_specs=out_specs, check_vma=False)
```

```python
import functools
import math

import jax
import jax.numpy as jnp
from jax import lax
from jax.experimental import pallas as pl
from jax.experimental.pallas import tpu as pltpu
from jax.sharding import PartitionSpec as P

H = 16
HD = 256
PAD = 32

eps = 1e-06
rope_base = 10000.0
masked_score = -1e30
ALL = ("y", "x", "zh", "zl", "r")
DP = ("y", "x")
GROUP = ("x", "y")
RING = ("zh", "zl", "r")
f32 = jnp.float32
bf16 = jnp.bfloat16


def layout(lengths, row_total):
    padded = (lengths + PAD - 1) // PAD * PAD
    count = lengths.shape[0]
    ends = []
    for s in range(count):
        ends.append(padded[s] if s == 0 else ends[-1] + padded[s])
    row = lax.broadcasted_iota(jnp.int32, (row_total, 1), 0)
    segment = jnp.zeros_like(row)
    start = jnp.zeros_like(row)
    alive = jnp.zeros(row.shape, jnp.bool_)
    for s in range(count):
        first = ends[s] - padded[s]
        member = (row >= first) & (row < ends[s])
        segment = jnp.where(member, s + 1, segment)
        start = jnp.where(member, first, start)
        alive = alive | (member & (row - first < lengths[s]))
    return row - start, alive, segment


def angles(offset, head_size):
    half_width = head_size // 2
    frequency = jnp.exp(
        jnp.arange(half_width, dtype=f32) * (-2.0 * math.log(rope_base) / head_size)
    )
    phase = offset.astype(f32) * frequency[None, :]
    return (jnp.cos(phase), jnp.sin(phase))


def rotate(values, cos_part, sin_part):
    half_width = values.shape[-1] // 2
    first_half = values[..., :half_width]
    second_half = values[..., half_width:]
    return jnp.concatenate(
        [
            first_half * cos_part - second_half * sin_part,
            second_half * cos_part + first_half * sin_part,
        ],
        axis=-1,
    )


def normalize(values, scale_gain):
    factor = lax.rsqrt(jnp.mean(values * values, axis=-1, keepdims=True) + eps)
    normed = values * factor
    return (normed * scale_gain, normed, factor)


def normalize_back(upstream, normed, factor, scale_gain):
    scaled = upstream * scale_gain
    gain_grad = jnp.sum(upstream * normed, axis=0)
    inner_mean = jnp.mean(scaled * normed, axis=-1, keepdims=True)
    return (factor * (scaled - normed * inner_mean), gain_grad)


def dot(a, b):
    return jnp.dot(a, b, preferred_element_type=f32)


def dot_nt(a, b):
    return lax.dot_general(a, b, (((1,), (1,)), ((), ())), preferred_element_type=f32)


def dot_tn(a, b):
    return lax.dot_general(a, b, (((0,), (0,)), ((), ())), preferred_element_type=f32)


def after(values, *others):
    return lax.optimization_barrier((values, others))[0]


def trade(values, axis):
    return lax.ppermute(values, axis, [(0, 1), (1, 0)])


def gather_quad(values, first, second):
    half = values.shape[0] // 2
    one = trade(values, first)
    two = trade(values, second)
    three = jnp.concatenate([trade(two[:half], first), trade(one[half:], second)], axis=0)
    return [values, one, two, three]


def fetch_first(values, first, second):
    return trade(values, first), trade(values, second)


def fetch_last(values, found, first, second):
    one, two = found
    half = values.shape[0] // 2
    return [values, one, two, trade(two[:half], first), trade(one[half:], second)]


def first_loads(slots):
    half = slots[1].shape[0] // 2
    return (
        jnp.concatenate([slots[1][:half], slots[3][:half]], axis=0),
        jnp.concatenate([slots[2][half:], slots[3][half:]], axis=0),
    )


def send_loads(loads, first, second):
    return trade(loads[0], first), trade(loads[1], second)


def last_loads(slots, sent):
    half, (ra, rb) = slots[1].shape[0] // 2, sent
    return (
        (slots[2][:half].astype(f32) + ra[half:].astype(f32)).astype(bf16),
        (slots[1][half:].astype(f32) + rb[half:].astype(f32)).astype(bf16),
    )


def sum_up(own, sent, last):
    half, own = own.shape[0] // 2, own.astype(f32)
    return jnp.concatenate(
        [
            own[:half] + sent[0][:half].astype(f32) + last[0].astype(f32),
            own[half:] + sent[1][:half].astype(f32) + last[1].astype(f32),
        ],
        axis=0,
    )


def send_first(slots, first, second):
    return send_loads(first_loads(slots), first, second)


def send_last(slots, sent, first, second):
    return sum_up(slots[0], sent, send_loads(last_loads(slots, sent), second, first))


def scatter_quad(slots, first, second):
    return send_last(slots, send_first(slots, first, second), first, second)


def scatter_rows(own, others, first, second):
    rows = own.shape[0]
    slots = [own] + [others[i * rows : (i + 1) * rows] for i in range(3)]
    return scatter_quad(slots, first, second)


def join_cores(mine, theirs):
    if theirs is None:
        return mine
    return (mine.astype(f32) + theirs.astype(f32)).astype(bf16)


def small_first(values, cores, n):
    if cores == 2:
        total = join_cores(values[0], trade(values[1], "r"))
    else:
        total = values[0].reshape(16, cores, n, -1)
        total = lax.psum_scatter(total, "r", scatter_dimension=1, tiled=False)
    total = total.reshape(4, 4 * n, -1)
    me = lax.axis_index(DP)
    return [lax.dynamic_index_in_dim(total, me ^ code, 0, keepdims=False) for code in range(4)]


def pairs_along_z(total):
    total = total.reshape(4, -1, total.shape[1])
    me = lax.axis_index("zh") * 2 + lax.axis_index("zl")
    return [lax.dynamic_index_in_dim(total, me ^ code, 0, keepdims=False) for code in range(4)]


def add_up(parts):
    total = parts[0].astype(f32)
    for part in parts[1:]:
        total = total + part.astype(f32)
    return total


def along_z(values, code):
    return lax.ppermute(values, ("zh", "zl"), [(i, i ^ code) for i in range(4)])


def share_small(values, cores):
    n, c = values.shape
    if cores != 2:
        whole = lax.all_gather(values, RING, axis=0, tiled=True)
        return jnp.concatenate(gather_quad(whole, *GROUP), axis=0), whole
    core, place = lax.axis_index("r"), lax.axis_index("zh") * 2 + lax.axis_index("zl")
    line = jnp.stack([values] + [along_z(values, code) for code in (1, 2, 3)])
    line = [lax.dynamic_index_in_dim(line, place ^ k, 0, keepdims=False) for k in range(4)]
    line = jnp.concatenate(line, axis=0)
    total = jnp.zeros((4, 4, 2, n, c), values.dtype)
    for slot, part in enumerate(gather_quad(line, *GROUP)):
        for where, piece in ((core, part), (1 - core, trade(part, "r"))):
            total = lax.dynamic_update_slice(total, piece.reshape(1, 4, 1, n, c), (slot, 0, where, 0, 0))
    return total.reshape(32 * n, c), line


def swap_blocks(block):
    me = lax.axis_index(DP)
    found = [block(me)]
    for code in (1, 2, 3):
        found.append(lax.ppermute(block(me ^ code), DP, [(i, i ^ code) for i in range(4)]))
    return found


def in_order(found):
    me, found = lax.axis_index(DP), jnp.stack(found)
    return [lax.dynamic_index_in_dim(found, me ^ k, 0, keepdims=False) for k in range(4)]


def take_columns(weight, k, members):
    step = weight.shape[1] // members
    return lax.dynamic_slice_in_dim(weight, k * step, step, 1)


def turn(values, cos_part, sin_part):
    half = values.shape[-1] // 2
    one, two = values[:, :half], values[:, half:]
    return jnp.concatenate([one * cos_part - two * sin_part, two * cos_part + one * sin_part], axis=-1)


def spans(lengths_ref, member):
    first, found = 0, []
    for s in range(lengths_ref.shape[1]):
        length = lengths_ref[member, s]
        end = first + (length + PAD - 1) // PAD * PAD
        found.append((first, end, first + length))
        first = end
    return found


def fill_angles(lengths_ref, cos_ref, sin_ref):
    rows, half = cos_ref.shape
    row = lax.broadcasted_iota(jnp.int32, (rows, half), 0)
    position = row
    for first, end, _ in spans(lengths_ref, pl.program_id(0)):
        position = jnp.where((row >= first) & (row < end), row - first, position)
    step = lax.broadcasted_iota(jnp.int32, (rows, half), 1).astype(f32)
    phase = position.astype(f32) * jnp.exp(step * (-math.log(rope_base) / half))
    cos_ref[...] = jnp.cos(phase)
    sin_ref[...] = jnp.sin(phase)


def probabilities(query_rot, key_rot, lengths_ref):
    rows = query_rot.shape[0]
    scores = dot_nt(query_rot, key_rot) * (1.0 / math.sqrt(HD))
    i = lax.broadcasted_iota(jnp.int32, (rows, rows), 0)
    j = lax.broadcasted_iota(jnp.int32, (rows, rows), 1)
    allowed = i == j
    for first, end, live in spans(lengths_ref, pl.program_id(0)):
        allowed = allowed | ((i >= first) & (i < end) & (j >= first) & (j < live) & (j <= i))
    scores = jnp.where(allowed, scores, masked_score)
    expo = jnp.exp(scores - jnp.max(scores, axis=-1, keepdims=True))
    return expo / jnp.sum(expo, axis=-1, keepdims=True)


def query_block(weight_ref, member, heads):
    ring, rows, width = weight_ref.shape
    high, low = divmod(member, 2)
    part = weight_ref[:, low * rows // 2 : (low + 1) * rows // 2, high * width // 2 : (high + 1) * width // 2]
    return part.reshape(ring * rows // 2, width // 2)


def attend_kernel(
    members,
    heads,
    lengths_ref,
    latent_ref,
    weight_ref,
    out_ref,
    key_ref,
    value_ref,
    query_ref,
    mix_ref,
    back_ref,
    cos_ref,
    sin_ref,
):
    fill_angles(lengths_ref, cos_ref, sin_ref)
    step = latent_ref.shape[1] // members
    queries = dot(latent_ref[:, :step], query_block(weight_ref, 0, heads))
    for k in range(1, members):
        queries += dot(latent_ref[:, k * step : (k + 1) * step], query_block(weight_ref, k, heads))
    for head in range(heads):
        columns = slice(head * HD, (head + 1) * HD)
        query_rot = turn(queries[:, columns], cos_ref[...], sin_ref[...]).astype(bf16)
        query_ref[:, columns] = query_rot
        probs = probabilities(query_rot, key_ref[...], lengths_ref)
        mix_ref[:, columns] = dot(probs.astype(bf16), value_ref[...]).astype(bf16)
    out_full = out_ref[...].reshape(heads * HD, -1)
    back_ref[...] = dot(mix_ref[...], out_full).astype(bf16)


def packed_specs(gathered):
    ring, rows, width = gathered.shape
    third = rows // 3
    return [
        pl.BlockSpec((ring, third, width), lambda m, s: (0, 2, 0), pipeline_mode=pl.Buffered(1)),
        pl.BlockSpec((ring, 2 * third, width), lambda m, s: (0, 0, 0), pipeline_mode=pl.Buffered(1)),
    ]


def attend(lengths, packed, gathered, rows, heads):
    total, width = packed.shape[0], gathered.shape[2]
    latent_width = packed.shape[1] - 2 * HD
    last, members = latent_width // HD, total // rows
    block = pl.BlockSpec((rows, heads * HD), lambda m, s: (m, 0))
    out = jax.ShapeDtypeStruct((total, heads * HD), bf16)
    return pl.pallas_call(
        functools.partial(attend_kernel, members, heads),
        grid_spec=pltpu.PrefetchScalarGridSpec(
            num_scalar_prefetch=1,
            grid=(members,),
            in_specs=[
                pl.BlockSpec((rows, latent_width), lambda m, s: (m, 0)),
                *packed_specs(gathered),
                pl.BlockSpec((rows, HD), lambda m, s: (m, last)),
                pl.BlockSpec((rows, HD), lambda m, s: (m, last + 1)),
            ],
            out_specs=[block, block, pl.BlockSpec((rows, width), lambda m, s: (m, 0))],
            scratch_shapes=[pltpu.VMEM((rows, HD // 2), f32), pltpu.VMEM((rows, HD // 2), f32)],
        ),
        out_shape=[out, out, jax.ShapeDtypeStruct((total, width), bf16)],
        compiler_params=pltpu.CompilerParams(vmem_limit_bytes=40 * 2**20),
        cost_estimate=pl.CostEstimate(
            flops=2 * total * heads * HD * (latent_width + 2 * rows + width),
            bytes_accessed=total * heads * HD * 4 + total * latent_width * 3 + 8 * 2**20,
            transcendentals=total * heads * rows,
        ),
    )(lengths, packed, gathered, gathered, packed, packed)


def attend_back_kernel(
    members,
    heads,
    lengths_ref,
    grad_ref,
    weight_ref,
    out_ref,
    query_ref,
    key_ref,
    value_ref,
    packed_ref,
    query_grads_ref,
    cos_ref,
    sin_ref,
):
    fill_angles(lengths_ref, cos_ref, sin_ref)
    latent_width = packed_ref.shape[1] - 2 * HD
    step = latent_width // members
    out_full = out_ref[...].reshape(heads * HD, -1)
    scale = 1.0 / math.sqrt(HD)
    key_rot, value_low = key_ref[...], value_ref[...]
    mixture_grads = dot_nt(grad_ref[...], out_full).astype(bf16)
    key_grad = jnp.zeros(key_rot.shape, f32)
    value_grad = jnp.zeros(key_rot.shape, f32)
    for head in range(heads):
        columns = slice(head * HD, (head + 1) * HD)
        query_rot, mixture_grad = query_ref[:, columns], mixture_grads[:, columns]
        probs = probabilities(query_rot, key_rot, lengths_ref)
        probs_grad = dot_nt(mixture_grad, value_low)
        row_dot = jnp.sum(probs * probs_grad, axis=-1, keepdims=True)
        score_grad = (probs * (probs_grad - row_dot)).astype(bf16)
        query_rot_grad = dot(score_grad, key_rot) * scale
        query_grads_ref[:, columns] = turn(query_rot_grad, cos_ref[...], -sin_ref[...]).astype(bf16)
        key_grad += dot_tn(score_grad, query_rot)
        value_grad += dot_tn(probs.astype(bf16), mixture_grad)
    for k in range(members):
        latent_part = dot_nt(query_grads_ref[...], query_block(weight_ref, k, heads))
        packed_ref[:, k * step : (k + 1) * step] = latent_part.astype(bf16)
    packed_ref[:, latent_width : latent_width + HD] = (key_grad * scale).astype(bf16)
    packed_ref[:, latent_width + HD :] = value_grad.astype(bf16)


def gathered_grad_kernel(members, heads, grads_ref, mixes_ref, latents_ref, query_grads_ref, gathered_grad_ref):
    ring, held, width = gathered_grad_ref.shape
    held = held // 3
    count, step = HD // (2 * held), latents_ref.shape[1] // members
    for head in range(heads):
        columns = slice(head * HD, (head + 1) * HD)
        part = dot_tn(mixes_ref[:, columns], grads_ref[...]).astype(bf16)
        gathered_grad_ref[head * count : (head + 1) * count, : 2 * held] = part.reshape(count, 2 * held, width)
    for k in range(members):
        part = dot_tn(latents_ref[:, k * step : (k + 1) * step], query_grads_ref[...]).astype(bf16)
        high, low = divmod(k, 2)
        place = slice(2 * held + low * held // 2, 2 * held + (low + 1) * held // 2)
        columns = slice(high * width // 2, (high + 1) * width // 2)
        gathered_grad_ref[:, place, columns] = part.reshape(ring, held // 2, width // 2)


def gathered_grads(attn_grad, mixture, packed, query_grads, shape, heads):
    total, width = attn_grad.shape
    members, latent_width = 4, packed.shape[1] - 2 * HD

    def whole(columns):
        return pl.BlockSpec((total, columns), lambda i: (0, 0))

    return pl.pallas_call(
        functools.partial(gathered_grad_kernel, members, heads),
        grid=(1,),
        in_specs=[whole(width), whole(heads * HD), whole(latent_width), whole(heads * HD)],
        out_specs=pl.BlockSpec(shape, lambda i: (0, 0, 0)),
        out_shape=jax.ShapeDtypeStruct(shape, bf16),
        compiler_params=pltpu.CompilerParams(vmem_limit_bytes=52 * 2**20),
        cost_estimate=pl.CostEstimate(
            flops=2 * total * heads * HD * (width + latent_width),
            bytes_accessed=16 * 2**20,
            transcendentals=0,
        ),
    )(attn_grad, mixture, packed, query_grads)


def attend_back(lengths, attn_grad, gathered, query_rot, packed, rows, heads):
    total, width = attn_grad.shape
    latent_width = packed.shape[1] - 2 * HD
    last, members = latent_width // HD, total // rows
    block = pl.BlockSpec((rows, heads * HD), lambda m, s: (m, 0))

    return pl.pallas_call(
        functools.partial(attend_back_kernel, members, heads),
        grid_spec=pltpu.PrefetchScalarGridSpec(
            num_scalar_prefetch=1,
            grid=(members,),
            in_specs=[
                pl.BlockSpec((rows, width), lambda m, s: (m, 0)),
                *packed_specs(gathered),
                block,
                pl.BlockSpec((rows, HD), lambda m, s: (m, last)),
                pl.BlockSpec((rows, HD), lambda m, s: (m, last + 1)),
            ],
            out_specs=[
                pl.BlockSpec((rows, packed.shape[1]), lambda m, s: (m, 0)),
                block,
            ],
            scratch_shapes=[
                pltpu.VMEM((rows, HD // 2), f32),
                pltpu.VMEM((rows, HD // 2), f32),
            ],
        ),
        out_shape=[
            jax.ShapeDtypeStruct(packed.shape, bf16),
            jax.ShapeDtypeStruct((total, heads * HD), bf16),
        ],
        compiler_params=pltpu.CompilerParams(vmem_limit_bytes=56 * 2**20),
        cost_estimate=pl.CostEstimate(
            flops=2 * total * heads * HD * (width + latent_width + 5 * rows),
            bytes_accessed=total * heads * HD * 8 + total * width * 4,
            transcendentals=total * heads * rows,
        ),
    )(lengths, attn_grad, gathered, gathered, query_rot, packed, packed)


def finish_kernel(
    devices,
    held,
    cores,
    me_ref,
    own_ref,
    first_ref,
    second_ref,
    last_a_ref,
    last_b_ref,
    latent_ref,
    latent_scale_ref,
    cos_ref,
    sin_ref,
    attn_in_ref,
    tokens_ref,
    attn_scale_ref,
    parts_ref,
    residual_grad_ref,
    mlp_gain_ref,
    *results,
):
    small_refs, (tokens_grad_ref, qkv_ref, back_ref) = results[:-3], results[-3:]
    rows, latent_width = latent_ref.shape
    width = tokens_ref.shape[1]
    qkv_width = qkv_ref.shape[1]
    half, members = rows // 2, 4
    step = width // members
    top = own_ref[:half].astype(f32) + first_ref[:half].astype(f32) + last_a_ref[...].astype(f32)
    low = own_ref[half:].astype(f32) + second_ref[:half].astype(f32) + last_b_ref[...].astype(f32)
    grads = jnp.concatenate([top, low], axis=0)
    _, normed, factor = normalize(latent_ref[...], 1.0)
    upstream = grads[:, :latent_width]
    latent_gain = jnp.sum(upstream * normed, axis=0, keepdims=True)
    scaled = upstream * latent_scale_ref[...]
    inner = jnp.mean(scaled * normed, axis=-1, keepdims=True)
    qkv_ref[:, :latent_width] = (factor * (scaled - normed * inner)).astype(bf16)
    key_grad = turn(grads[:, latent_width : latent_width + HD], cos_ref[...], -sin_ref[...])
    qkv_ref[:, latent_width : latent_width + HD] = key_grad.astype(bf16)
    qkv_ref[:, latent_width + HD :] = grads[:, latent_width + HD :].astype(bf16)
    qkv_grad = qkv_ref[...]
    for slot in range(members):
        part = dot_nt(qkv_grad, parts_ref[slot * step : (slot + 1) * step, :qkv_width])
        place = pl.multiple_of((me_ref[0] ^ slot) * step, step)
        back_ref[:, pl.ds(place, step)] = part
    _, normed, factor = normalize(tokens_ref[...].astype(f32), 1.0)
    upstream = back_ref[...]
    attn_gain = jnp.sum(upstream * normed, axis=0, keepdims=True)
    scaled = upstream * attn_scale_ref[...]
    inner = jnp.mean(scaled * normed, axis=-1, keepdims=True)
    tokens_grad_ref[...] = residual_grad_ref[...] + factor * (scaled - normed * inner)
    def store(start, columns, part):
        if cores != 2:
            small_refs[0][start : start + part.shape[0], columns] = part
            return
        part = part.reshape(-1, 2, width // devices, part.shape[1])
        one, two = (part[:, r].reshape(-1, part.shape[3]) for r in range(2))
        place = slice(start // 2, start // 2 + one.shape[0])
        for core, (mine, other) in enumerate(((one, two), (two, one))):

            @pl.when(me_ref[1] == core)
            def _():
                small_refs[0][place, columns] = mine
                small_refs[1][place, columns] = other

    for start in range(0, width, step):
        part = dot_tn(attn_in_ref[:, start : start + step], qkv_grad)
        store(start, slice(0, qkv_width), part.astype(bf16))
    line = lax.broadcasted_iota(jnp.int32, (128, width), 0)
    gains = jnp.where(line == 0, attn_gain, jnp.where(line == 1, mlp_gain_ref[...], 0.0))
    line = lax.broadcasted_iota(jnp.int32, (128, latent_width), 0)
    latents = jnp.where(line == 2, latent_gain, 0.0).T.reshape(devices, held, 128)
    gap = jnp.zeros((devices, width // devices - held, 128), f32)
    latents = jnp.concatenate([latents, gap], axis=1).reshape(width, 128)
    store(0, slice(qkv_width, qkv_width + 128), (gains.T + latents).astype(bf16))


def finish(me, cores, devices, held, own, sent, last, latent, latent_scale, cos_part, sin_part, attn_in, tokens,
           attn_scale, parts, residual_grad, mlp_gain_grad):
    args = (own, *sent, *last, latent, latent_scale, cos_part, sin_part, attn_in, tokens, attn_scale, parts,
            residual_grad, mlp_gain_grad)
    width, qkv_width = tokens.shape[1], own.shape[1]
    whole = pl.BlockSpec(memory_space=pltpu.VMEM)
    halves = 2 if cores == 2 else 1
    small = [jax.ShapeDtypeStruct((parts.shape[0] // halves, parts.shape[1]), bf16)] * halves
    return pl.pallas_call(
        functools.partial(finish_kernel, devices, held, cores),
        in_specs=[pl.BlockSpec(memory_space=pltpu.SMEM)] + [whole] * len(args),
        out_specs=[whole] * (len(small) + 1),
        out_shape=[*small, jax.ShapeDtypeStruct(residual_grad.shape, f32)],
        scratch_shapes=[pltpu.VMEM(own.shape, bf16), pltpu.VMEM(tokens.shape, f32)],
        compiler_params=pltpu.CompilerParams(vmem_limit_bytes=52 * 2**20),
        cost_estimate=pl.CostEstimate(
            flops=4 * tokens.shape[0] * width * qkv_width,
            bytes_accessed=parts.size * 4 + tokens.size * 14,
            transcendentals=0,
        ),
    )(jnp.stack([me, lax.axis_index("r")]), *args)


def ffn_kernel(rows_ref, gate_ref, up_ref, hidden_ref, slope_ref, silu_ref):
    weights = jnp.concatenate([gate_ref[...], up_ref[...]], axis=1)
    act = dot(rows_ref[...], weights)
    gate, up = act[:, : gate_ref.shape[1]], act[:, gate_ref.shape[1] :]
    sigmoid = jax.nn.sigmoid(gate)
    silu = gate * sigmoid
    hidden_ref[...] = (silu * up).astype(bf16)
    slope_ref[...] = (up * sigmoid * (1.0 + gate * (1.0 - sigmoid))).astype(bf16)
    silu_ref[...] = silu.astype(bf16)


def ffn(rows, gate_up):
    total, width = rows.shape
    cut = gate_up.shape[1] // 2
    tile = 128
    block = pl.BlockSpec((total, tile), lambda j: (0, j))
    out = jax.ShapeDtypeStruct((total, cut), bf16)
    return pl.pallas_call(
        ffn_kernel,
        grid=(cut // tile,),
        in_specs=[
            pl.BlockSpec((total, width), lambda j: (0, 0), pipeline_mode=pl.Buffered(1)),
            pl.BlockSpec((width, tile), lambda j: (0, j)),
            pl.BlockSpec((width, tile), lambda j: (0, cut // tile + j)),
        ],
        out_specs=[block, block, block],
        out_shape=[out, out, out],
        compiler_params=pltpu.CompilerParams(vmem_limit_bytes=58 * 2**20),
        cost_estimate=pl.CostEstimate(
            flops=4 * total * width * cut,
            bytes_accessed=2 * (gate_up.size + rows.size + 3 * total * cut),
            transcendentals=total * cut,
        ),
    )(rows, gate_up, gate_up)


def ffn_back_kernel(grad_ref, down_ref, slope_ref, silu_ref, out_ref):
    cut = slope_ref.shape[1]
    hidden_grad = dot_nt(grad_ref[...], down_ref[...])
    out_ref[:, :cut] = (hidden_grad * slope_ref[...].astype(f32)).astype(bf16)
    out_ref[:, cut:] = (hidden_grad * silu_ref[...].astype(f32)).astype(bf16)


def ffn_back(grads, down_full, slope, silu):
    total, width = grads.shape
    cut, tile = slope.shape[1], total // 2
    block = pl.BlockSpec((tile, cut), lambda i: (i, 0))
    return pl.pallas_call(
        ffn_back_kernel,
        grid=(total // tile,),
        in_specs=[
            pl.BlockSpec((tile, width), lambda i: (i, 0)),
            pl.BlockSpec((cut, width), lambda i: (0, 0), pipeline_mode=pl.Buffered(1)),
            block,
            block,
        ],
        out_specs=pl.BlockSpec((tile, 2 * cut), lambda i: (i, 0)),
        out_shape=jax.ShapeDtypeStruct((total, 2 * cut), bf16),
        compiler_params=pltpu.CompilerParams(vmem_limit_bytes=58 * 2**20),
        cost_estimate=pl.CostEstimate(
            flops=2 * total * width * cut,
            bytes_accessed=2 * (grads.size + down_full.size + 4 * total * cut),
            transcendentals=0,
        ),
    )(grads, down_full, slope, silu)


def by_block(values, code, count):
    step = values.shape[1] // count
    return jnp.concatenate(
        [lax.dynamic_slice_in_dim(values, (code ^ k) * step, step, 1) for k in range(count)], axis=1
    )


def shards(
    members,
    ring,
    cores,
    tokens,
    lengths,
    attn_gain,
    query_down,
    query_gain,
    query_up,
    key_weight,
    value_weight,
    out_weight,
    mlp_gain,
    gate_weight,
    up_weight,
    down_weight,
    cotangent,
):
    rows = tokens.shape[0]
    width = tokens.shape[1]
    latent_width = query_down.shape[1]
    heads = H // members
    devices = members * ring
    score_scale = 1.0 / math.sqrt(HD)
    d_rows = query_down.shape[0]

    def column(v):
        v = v.astype(bf16).reshape(-1, 1)
        return jnp.pad(v, ((0, d_rows - v.shape[0]), (0, 0)))

    own_offset, own_alive, _ = layout(lengths[0], rows)
    living = own_alive.astype(f32)
    own_cos, own_sin = angles(own_offset, HD)
    grad_rows = cotangent.astype(f32)
    ffn_grad_own = (living * grad_rows).astype(bf16)

    extra = jnp.concatenate(
        [column(attn_gain), column(mlp_gain), column(query_gain), column(lengths[0])], axis=1
    )
    extra = jnp.pad(extra, ((0, 0), (0, 128 - extra.shape[1])))
    small = jnp.concatenate([query_down, key_weight, value_weight, extra], axis=1)
    query_own = in_order(swap_blocks(lambda k: take_columns(query_up, k, members)))
    query_own = jnp.concatenate(
        [jnp.concatenate(query_own[:2], axis=0), jnp.concatenate(query_own[2:], axis=0)], axis=1
    )
    gathered = jnp.concatenate([out_weight, query_own], axis=0)
    qkv_parts, line = share_small(small, cores)
    gathered = lax.all_gather(after(gathered, line), RING, axis=0, tiled=False)
    gate_up_own = swap_blocks(
        lambda k: jnp.concatenate(
            [take_columns(gate_weight, k, members), take_columns(up_weight, k, members)], axis=1
        )
    )
    gate_up_own, down_own = after((jnp.stack(in_order(gate_up_own)), down_weight), qkv_parts)
    down_full = lax.all_gather(down_own, RING, axis=0, tiled=True)

    me, lane = lax.axis_index(DP), lax.axis_index(RING)
    qkv_width = latent_width + 2 * HD
    extra = qkv_parts[:, qkv_width:].reshape(members, ring * d_rows, -1)
    group_lengths = lax.dynamic_slice(
        extra, (0, lane * d_rows, 3), (members, lengths.shape[1], 1)
    ).reshape(members, -1).astype(jnp.int32)
    extra = [lax.dynamic_index_in_dim(extra, me ^ k, 0, keepdims=False) for k in range(members)]
    extra = jnp.concatenate(extra, axis=0).astype(f32).T
    attn_scale = extra[0:1]
    mlp_scale = extra[1:2]
    latent_scale = extra[2].reshape(devices, d_rows)[:, : query_gain.shape[0]].reshape(1, -1)

    token_rows = tokens.astype(f32)
    attn_out, _, _ = normalize(token_rows, attn_scale)
    attn_in = attn_out.astype(bf16)
    low = dot(by_block(attn_in, me, members), qkv_parts)
    latent = low[:, :latent_width]
    latent_out, _, _ = normalize(latent, latent_scale)
    latent_in = latent_out.astype(bf16)
    key_own = rotate(low[:, latent_width : latent_width + HD], own_cos, own_sin)
    value_own = low[:, latent_width + HD : qkv_width]
    packed = jnp.concatenate([latent_in, key_own.astype(bf16), value_own.astype(bf16)], axis=1)
    packed_found = fetch_first(packed, *GROUP)
    gate_up = lax.all_gather(gate_up_own, RING, axis=1, tiled=True).reshape(width, -1)
    cut = gate_up.shape[1] // 2
    packed = jnp.concatenate(fetch_last(packed, packed_found, *GROUP), axis=0)
    query_rot, mixture, attn_back = attend(group_lengths, packed, gathered, rows, heads)
    ffn_grad_found = fetch_first(after(ffn_grad_own, packed), *GROUP)
    attn_back = after(attn_back, ffn_grad_found)
    attn_slots = [attn_back[i * rows : (i + 1) * rows] for i in range(members)]
    attn_sent = send_first(attn_slots, *GROUP)
    one, two = ffn_grad_found
    ffn_grad = jnp.concatenate([ffn_grad_own, one, two, two], axis=0)
    ffn_grad_rest = (two[: rows // 2], one[rows // 2 :])
    attn_sum = send_last(attn_slots, after(attn_sent, ffn_grad, ffn_grad_rest), *GROUP)
    residual = token_rows + living * attn_sum

    ffn_out, ffn_normed, ffn_factor = normalize(residual, mlp_scale)
    ffn_in = jnp.concatenate(gather_quad(ffn_out.astype(bf16), *GROUP), axis=0)
    hidden, slope, silu_gate = ffn(ffn_in, gate_up)
    ffn_grad_rest = after(ffn_grad_rest, ffn_in)
    ffn_grad_rest = after((trade(ffn_grad_rest[0], "x"), trade(ffn_grad_rest[1], "y")), hidden)
    ffn_grad = lax.dynamic_update_slice(ffn_grad, ffn_grad_rest[0], (3 * rows, 0))
    ffn_grad = lax.dynamic_update_slice(ffn_grad, ffn_grad_rest[1], (3 * rows + rows // 2, 0))
    down_wgrad = dot_tn(hidden, ffn_grad).astype(bf16)
    down_share = lax.psum_scatter(down_wgrad, RING, scatter_dimension=0, tiled=True)

    gate_up_grad = ffn_back(after(ffn_grad, down_wgrad), down_full, slope, silu_gate)
    back = dot_nt(gate_up_grad, gate_up).astype(bf16)
    slots = [back[i * rows : (i + 1) * rows] for i in range(members)]
    loads = first_loads(slots)
    back_sent = send_loads(loads, *GROUP)
    gate_up_wgrad = dot_tn(ffn_in, after(gate_up_grad, loads)).astype(bf16)
    loads = last_loads(slots, after(back_sent, gate_up_wgrad))
    gate_up_wgrad = after(gate_up_wgrad, loads)
    ffn_in_grad = sum_up(slots[0], back_sent, send_loads(loads, *GROUP[::-1]))
    residual_back, mlp_scale_grad = normalize_back(ffn_in_grad, ffn_normed, ffn_factor, mlp_scale)
    residual_grad = grad_rows + residual_back
    attn_grad = (living * residual_grad).astype(bf16)
    attn_grad = after(attn_grad, down_share, gate_up_wgrad)
    gate_up_share = lax.psum_scatter(
        gate_up_wgrad.reshape(members, width // members, -1), RING, scatter_dimension=1, tiled=True
    )
    attn_found = fetch_first(attn_grad, *GROUP)
    ffn_part = dot(after(hidden, attn_grad), down_full).astype(bf16)
    ffn_slots = [ffn_part[i * rows : (i + 1) * rows] for i in range(members)]
    attn_found = after(attn_found, ffn_part)
    attn_grad = jnp.concatenate(fetch_last(attn_grad, attn_found, *GROUP), axis=0)
    ffn_sent = send_loads(after(first_loads(ffn_slots), attn_grad), *GROUP)
    packed_grad, query_grads = attend_back(
        group_lengths,
        attn_grad,
        gathered,
        query_rot,
        packed,
        rows,
        heads,
    )
    packed_grad = after(packed_grad, ffn_sent)
    slots = [packed_grad[i * rows : (i + 1) * rows] for i in range(members)]
    loads = first_loads(slots)
    packed_sent = send_loads(loads, *GROUP)
    gathered_grad = gathered_grads(
        attn_grad, mixture, packed, after(query_grads, loads), gathered.shape, heads
    )
    loads = last_loads(slots, after(packed_sent, gathered_grad))
    gathered_grad = after(gathered_grad, loads)
    gathered_share = lax.psum_scatter(gathered_grad, RING, scatter_dimension=0, tiled=False)
    packed_last = send_loads(loads, *GROUP[::-1])
    *small_grad, tokens_grad = finish(
        me,
        cores,
        devices,
        query_gain.shape[0],
        slots[0],
        packed_sent,
        packed_last,
        latent,
        latent_scale,
        own_cos,
        own_sin,
        attn_in,
        tokens,
        attn_scale,
        qkv_parts,
        residual_grad,
        mlp_scale_grad.reshape(1, -1),
    )
    ffn_last = send_loads(last_loads(ffn_slots, ffn_sent), *GROUP[::-1])
    small_grad = after(small_grad, ffn_last)
    small_slots = small_first(small_grad, cores, d_rows)
    small_slots = after(small_slots, gate_up_share)
    small_sent = send_first(small_slots, *GROUP)
    loads = last_loads(small_slots, small_sent)
    small_last = send_loads(loads, *GROUP[::-1])
    gate_up_share = after(gate_up_share, loads).reshape(members, d_rows, -1)
    gate_up_found = swap_blocks(lambda k: lax.dynamic_index_in_dim(gate_up_share, k, 0, keepdims=False))
    small_last = after(small_last, gate_up_found)
    small_pairs = pairs_along_z(sum_up(small_slots[0], small_sent, small_last).astype(bf16))
    small_pairs = after(small_pairs, gathered_share)
    along = [along_z(small_pairs[code], code) for code in (1, 2, 3)]
    gathered_share, down_share = after((gathered_share, down_share), small_pairs)
    held = out_weight.shape[0]
    out_share = gathered_share[:held]

    query_share = after(gathered_share, along[0])

    def query_part(k):
        low = lax.dynamic_slice_in_dim(query_share, held + (k % 2) * (held // 4), held // 4, 0)
        return lax.dynamic_slice_in_dim(low, (k // 2) * (width // 2), width // 2, 1)

    query_found = swap_blocks(query_part)
    small_share = add_up([small_pairs[0], *after(along, query_found)])
    ffn_sum = sum_up(*after((ffn_slots[0], ffn_sent, ffn_last), small_slots))
    layer_out = (residual + living * ffn_sum).astype(bf16)
    found = in_order(gate_up_found)
    gate_share = jnp.concatenate([part[:, :cut] for part in found], axis=1).astype(f32)
    up_share = jnp.concatenate([part[:, cut:] for part in found], axis=1).astype(f32)
    found = in_order(query_found)
    query_share = jnp.concatenate(found, axis=1).astype(f32)
    return (
        layer_out,
        tokens_grad,
        small_share[:, latent_width + 2 * HD],
        small_share[:, :latent_width],
        small_share[: query_gain.shape[0], latent_width + 2 * HD + 2],
        query_share,
        small_share[:, latent_width : latent_width + HD],
        small_share[:, latent_width + HD : latent_width + 2 * HD],
        out_share.astype(f32),
        small_share[:, latent_width + 2 * HD + 1],
        gate_share,
        up_share,
        down_share.astype(f32),
    )


def solution(mesh):
    members, ring = mesh.shape["dp"], mesh.shape["fsdp"]
    cores = mesh.devices.size // 16
    fine = jax.sharding.Mesh(mesh.devices.reshape(2, 2, 2, 2, cores), ALL)
    matrix, vector = P(ALL, None), P(ALL)
    in_specs = (
        matrix,
        matrix,
        vector,
        matrix,
        vector,
        matrix,
        matrix,
        matrix,
        matrix,
        vector,
        matrix,
        matrix,
        matrix,
        matrix,
    )
    out_specs = (
        matrix,
        matrix,
        vector,
        matrix,
        vector,
        matrix,
        matrix,
        matrix,
        matrix,
        vector,
        matrix,
        matrix,
        matrix,
    )

    def body(*args):
        return shards(members, ring, cores, *args)

    return jax.shard_map(body, mesh=fine, in_specs=in_specs, out_specs=out_specs, check_vma=False)
```

```python
import functools
import math

import jax
import jax.numpy as jnp
from jax import lax
from jax.experimental import pallas as pl
from jax.experimental.pallas import tpu as pltpu
from jax.sharding import PartitionSpec as P

H = 16
HD = 256
PAD = 32

eps = 1e-06
rope_base = 10000.0
masked_score = -1e30
ALL = ("y", "x", "zh", "zl", "r")
DP = ("y", "x")
GROUP = ("x", "y")
RING = ("zh", "zl", "r")
f32 = jnp.float32
bf16 = jnp.bfloat16


def layout(lengths, row_total):
    padded = (lengths + PAD - 1) // PAD * PAD
    count = lengths.shape[0]
    ends = []
    for s in range(count):
        ends.append(padded[s] if s == 0 else ends[-1] + padded[s])
    row = lax.broadcasted_iota(jnp.int32, (row_total, 1), 0)
    segment = jnp.zeros_like(row)
    start = jnp.zeros_like(row)
    alive = jnp.zeros(row.shape, jnp.bool_)
    for s in range(count):
        first = ends[s] - padded[s]
        member = (row >= first) & (row < ends[s])
        segment = jnp.where(member, s + 1, segment)
        start = jnp.where(member, first, start)
        alive = alive | (member & (row - first < lengths[s]))
    return row - start, alive, segment


def angles(offset, head_size):
    half_width = head_size // 2
    frequency = jnp.exp(
        jnp.arange(half_width, dtype=f32) * (-2.0 * math.log(rope_base) / head_size)
    )
    phase = offset.astype(f32) * frequency[None, :]
    return (jnp.cos(phase), jnp.sin(phase))


def rotate(values, cos_part, sin_part):
    half_width = values.shape[-1] // 2
    first_half = values[..., :half_width]
    second_half = values[..., half_width:]
    return jnp.concatenate(
        [
            first_half * cos_part - second_half * sin_part,
            second_half * cos_part + first_half * sin_part,
        ],
        axis=-1,
    )


def normalize(values, scale_gain):
    factor = lax.rsqrt(jnp.mean(values * values, axis=-1, keepdims=True) + eps)
    normed = values * factor
    return (normed * scale_gain, normed, factor)


def normalize_back(upstream, normed, factor, scale_gain):
    scaled = upstream * scale_gain
    gain_grad = jnp.sum(upstream * normed, axis=0)
    inner_mean = jnp.mean(scaled * normed, axis=-1, keepdims=True)
    return (factor * (scaled - normed * inner_mean), gain_grad)


def dot(a, b):
    return jnp.dot(a, b, preferred_element_type=f32)


def dot_nt(a, b):
    return lax.dot_general(a, b, (((1,), (1,)), ((), ())), preferred_element_type=f32)


def dot_tn(a, b):
    return lax.dot_general(a, b, (((0,), (0,)), ((), ())), preferred_element_type=f32)


def after(values, *others):
    return lax.optimization_barrier((values, others))[0]


def trade(values, axis):
    return lax.ppermute(values, axis, [(0, 1), (1, 0)])


def gather_quad(values, first, second):
    half = values.shape[0] // 2
    one = trade(values, first)
    two = trade(values, second)
    three = jnp.concatenate([trade(two[:half], first), trade(one[half:], second)], axis=0)
    return [values, one, two, three]


def fetch_first(values, first, second):
    return trade(values, first), trade(values, second)


def fetch_last(values, found, first, second):
    one, two = found
    half = values.shape[0] // 2
    return [values, one, two, trade(two[:half], first), trade(one[half:], second)]


def first_loads(slots):
    half = slots[1].shape[0] // 2
    return (
        jnp.concatenate([slots[1][:half], slots[3][:half]], axis=0),
        jnp.concatenate([slots[2][half:], slots[3][half:]], axis=0),
    )


def send_loads(loads, first, second):
    return trade(loads[0], first), trade(loads[1], second)


def last_loads(slots, sent):
    half, (ra, rb) = slots[1].shape[0] // 2, sent
    return (
        (slots[2][:half].astype(f32) + ra[half:].astype(f32)).astype(bf16),
        (slots[1][half:].astype(f32) + rb[half:].astype(f32)).astype(bf16),
    )


def sum_up(own, sent, last):
    half, own = own.shape[0] // 2, own.astype(f32)
    return jnp.concatenate(
        [
            own[:half] + sent[0][:half].astype(f32) + last[0].astype(f32),
            own[half:] + sent[1][:half].astype(f32) + last[1].astype(f32),
        ],
        axis=0,
    )


def send_first(slots, first, second):
    return send_loads(first_loads(slots), first, second)


def send_last(slots, sent, first, second):
    return sum_up(slots[0], sent, send_loads(last_loads(slots, sent), second, first))


def scatter_quad(slots, first, second):
    return send_last(slots, send_first(slots, first, second), first, second)


def scatter_rows(own, others, first, second):
    rows = own.shape[0]
    slots = [own] + [others[i * rows : (i + 1) * rows] for i in range(3)]
    return scatter_quad(slots, first, second)


def join_cores(mine, theirs):
    if theirs is None:
        return mine
    return (mine.astype(f32) + theirs.astype(f32)).astype(bf16)


def small_first(values, cores, n):
    if cores == 2:
        total = join_cores(values[0], trade(values[1], "r"))
    else:
        total = values[0].reshape(16, cores, n, -1)
        total = lax.psum_scatter(total, "r", scatter_dimension=1, tiled=False)
    total = total.reshape(4, 4 * n, -1)
    me = lax.axis_index(DP)
    return [lax.dynamic_index_in_dim(total, me ^ code, 0, keepdims=False) for code in range(4)]


def pairs_along_z(total):
    total = total.reshape(4, -1, total.shape[1])
    me = lax.axis_index("zh") * 2 + lax.axis_index("zl")
    return [lax.dynamic_index_in_dim(total, me ^ code, 0, keepdims=False) for code in range(4)]


def add_up(parts):
    total = parts[0].astype(f32)
    for part in parts[1:]:
        total = total + part.astype(f32)
    return total


def along_z(values, code):
    return lax.ppermute(values, ("zh", "zl"), [(i, i ^ code) for i in range(4)])


def share_small(values, cores):
    n, c = values.shape
    if cores != 2:
        whole = lax.all_gather(values, RING, axis=0, tiled=True)
        return jnp.concatenate(gather_quad(whole, *GROUP), axis=0), whole
    core, place = lax.axis_index("r"), lax.axis_index("zh") * 2 + lax.axis_index("zl")
    sent = [along_z(values, code) for code in (1, 2, 3)]
    line = jnp.stack([values] + sent)
    line = [lax.dynamic_index_in_dim(line, place ^ k, 0, keepdims=False) for k in range(4)]
    line = jnp.concatenate(line, axis=0)
    total = jnp.zeros((4, 4, 2, n, c), values.dtype)
    for slot, part in enumerate(gather_quad(line, *GROUP)):
        for where, piece in ((core, part), (1 - core, trade(part, "r"))):
            total = lax.dynamic_update_slice(total, piece.reshape(1, 4, 1, n, c), (slot, 0, where, 0, 0))
    return total.reshape(32 * n, c), sent[:2]


def swap_blocks(block):
    me = lax.axis_index(DP)
    found = [block(me)]
    for code in (1, 2, 3):
        found.append(lax.ppermute(block(me ^ code), DP, [(i, i ^ code) for i in range(4)]))
    return found


def in_order(found):
    me, found = lax.axis_index(DP), jnp.stack(found)
    return [lax.dynamic_index_in_dim(found, me ^ k, 0, keepdims=False) for k in range(4)]


def take_columns(weight, k, members):
    step = weight.shape[1] // members
    return lax.dynamic_slice_in_dim(weight, k * step, step, 1)


def turn(values, cos_part, sin_part):
    half = values.shape[-1] // 2
    one, two = values[:, :half], values[:, half:]
    return jnp.concatenate([one * cos_part - two * sin_part, two * cos_part + one * sin_part], axis=-1)


def spans(lengths_ref, member):
    first, found = 0, []
    for s in range(lengths_ref.shape[1]):
        length = lengths_ref[member, s]
        end = first + (length + PAD - 1) // PAD * PAD
        found.append((first, end, first + length))
        first = end
    return found


def fill_angles(lengths_ref, cos_ref, sin_ref):
    rows, half = cos_ref.shape
    row = lax.broadcasted_iota(jnp.int32, (rows, half), 0)
    position = row
    for first, end, _ in spans(lengths_ref, pl.program_id(0)):
        position = jnp.where((row >= first) & (row < end), row - first, position)
    step = lax.broadcasted_iota(jnp.int32, (rows, half), 1).astype(f32)
    phase = position.astype(f32) * jnp.exp(step * (-math.log(rope_base) / half))
    cos_ref[...] = jnp.cos(phase)
    sin_ref[...] = jnp.sin(phase)


def probabilities(query_rot, key_rot, lengths_ref):
    rows = query_rot.shape[0]
    scores = dot_nt(query_rot, key_rot) * (1.0 / math.sqrt(HD))
    i = lax.broadcasted_iota(jnp.int32, (rows, rows), 0)
    j = lax.broadcasted_iota(jnp.int32, (rows, rows), 1)
    allowed = i == j
    for first, end, live in spans(lengths_ref, pl.program_id(0)):
        allowed = allowed | ((i >= first) & (i < end) & (j >= first) & (j < live) & (j <= i))
    scores = jnp.where(allowed, scores, masked_score)
    expo = jnp.exp(scores - jnp.max(scores, axis=-1, keepdims=True))
    return expo / jnp.sum(expo, axis=-1, keepdims=True)


def query_block(weight_ref, member, heads):
    ring, rows, width = weight_ref.shape
    high, low = divmod(member, 2)
    part = weight_ref[:, low * rows // 2 : (low + 1) * rows // 2, high * width // 2 : (high + 1) * width // 2]
    return part.reshape(ring * rows // 2, width // 2)


def attend_kernel(
    members,
    heads,
    lengths_ref,
    latent_ref,
    weight_ref,
    out_ref,
    key_ref,
    value_ref,
    query_ref,
    mix_ref,
    back_ref,
    cos_ref,
    sin_ref,
):
    fill_angles(lengths_ref, cos_ref, sin_ref)
    step = latent_ref.shape[1] // members
    queries = dot(latent_ref[:, :step], query_block(weight_ref, 0, heads))
    for k in range(1, members):
        queries += dot(latent_ref[:, k * step : (k + 1) * step], query_block(weight_ref, k, heads))
    for head in range(heads):
        columns = slice(head * HD, (head + 1) * HD)
        query_rot = turn(queries[:, columns], cos_ref[...], sin_ref[...]).astype(bf16)
        query_ref[:, columns] = query_rot
        probs = probabilities(query_rot, key_ref[...], lengths_ref)
        mix_ref[:, columns] = dot(probs.astype(bf16), value_ref[...]).astype(bf16)
    out_full = out_ref[...].reshape(heads * HD, -1)
    back_ref[...] = dot(mix_ref[...], out_full).astype(bf16)


def packed_specs(gathered):
    ring, rows, width = gathered.shape
    third = rows // 3
    return [
        pl.BlockSpec((ring, third, width), lambda m, s: (0, 2, 0), pipeline_mode=pl.Buffered(1)),
        pl.BlockSpec((ring, 2 * third, width), lambda m, s: (0, 0, 0), pipeline_mode=pl.Buffered(1)),
    ]


def attend(lengths, packed, gathered, rows, heads):
    total, width = packed.shape[0], gathered.shape[2]
    latent_width = packed.shape[1] - 2 * HD
    last, members = latent_width // HD, total // rows
    block = pl.BlockSpec((rows, heads * HD), lambda m, s: (m, 0))
    out = jax.ShapeDtypeStruct((total, heads * HD), bf16)
    return pl.pallas_call(
        functools.partial(attend_kernel, members, heads),
        grid_spec=pltpu.PrefetchScalarGridSpec(
            num_scalar_prefetch=1,
            grid=(members,),
            in_specs=[
                pl.BlockSpec((rows, latent_width), lambda m, s: (m, 0)),
                *packed_specs(gathered),
                pl.BlockSpec((rows, HD), lambda m, s: (m, last)),
                pl.BlockSpec((rows, HD), lambda m, s: (m, last + 1)),
            ],
            out_specs=[block, block, pl.BlockSpec((rows, width), lambda m, s: (m, 0))],
            scratch_shapes=[pltpu.VMEM((rows, HD // 2), f32), pltpu.VMEM((rows, HD // 2), f32)],
        ),
        out_shape=[out, out, jax.ShapeDtypeStruct((total, width), bf16)],
        compiler_params=pltpu.CompilerParams(vmem_limit_bytes=40 * 2**20),
        cost_estimate=pl.CostEstimate(
            flops=2 * total * heads * HD * (latent_width + 2 * rows + width),
            bytes_accessed=total * heads * HD * 4 + total * latent_width * 3 + 8 * 2**20,
            transcendentals=total * heads * rows,
        ),
    )(lengths, packed, gathered, gathered, packed, packed)


def attend_back_kernel(
    members,
    heads,
    lengths_ref,
    grad_ref,
    weight_ref,
    out_ref,
    query_ref,
    key_ref,
    value_ref,
    packed_ref,
    query_grads_ref,
    cos_ref,
    sin_ref,
):
    fill_angles(lengths_ref, cos_ref, sin_ref)
    latent_width = packed_ref.shape[1] - 2 * HD
    step = latent_width // members
    out_full = out_ref[...].reshape(heads * HD, -1)
    scale = 1.0 / math.sqrt(HD)
    key_rot, value_low = key_ref[...], value_ref[...]
    mixture_grads = dot_nt(grad_ref[...], out_full).astype(bf16)
    key_grad = jnp.zeros(key_rot.shape, f32)
    value_grad = jnp.zeros(key_rot.shape, f32)
    for head in range(heads):
        columns = slice(head * HD, (head + 1) * HD)
        query_rot, mixture_grad = query_ref[:, columns], mixture_grads[:, columns]
        probs = probabilities(query_rot, key_rot, lengths_ref)
        probs_grad = dot_nt(mixture_grad, value_low)
        row_dot = jnp.sum(probs * probs_grad, axis=-1, keepdims=True)
        score_grad = (probs * (probs_grad - row_dot)).astype(bf16)
        query_rot_grad = dot(score_grad, key_rot) * scale
        query_grads_ref[:, columns] = turn(query_rot_grad, cos_ref[...], -sin_ref[...]).astype(bf16)
        key_grad += dot_tn(score_grad, query_rot)
        value_grad += dot_tn(probs.astype(bf16), mixture_grad)
    for k in range(members):
        latent_part = dot_nt(query_grads_ref[...], query_block(weight_ref, k, heads))
        packed_ref[:, k * step : (k + 1) * step] = latent_part.astype(bf16)
    packed_ref[:, latent_width : latent_width + HD] = (key_grad * scale).astype(bf16)
    packed_ref[:, latent_width + HD :] = value_grad.astype(bf16)


def gathered_grad_kernel(members, heads, grads_ref, mixes_ref, latents_ref, query_grads_ref, gathered_grad_ref):
    ring, held, width = gathered_grad_ref.shape
    held = held // 3
    count, step = HD // (2 * held), latents_ref.shape[1] // members
    for head in range(heads):
        columns = slice(head * HD, (head + 1) * HD)
        part = dot_tn(mixes_ref[:, columns], grads_ref[...]).astype(bf16)
        gathered_grad_ref[head * count : (head + 1) * count, : 2 * held] = part.reshape(count, 2 * held, width)
    for k in range(members):
        part = dot_tn(latents_ref[:, k * step : (k + 1) * step], query_grads_ref[...]).astype(bf16)
        high, low = divmod(k, 2)
        place = slice(2 * held + low * held // 2, 2 * held + (low + 1) * held // 2)
        columns = slice(high * width // 2, (high + 1) * width // 2)
        gathered_grad_ref[:, place, columns] = part.reshape(ring, held // 2, width // 2)


def gathered_grads(attn_grad, mixture, packed, query_grads, shape, heads):
    total, width = attn_grad.shape
    members, latent_width = 4, packed.shape[1] - 2 * HD

    def whole(columns):
        return pl.BlockSpec((total, columns), lambda i: (0, 0))

    return pl.pallas_call(
        functools.partial(gathered_grad_kernel, members, heads),
        grid=(1,),
        in_specs=[whole(width), whole(heads * HD), whole(latent_width), whole(heads * HD)],
        out_specs=pl.BlockSpec(shape, lambda i: (0, 0, 0)),
        out_shape=jax.ShapeDtypeStruct(shape, bf16),
        compiler_params=pltpu.CompilerParams(vmem_limit_bytes=52 * 2**20),
        cost_estimate=pl.CostEstimate(
            flops=2 * total * heads * HD * (width + latent_width),
            bytes_accessed=16 * 2**20,
            transcendentals=0,
        ),
    )(attn_grad, mixture, packed, query_grads)


def attend_back(lengths, attn_grad, gathered, query_rot, packed, rows, heads):
    total, width = attn_grad.shape
    latent_width = packed.shape[1] - 2 * HD
    last, members = latent_width // HD, total // rows
    block = pl.BlockSpec((rows, heads * HD), lambda m, s: (m, 0))

    return pl.pallas_call(
        functools.partial(attend_back_kernel, members, heads),
        grid_spec=pltpu.PrefetchScalarGridSpec(
            num_scalar_prefetch=1,
            grid=(members,),
            in_specs=[
                pl.BlockSpec((rows, width), lambda m, s: (m, 0)),
                *packed_specs(gathered),
                block,
                pl.BlockSpec((rows, HD), lambda m, s: (m, last)),
                pl.BlockSpec((rows, HD), lambda m, s: (m, last + 1)),
            ],
            out_specs=[
                pl.BlockSpec((rows, packed.shape[1]), lambda m, s: (m, 0)),
                block,
            ],
            scratch_shapes=[
                pltpu.VMEM((rows, HD // 2), f32),
                pltpu.VMEM((rows, HD // 2), f32),
            ],
        ),
        out_shape=[
            jax.ShapeDtypeStruct(packed.shape, bf16),
            jax.ShapeDtypeStruct((total, heads * HD), bf16),
        ],
        compiler_params=pltpu.CompilerParams(vmem_limit_bytes=56 * 2**20),
        cost_estimate=pl.CostEstimate(
            flops=2 * total * heads * HD * (width + latent_width + 5 * rows),
            bytes_accessed=total * heads * HD * 8 + total * width * 4,
            transcendentals=total * heads * rows,
        ),
    )(lengths, attn_grad, gathered, gathered, query_rot, packed, packed)


def finish_kernel(
    devices,
    held,
    cores,
    me_ref,
    own_ref,
    first_ref,
    second_ref,
    last_a_ref,
    last_b_ref,
    latent_ref,
    latent_scale_ref,
    cos_ref,
    sin_ref,
    attn_in_ref,
    tokens_ref,
    attn_scale_ref,
    parts_ref,
    residual_grad_ref,
    mlp_gain_ref,
    *results,
):
    small_refs, (tokens_grad_ref, qkv_ref, back_ref) = results[:-3], results[-3:]
    rows, latent_width = latent_ref.shape
    width = tokens_ref.shape[1]
    qkv_width = qkv_ref.shape[1]
    half, members = rows // 2, 4
    step = width // members
    top = own_ref[:half].astype(f32) + first_ref[:half].astype(f32) + last_a_ref[...].astype(f32)
    low = own_ref[half:].astype(f32) + second_ref[:half].astype(f32) + last_b_ref[...].astype(f32)
    grads = jnp.concatenate([top, low], axis=0)
    _, normed, factor = normalize(latent_ref[...], 1.0)
    upstream = grads[:, :latent_width]
    latent_gain = jnp.sum(upstream * normed, axis=0, keepdims=True)
    scaled = upstream * latent_scale_ref[...]
    inner = jnp.mean(scaled * normed, axis=-1, keepdims=True)
    qkv_ref[:, :latent_width] = (factor * (scaled - normed * inner)).astype(bf16)
    key_grad = turn(grads[:, latent_width : latent_width + HD], cos_ref[...], -sin_ref[...])
    qkv_ref[:, latent_width : latent_width + HD] = key_grad.astype(bf16)
    qkv_ref[:, latent_width + HD :] = grads[:, latent_width + HD :].astype(bf16)
    qkv_grad = qkv_ref[...]
    for slot in range(members):
        part = dot_nt(qkv_grad, parts_ref[slot * step : (slot + 1) * step, :qkv_width])
        place = pl.multiple_of((me_ref[0] ^ slot) * step, step)
        back_ref[:, pl.ds(place, step)] = part
    _, normed, factor = normalize(tokens_ref[...].astype(f32), 1.0)
    upstream = back_ref[...]
    attn_gain = jnp.sum(upstream * normed, axis=0, keepdims=True)
    scaled = upstream * attn_scale_ref[...]
    inner = jnp.mean(scaled * normed, axis=-1, keepdims=True)
    tokens_grad_ref[...] = residual_grad_ref[...] + factor * (scaled - normed * inner)
    def store(start, columns, part):
        if cores != 2:
            small_refs[0][start : start + part.shape[0], columns] = part
            return
        part = part.reshape(-1, 2, width // devices, part.shape[1])
        one, two = (part[:, r].reshape(-1, part.shape[3]) for r in range(2))
        place = slice(start // 2, start // 2 + one.shape[0])
        for core, (mine, other) in enumerate(((one, two), (two, one))):

            @pl.when(me_ref[1] == core)
            def _():
                small_refs[0][place, columns] = mine
                small_refs[1][place, columns] = other

    for start in range(0, width, step):
        part = dot_tn(attn_in_ref[:, start : start + step], qkv_grad)
        store(start, slice(0, qkv_width), part.astype(bf16))
    line = lax.broadcasted_iota(jnp.int32, (128, width), 0)
    gains = jnp.where(line == 0, attn_gain, jnp.where(line == 1, mlp_gain_ref[...], 0.0))
    line = lax.broadcasted_iota(jnp.int32, (128, latent_width), 0)
    latents = jnp.where(line == 2, latent_gain, 0.0).T.reshape(devices, held, 128)
    gap = jnp.zeros((devices, width // devices - held, 128), f32)
    latents = jnp.concatenate([latents, gap], axis=1).reshape(width, 128)
    store(0, slice(qkv_width, qkv_width + 128), (gains.T + latents).astype(bf16))


def finish(me, cores, devices, held, own, sent, last, latent, latent_scale, cos_part, sin_part, attn_in, tokens,
           attn_scale, parts, residual_grad, mlp_gain_grad):
    args = (own, *sent, *last, latent, latent_scale, cos_part, sin_part, attn_in, tokens, attn_scale, parts,
            residual_grad, mlp_gain_grad)
    width, qkv_width = tokens.shape[1], own.shape[1]
    whole = pl.BlockSpec(memory_space=pltpu.VMEM)
    halves = 2 if cores == 2 else 1
    small = [jax.ShapeDtypeStruct((parts.shape[0] // halves, parts.shape[1]), bf16)] * halves
    return pl.pallas_call(
        functools.partial(finish_kernel, devices, held, cores),
        in_specs=[pl.BlockSpec(memory_space=pltpu.SMEM)] + [whole] * len(args),
        out_specs=[whole] * (len(small) + 1),
        out_shape=[*small, jax.ShapeDtypeStruct(residual_grad.shape, f32)],
        scratch_shapes=[pltpu.VMEM(own.shape, bf16), pltpu.VMEM(tokens.shape, f32)],
        compiler_params=pltpu.CompilerParams(vmem_limit_bytes=52 * 2**20),
        cost_estimate=pl.CostEstimate(
            flops=4 * tokens.shape[0] * width * qkv_width,
            bytes_accessed=parts.size * 4 + tokens.size * 14,
            transcendentals=0,
        ),
    )(jnp.stack([me, lax.axis_index("r")]), *args)


def ffn_kernel(rows_ref, gate_ref, up_ref, hidden_ref, slope_ref, silu_ref):
    weights = jnp.concatenate([gate_ref[...], up_ref[...]], axis=1)
    act = dot(rows_ref[...], weights)
    gate, up = act[:, : gate_ref.shape[1]], act[:, gate_ref.shape[1] :]
    sigmoid = jax.nn.sigmoid(gate)
    silu = gate * sigmoid
    hidden_ref[...] = (silu * up).astype(bf16)
    slope_ref[...] = (up * sigmoid * (1.0 + gate * (1.0 - sigmoid))).astype(bf16)
    silu_ref[...] = silu.astype(bf16)


def ffn(rows, gate_up):
    total, width = rows.shape
    cut = gate_up.shape[1] // 2
    tile = 128
    block = pl.BlockSpec((total, tile), lambda j: (0, j))
    out = jax.ShapeDtypeStruct((total, cut), bf16)
    return pl.pallas_call(
        ffn_kernel,
        grid=(cut // tile,),
        in_specs=[
            pl.BlockSpec((total, width), lambda j: (0, 0), pipeline_mode=pl.Buffered(1)),
            pl.BlockSpec((width, tile), lambda j: (0, j)),
            pl.BlockSpec((width, tile), lambda j: (0, cut // tile + j)),
        ],
        out_specs=[block, block, block],
        out_shape=[out, out, out],
        compiler_params=pltpu.CompilerParams(vmem_limit_bytes=58 * 2**20),
        cost_estimate=pl.CostEstimate(
            flops=4 * total * width * cut,
            bytes_accessed=2 * (gate_up.size + rows.size + 3 * total * cut),
            transcendentals=total * cut,
        ),
    )(rows, gate_up, gate_up)


def ffn_back_kernel(grad_ref, down_ref, slope_ref, silu_ref, out_ref):
    cut = slope_ref.shape[1]
    hidden_grad = dot_nt(grad_ref[...], down_ref[...])
    out_ref[:, :cut] = (hidden_grad * slope_ref[...].astype(f32)).astype(bf16)
    out_ref[:, cut:] = (hidden_grad * silu_ref[...].astype(f32)).astype(bf16)


def ffn_back(grads, down_full, slope, silu):
    total, width = grads.shape
    cut, tile = slope.shape[1], total // 2
    block = pl.BlockSpec((tile, cut), lambda i: (i, 0))
    return pl.pallas_call(
        ffn_back_kernel,
        grid=(total // tile,),
        in_specs=[
            pl.BlockSpec((tile, width), lambda i: (i, 0)),
            pl.BlockSpec((cut, width), lambda i: (0, 0), pipeline_mode=pl.Buffered(1)),
            block,
            block,
        ],
        out_specs=pl.BlockSpec((tile, 2 * cut), lambda i: (i, 0)),
        out_shape=jax.ShapeDtypeStruct((total, 2 * cut), bf16),
        compiler_params=pltpu.CompilerParams(vmem_limit_bytes=58 * 2**20),
        cost_estimate=pl.CostEstimate(
            flops=2 * total * width * cut,
            bytes_accessed=2 * (grads.size + down_full.size + 4 * total * cut),
            transcendentals=0,
        ),
    )(grads, down_full, slope, silu)


def by_block(values, code, count):
    step = values.shape[1] // count
    return jnp.concatenate(
        [lax.dynamic_slice_in_dim(values, (code ^ k) * step, step, 1) for k in range(count)], axis=1
    )


def shards(
    members,
    ring,
    cores,
    tokens,
    lengths,
    attn_gain,
    query_down,
    query_gain,
    query_up,
    key_weight,
    value_weight,
    out_weight,
    mlp_gain,
    gate_weight,
    up_weight,
    down_weight,
    cotangent,
):
    rows = tokens.shape[0]
    width = tokens.shape[1]
    latent_width = query_down.shape[1]
    heads = H // members
    devices = members * ring
    score_scale = 1.0 / math.sqrt(HD)
    d_rows = query_down.shape[0]

    def column(v):
        v = v.astype(bf16).reshape(-1, 1)
        return jnp.pad(v, ((0, d_rows - v.shape[0]), (0, 0)))

    own_offset, own_alive, _ = layout(lengths[0], rows)
    living = own_alive.astype(f32)
    own_cos, own_sin = angles(own_offset, HD)
    grad_rows = cotangent.astype(f32)
    ffn_grad_own = (living * grad_rows).astype(bf16)

    extra = jnp.concatenate(
        [column(attn_gain), column(mlp_gain), column(query_gain), column(lengths[0])], axis=1
    )
    extra = jnp.pad(extra, ((0, 0), (0, 128 - extra.shape[1])))
    small = jnp.concatenate([query_down, key_weight, value_weight, extra], axis=1)
    query_own = in_order(swap_blocks(lambda k: take_columns(query_up, k, members)))
    query_own = jnp.concatenate(
        [jnp.concatenate(query_own[:2], axis=0), jnp.concatenate(query_own[2:], axis=0)], axis=1
    )
    gathered = jnp.concatenate([out_weight, query_own], axis=0)
    qkv_parts, line = share_small(small, cores)
    gathered = lax.all_gather(after(gathered, line), RING, axis=0, tiled=False)
    gate_up_own = swap_blocks(
        lambda k: jnp.concatenate(
            [take_columns(gate_weight, k, members), take_columns(up_weight, k, members)], axis=1
        )
    )
    gate_up_own, down_own = after((jnp.stack(in_order(gate_up_own)), down_weight), qkv_parts)
    down_full = lax.all_gather(down_own, RING, axis=0, tiled=True)

    me, lane = lax.axis_index(DP), lax.axis_index(RING)
    qkv_width = latent_width + 2 * HD
    extra = qkv_parts[:, qkv_width:].reshape(members, ring * d_rows, -1)
    group_lengths = lax.dynamic_slice(
        extra, (0, lane * d_rows, 3), (members, lengths.shape[1], 1)
    ).reshape(members, -1).astype(jnp.int32)
    extra = [lax.dynamic_index_in_dim(extra, me ^ k, 0, keepdims=False) for k in range(members)]
    extra = jnp.concatenate(extra, axis=0).astype(f32).T
    attn_scale = extra[0:1]
    mlp_scale = extra[1:2]
    latent_scale = extra[2].reshape(devices, d_rows)[:, : query_gain.shape[0]].reshape(1, -1)

    token_rows = tokens.astype(f32)
    attn_out, _, _ = normalize(token_rows, attn_scale)
    attn_in = attn_out.astype(bf16)
    low = dot(by_block(attn_in, me, members), qkv_parts)
    latent = low[:, :latent_width]
    latent_out, _, _ = normalize(latent, latent_scale)
    latent_in = latent_out.astype(bf16)
    key_own = rotate(low[:, latent_width : latent_width + HD], own_cos, own_sin)
    value_own = low[:, latent_width + HD : qkv_width]
    packed = jnp.concatenate([latent_in, key_own.astype(bf16), value_own.astype(bf16)], axis=1)
    packed_found = fetch_first(packed, *GROUP)
    gate_up = lax.all_gather(gate_up_own, RING, axis=1, tiled=True).reshape(width, -1)
    cut = gate_up.shape[1] // 2
    packed = jnp.concatenate(fetch_last(packed, packed_found, *GROUP), axis=0)
    query_rot, mixture, attn_back = attend(group_lengths, packed, gathered, rows, heads)
    ffn_grad_found = fetch_first(after(ffn_grad_own, packed), *GROUP)
    attn_back = after(attn_back, ffn_grad_found)
    attn_slots = [attn_back[i * rows : (i + 1) * rows] for i in range(members)]
    attn_sent = send_first(attn_slots, *GROUP)
    one, two = ffn_grad_found
    ffn_grad = jnp.concatenate([ffn_grad_own, one, two, two], axis=0)
    ffn_grad_rest = (two[: rows // 2], one[rows // 2 :])
    attn_sum = send_last(attn_slots, after(attn_sent, ffn_grad, ffn_grad_rest), *GROUP)
    residual = token_rows + living * attn_sum

    ffn_out, ffn_normed, ffn_factor = normalize(residual, mlp_scale)
    ffn_in = jnp.concatenate(gather_quad(ffn_out.astype(bf16), *GROUP), axis=0)
    hidden, slope, silu_gate = ffn(ffn_in, gate_up)
    ffn_grad_rest = after(ffn_grad_rest, ffn_in)
    ffn_grad_rest = after((trade(ffn_grad_rest[0], "x"), trade(ffn_grad_rest[1], "y")), hidden)
    ffn_grad = lax.dynamic_update_slice(ffn_grad, ffn_grad_rest[0], (3 * rows, 0))
    ffn_grad = lax.dynamic_update_slice(ffn_grad, ffn_grad_rest[1], (3 * rows + rows // 2, 0))
    down_wgrad = dot_tn(hidden, ffn_grad).astype(bf16)
    down_share = lax.psum_scatter(down_wgrad, RING, scatter_dimension=0, tiled=True)

    gate_up_grad = ffn_back(after(ffn_grad, down_wgrad), down_full, slope, silu_gate)
    back = dot_nt(gate_up_grad, gate_up).astype(bf16)
    slots = [back[i * rows : (i + 1) * rows] for i in range(members)]
    loads = first_loads(slots)
    back_sent = send_loads(loads, *GROUP)
    gate_up_wgrad = dot_tn(ffn_in, after(gate_up_grad, loads)).astype(bf16)
    loads = last_loads(slots, after(back_sent, gate_up_wgrad))
    gate_up_wgrad = after(gate_up_wgrad, loads)
    ffn_in_grad = sum_up(slots[0], back_sent, send_loads(loads, *GROUP[::-1]))
    residual_back, mlp_scale_grad = normalize_back(ffn_in_grad, ffn_normed, ffn_factor, mlp_scale)
    residual_grad = grad_rows + residual_back
    attn_grad = (living * residual_grad).astype(bf16)
    attn_grad = after(attn_grad, down_share, gate_up_wgrad)
    gate_up_share = lax.psum_scatter(
        gate_up_wgrad.reshape(members, width // members, -1), RING, scatter_dimension=1, tiled=True
    )
    attn_found = fetch_first(attn_grad, *GROUP)
    ffn_part = dot(after(hidden, attn_grad), down_full).astype(bf16)
    ffn_slots = [ffn_part[i * rows : (i + 1) * rows] for i in range(members)]
    attn_found = after(attn_found, ffn_part)
    attn_grad = jnp.concatenate(fetch_last(attn_grad, attn_found, *GROUP), axis=0)
    ffn_sent = send_loads(after(first_loads(ffn_slots), attn_grad), *GROUP)
    packed_grad, query_grads = attend_back(
        group_lengths,
        attn_grad,
        gathered,
        query_rot,
        packed,
        rows,
        heads,
    )
    packed_grad = after(packed_grad, ffn_sent)
    slots = [packed_grad[i * rows : (i + 1) * rows] for i in range(members)]
    loads = first_loads(slots)
    packed_sent = send_loads(loads, *GROUP)
    gathered_grad = gathered_grads(
        attn_grad, mixture, packed, after(query_grads, loads), gathered.shape, heads
    )
    loads = last_loads(slots, after(packed_sent, gathered_grad))
    gathered_grad = after(gathered_grad, loads)
    gathered_share = lax.psum_scatter(gathered_grad, RING, scatter_dimension=0, tiled=False)
    packed_last = send_loads(loads, *GROUP[::-1])
    *small_grad, tokens_grad = finish(
        me,
        cores,
        devices,
        query_gain.shape[0],
        slots[0],
        packed_sent,
        packed_last,
        latent,
        latent_scale,
        own_cos,
        own_sin,
        attn_in,
        tokens,
        attn_scale,
        qkv_parts,
        residual_grad,
        mlp_scale_grad.reshape(1, -1),
    )
    ffn_last = send_loads(last_loads(ffn_slots, ffn_sent), *GROUP[::-1])
    small_grad = after(small_grad, ffn_last)
    small_slots = small_first(small_grad, cores, d_rows)
    small_slots = after(small_slots, gate_up_share)
    small_sent = send_first(small_slots, *GROUP)
    loads = last_loads(small_slots, small_sent)
    small_last = send_loads(loads, *GROUP[::-1])
    gate_up_share = after(gate_up_share, loads).reshape(members, d_rows, -1)
    gate_up_found = swap_blocks(lambda k: lax.dynamic_index_in_dim(gate_up_share, k, 0, keepdims=False))
    small_last = after(small_last, gate_up_found)
    small_pairs = pairs_along_z(sum_up(small_slots[0], small_sent, small_last).astype(bf16))
    small_pairs = after(small_pairs, gathered_share)
    along = [along_z(small_pairs[code], code) for code in (1, 2, 3)]
    gathered_share, down_share = after((gathered_share, down_share), small_pairs)
    held = out_weight.shape[0]
    out_share = gathered_share[:held]

    query_share = after(gathered_share, along[0])

    def query_part(k):
        low = lax.dynamic_slice_in_dim(query_share, held + (k % 2) * (held // 4), held // 4, 0)
        return lax.dynamic_slice_in_dim(low, (k // 2) * (width // 2), width // 2, 1)

    query_found = swap_blocks(query_part)
    small_share = add_up([small_pairs[0], *after(along, query_found)])
    ffn_sum = sum_up(*after((ffn_slots[0], ffn_sent, ffn_last), small_slots))
    layer_out = (residual + living * ffn_sum).astype(bf16)
    found = in_order(gate_up_found)
    gate_share = jnp.concatenate([part[:, :cut] for part in found], axis=1).astype(f32)
    up_share = jnp.concatenate([part[:, cut:] for part in found], axis=1).astype(f32)
    found = in_order(query_found)
    query_share = jnp.concatenate(found, axis=1).astype(f32)
    return (
        layer_out,
        tokens_grad,
        small_share[:, latent_width + 2 * HD],
        small_share[:, :latent_width],
        small_share[: query_gain.shape[0], latent_width + 2 * HD + 2],
        query_share,
        small_share[:, latent_width : latent_width + HD],
        small_share[:, latent_width + HD : latent_width + 2 * HD],
        out_share.astype(f32),
        small_share[:, latent_width + 2 * HD + 1],
        gate_share,
        up_share,
        down_share.astype(f32),
    )


def solution(mesh):
    members, ring = mesh.shape["dp"], mesh.shape["fsdp"]
    cores = mesh.devices.size // 16
    fine = jax.sharding.Mesh(mesh.devices.reshape(2, 2, 2, 2, cores), ALL)
    matrix, vector = P(ALL, None), P(ALL)
    in_specs = (
        matrix,
        matrix,
        vector,
        matrix,
        vector,
        matrix,
        matrix,
        matrix,
        matrix,
        vector,
        matrix,
        matrix,
        matrix,
        matrix,
    )
    out_specs = (
        matrix,
        matrix,
        vector,
        matrix,
        vector,
        matrix,
        matrix,
        matrix,
        matrix,
        vector,
        matrix,
        matrix,
        matrix,
    )

    def body(*args):
        return shards(members, ring, cores, *args)

    return jax.shard_map(body, mesh=fine, in_specs=in_specs, out_specs=out_specs, check_vma=False)
```
